256 devices in a mesh: gz: 64 (over z, x, core), gy: 4 (over y).
Axes of the slice: x: 4, y: 4, z: 8, core: 2. Of those that a mesh axis runs over, the one named last changes fastest.
Arguments:
- parcel_cell: int32 [1048576], P(('gz', 'gy')), may hold values from 0 to 131071
- parcel_offset: float32 [3, 1048576], P(None, ('gz', 'gy')), may hold values from 0 to 1
- parcel_volume: float32 [1048576], P(('gz', 'gy')), may hold values from 1 to 8
- parcel_force: float32 [3, 1048576], P(None, ('gz', 'gy')), may hold values from -24 to 24
- brick_counts: int32 [64, 4], P('gz', 'gy'), may hold values from 1 to 4096, as said below
- divergence: float32 [512, 256, 256], P('gz', 'gy'), may hold values from -6 to 6
- pressure_prev: float32 [512, 256, 256], P('gz', 'gy'), may hold values from -6 to 6
- gas_density: float32 [512, 256, 256], P('gz', 'gy'), may hold values from 0.5 to 2
Outputs:
- gas_fraction: float32 [512, 256, 256], P('gz', 'gy')
- momentum_source: float32 [512, 3, 256, 256], P('gz', None, 'gy')
- pressure: float32 [512, 256, 256], P('gz', 'gy')
- residual: float32 [512, 256, 256], P('gz', 'gy')
The draws below stay inside these ranges and needn't reach their ends.
Inputs may be any that keep to these rules, and one draw needn't show every extreme that they name: brick_counts gives the number of live parcels of each brick, held in the brick's first slots; one brick holds exactly 4096 and one exactly 1.
All inputs are finite; a program needn't handle non-finite values.
Results may differ from the reference program's by a relative error of at most 0.0021.
Values sent between devices are 32-bit elements; how exact they have to be, the bound alone decides.
No kernel may reach another device: no remote copies, remote signals or barrier semaphores. Data moves between devices by JAX's collectives and lax.ppermute only.
A program may use at most 64 MiB of HBM per device.

```python
import math
import jax
import jax.numpy as jnp
from jax import lax

CZ = 8
CY = 64
CX = 256
PCAP = 4096
SWEEPS = 3
ITERS = 2
BRICKS_Z = 64
BRICKS_Y = 4
NZ = 512
NY = 256
NX = 256
PARCELS = 1048576


def draw_brick_counts(key, part):
    key_level = jax.random.fold_in(key, 11)
    key_jitter = jax.random.fold_in(key, 12)
    key_ranking = jax.random.fold_in(key, 13)
    bricks = BRICKS_Z * BRICKS_Y
    levels = jax.random.randint(key_level, (bricks,), 0, 4)
    jitter = jax.random.randint(key_jitter, (bricks,), 0, 64)
    counts = jnp.maximum(PCAP // jnp.left_shift(1, levels) - jitter, 1)
    ranking = jax.random.permutation(key_ranking, bricks)
    counts = counts.at[ranking[0]].set(PCAP)
    counts = counts.at[ranking[1]].set(1)
    return counts.reshape(BRICKS_Z, BRICKS_Y).astype(jnp.int32)


def plant(values, stream_key, least, high):
    shape = values.shape
    spot = [jax.random.randint(jax.random.fold_in(stream_key, axis), (), 0, shape[axis]) for axis in range(len(shape))]
    values = values.at[tuple(spot)].set(least)
    longest = shape.index(max(shape))
    spot[longest] = (spot[longest] + 1) % shape[longest]
    return values.at[tuple(spot)].set(high)


def steps_of(rng, dims, pieces, low, largest):
    factor_of, own = 1.0, jax.random.fold_in(rng, 6)
    for dim, shards_of in pieces:
        draws = jnp.exp(jax.random.uniform(jax.random.fold_in(own, dim), (shards_of,), jnp.float32, low / len(pieces), largest / len(pieces)))
        factor_of = factor_of * jnp.repeat(draws, dims[dim] // shards_of).reshape([-1 if axis == dim else 1 for axis in range(len(dims))])
    return factor_of


def noise(stream_key, extent, deviation, limit, split=(), kind=jnp.bfloat16):
    values = jax.random.normal(stream_key, extent, jnp.float32) * deviation
    if len(split) > 0:
        values = steps_of(stream_key, extent, split, -0.22, 0.18) * values
    return jnp.clip(values, min=-limit, max=limit).astype(kind)


def setup_inputs(seed: int = 0) -> dict:
    key_list = jax.random.split(jax.random.key(seed), 9)
    parcel_cell = plant(jax.random.randint(key_list[0], (PARCELS,), 0, CZ * CY * CX), jax.random.fold_in(key_list[0], 1), 0, (CZ * CY * CX) - 1).astype(jnp.int32)
    parcel_offset = jnp.clip(1.0 * jax.random.uniform(key_list[1], (3, PARCELS), jnp.float32) ** steps_of(key_list[1], (3, PARCELS), ((1, 256),), -0.2, 0.2), 0.0, 1.0)
    parcel_volume = jnp.clip(jnp.exp(math.log(8.0) - 2.0794415 * jax.random.uniform(key_list[2], (PARCELS,), jnp.float32) ** steps_of(key_list[2], (PARCELS,), ((0, 256),), -0.2, 0.2)), 1.0, 8.0)
    parcel_force = noise(key_list[3], (3, PARCELS), 4.0, 24.0, ((1, 256),), jnp.float32)
    brick_counts = draw_brick_counts(jax.random.fold_in(key_list[8], 71), 0)
    divergence = noise(key_list[5], (NZ, NY, NX), 1.0, 6.0, ((0, 64), (1, 4)), jnp.float32)
    pressure_prev = noise(key_list[6], (NZ, NY, NX), 1.0, 6.0, ((0, 64), (1, 4)), jnp.float32)
    gas_density = jnp.clip(jnp.exp(math.log(2.0) - 1.3862944 * jax.random.uniform(key_list[7], (NZ, NY, NX), jnp.float32) ** steps_of(key_list[7], (NZ, NY, NX), ((0, 64), (1, 4)), -0.2, 0.2)), 0.5, 2.0)
    return dict(parcel_cell=parcel_cell, parcel_offset=parcel_offset, parcel_volume=parcel_volume, parcel_force=parcel_force, brick_counts=brick_counts, divergence=divergence, pressure_prev=pressure_prev, gas_density=gas_density)


smooth_rate = 0.15
stiffness = 0.002


def tap_weight(distance):
    return jnp.exp(-0.5 * distance * distance)


def tap_norm(offset, home_cell, upper_bound):
    summed = jnp.zeros_like(offset)
    for shift_tap in range(-3, 4):
        inside = (home_cell + shift_tap >= 0) & (home_cell + shift_tap < upper_bound)
        summed = summed + jnp.where(inside, tap_weight(shift_tap + 0.5 - offset), 0.0)
    return summed


def axis_weights(home_cell, offset, upper_bound, norm_value):
    tap_list = jnp.arange(-3, 4, dtype=jnp.int32)
    places = home_cell[:, None] + tap_list[None, :]
    distance = tap_list[None, :].astype(jnp.float32) + 0.5 - offset[:, None]
    inside = (places >= 0) & (places < upper_bound)
    weights = jnp.where(inside, tap_weight(distance), 0.0) / norm_value[:, None]
    return weights, jnp.clip(places, 0, upper_bound - 1)


def smooth_field(values):
    size_y, size_x = values.shape[1], values.shape[2]
    padded = jnp.pad(values, ((0, 0), (1, 1), (1, 1)))
    beside = jnp.roll(values, 1, 0) + jnp.roll(values, -1, 0) + padded[:, :-2, 1:-1] + padded[:, 2:, 1:-1] + padded[:, 1:-1, :-2] + padded[:, 1:-1, 2:]
    rows_at = jnp.arange(size_y, dtype=jnp.int32)
    columns = jnp.arange(size_x, dtype=jnp.int32)
    count_y = (rows_at >= 1).astype(jnp.float32) + (rows_at <= size_y - 2).astype(jnp.float32)
    count_x = (columns >= 1).astype(jnp.float32) + (columns <= size_x - 2).astype(jnp.float32)
    neighbour_count = 2.0 + count_y[:, None] + count_x[None, :]
    return values + smooth_rate * (beside - neighbour_count * values)


def neighbour_list(values):
    padded = jnp.pad(values, ((0, 0), (1, 1), (1, 1)))
    return (jnp.roll(values, 1, 0), jnp.roll(values, -1, 0), padded[:, :-2, 1:-1], padded[:, 2:, 1:-1], padded[:, 1:-1, :-2], padded[:, 1:-1, 2:])


def reference(parcel_cell, parcel_offset, parcel_volume, parcel_force, brick_counts, divergence, pressure_prev, gas_density):
    slot_ids = jnp.arange(PARCELS, dtype=jnp.int32)
    brick_ids = slot_ids // PCAP
    live_slots = ((slot_ids - brick_ids * PCAP) < brick_counts.reshape(-1)[brick_ids]).astype(jnp.float32)
    parcel_load = jnp.concatenate([parcel_volume[None, :], parcel_volume[None, :] * parcel_force], axis=0) * live_slots[None, :]
    home_z = (brick_ids // BRICKS_Y) * CZ + parcel_cell // (CY * CX)
    home_y = (brick_ids % BRICKS_Y) * CY + (parcel_cell // CX) % CY
    home_x = parcel_cell % CX
    tap_list = jnp.arange(-3, 4, dtype=jnp.int32)
    norm_z = tap_norm(parcel_offset[0], home_z * 0 + 3, 7)
    distance_z = tap_list[None, :].astype(jnp.float32) + 0.5 - parcel_offset[0][:, None]
    weight_z = tap_weight(distance_z) / norm_z[:, None]
    place_z = (home_z[:, None] + tap_list[None, :]) % NZ
    weight_y, place_y = axis_weights(home_y, parcel_offset[1], NY, tap_norm(parcel_offset[1], home_y, NY))
    weight_x, place_x = axis_weights(home_x, parcel_offset[2], NX, tap_norm(parcel_offset[2], home_x, NX))
    x_weight = lax.optimization_barrier(weight_x.astype(jnp.bfloat16)).astype(jnp.float32)
    component_ids = jnp.arange(4, dtype=jnp.int32)

    def add_plane(deposited, plane_data):
        plane_weight, plane_place = plane_data
        split_weight = (parcel_load * plane_weight[None, :])[:, :, None] * weight_y[None, :, :]
        split_weight = lax.optimization_barrier(split_weight.astype(jnp.bfloat16)).astype(jnp.float32)
        values = split_weight[:, :, :, None] * x_weight[None, :, None, :]
        deposited = deposited.at[plane_place[None, :, None, None], component_ids[:, None, None, None], place_y[None, :, :, None], place_x[None, :, None, :]].add(values)
        return deposited, None

    deposited = jnp.zeros((NZ, 4, NY, NX), jnp.float32)
    deposited, unused_out = lax.scan(add_plane, deposited, (weight_z.T, place_z.T))
    filtered = []
    for component in range(4):
        smoothed = deposited[:, component]
        for sweep_index in range(SWEEPS):
            smoothed = smooth_field(smoothed)
        filtered.append(smoothed)
    gas_fraction = 1.0 / (1.0 + filtered[0])
    momentum_source = jnp.stack(filtered[1:], axis=1)
    mobility = gas_fraction / gas_density
    face_list = [0.5 * (mobility + other) for other in neighbour_list(mobility)]
    diagonal = stiffness * mobility + face_list[0] + face_list[1] + face_list[2] + face_list[3] + face_list[4] + face_list[5]
    along_z = neighbour_list(filtered[1])
    along_y = neighbour_list(filtered[2])
    along_x = neighbour_list(filtered[3])
    spread = 0.5 * (along_z[1] - along_z[0]) + 0.5 * (along_y[3] - along_y[2]) + 0.5 * (along_x[5] - along_x[4])
    right_side = divergence - spread

    def operate(values):
        others = neighbour_list(values)
        coupled = face_list[0] * others[0] + face_list[1] * others[1] + face_list[2] * others[2] + face_list[3] * others[3] + face_list[4] * others[4] + face_list[5] * others[5]
        return diagonal * values - coupled

    pressure = pressure_prev
    residual = right_side - operate(pressure)
    precond = residual / diagonal
    direction = precond
    scaled_norm = jnp.sum(residual * precond)
    for iteration in range(ITERS):
        mapped = operate(direction)
        step_size = scaled_norm / jnp.sum(direction * mapped)
        pressure = pressure + step_size * direction
        residual = residual - step_size * mapped
        if iteration + 1 < ITERS:
            precond = residual / diagonal
            norm_next = jnp.sum(residual * precond)
            direction = precond + (norm_next / scaled_norm) * direction
            scaled_norm = norm_next
    return (gas_fraction, momentum_source, pressure, residual)
```

```python
import functools

import jax
import jax.numpy as jnp
from jax import lax
from jax.experimental import pallas as pl
from jax.experimental.pallas import tpu as pltpu
from jax.sharding import PartitionSpec as P

CZ = 8
CY = 64
CX = 256
PCAP = 4096
ITERS = 2
REACH = 5
ZE = CZ + 2 * REACH
YE = 80
OWN_ROWS = 72
CHUNK = 512

smooth_rate = 0.15
stiffness = 0.002

VMEM_LIMIT = 48 * 1024 * 1024


def chunk_values(parcels, start, grid_rows, row_first, shift_y):
    cell = parcels[0:1].astype(jnp.int32)
    home_z = lax.shift_right_logical(cell, 14).astype(jnp.float32)
    home_y = (lax.shift_right_logical(cell, 8) & 63).astype(jnp.float32)
    home_x = (cell & 255).astype(jnp.float32)
    count = parcels.shape[1]
    taps = lax.broadcasted_iota(jnp.int32, (8, count), 0).astype(jnp.float32) - 3.0

    def tap_sum(offset, inside):
        distance = taps + 0.5 - offset
        weight = jnp.where(inside, jnp.exp(-0.5 * distance * distance), 0.0)
        return 1.0 / jnp.sum(weight, axis=0, keepdims=True)

    seven = taps < 3.5
    place_y = taps + (home_y + (row_first + shift_y))
    place_x = taps + home_x
    inv_z = tap_sum(parcels[1:2], seven)
    inv_y = tap_sum(parcels[2:3], seven & (place_y >= 0.0) & (place_y < grid_rows))
    inv_x = tap_sum(parcels[3:4], seven & (place_x >= 0.0) & (place_x < float(CX)))
    return home_z, home_y, home_x, inv_z, inv_y, inv_x


def axis_rows(rows, first, home, offset, inverse):
    place = lax.broadcasted_iota(jnp.int32, (rows, home.shape[1]), 0).astype(jnp.float32) + first
    tap = place - home
    distance = tap + 0.5 - offset
    weight = jnp.exp(-0.5 * distance * distance) * inverse
    return jnp.where(jnp.abs(tap) < 3.5, weight, 0.0), place


def used_slots(volume):
    slot = lax.broadcasted_iota(jnp.int32, volume.shape, 1).astype(jnp.float32) + 1.0
    return jnp.max(jnp.where(volume != 0.0, slot, 0.0)).astype(jnp.int32)


def x_columns(columns_ref, bundle):
    padded = jnp.concatenate(
        [bundle, jnp.zeros((128 - bundle.shape[0], bundle.shape[1]), jnp.float32)], axis=0
    )
    columns_ref[...] = padded.T


def deposit_tall(parcels_ref, base, row_first, grid_rows, shift_z, planes, plane_first, acc_ref, lhs_ref, rhs_ref, columns_ref):
    total = used_slots(parcels_ref[base + 4 : base + 5, :])

    def chunk_step(index, carry):
        start = pl.multiple_of(index * CHUNK, CHUNK)
        parcels = parcels_ref[base : base + 8, pl.ds(start, CHUNK)]
        home_z, home_y, home_x, inv_z, inv_y, inv_x = chunk_values(
            parcels, start, grid_rows, row_first, 0.0
        )
        volume = parcels[4:5]
        scaled = volume * inv_x
        bundle = jnp.concatenate(
            [home_x, 0.5 - parcels[3:4], scaled, scaled * parcels[5:6], scaled * parcels[6:7], scaled * parcels[7:8]],
            axis=0,
        )
        x_columns(columns_ref, bundle)
        weight_y, place_y = axis_rows(OWN_ROWS, -float(REACH), home_y, parcels[2:3], inv_y)
        place_y = place_y + row_first
        weight_y = jnp.where((place_y >= 0.0) & (place_y < grid_rows), weight_y, 0.0)
        rows_z = -(-planes // 8) * 8
        weight_z, unused = axis_rows(
            rows_z, float(plane_first - REACH - shift_z), home_z, parcels[1:2], inv_z
        )
        for pair in range(planes // 2):
            both = jnp.concatenate(
                [weight_z[2 * pair : 2 * pair + 1] * weight_y, weight_z[2 * pair + 1 : 2 * pair + 2] * weight_y],
                axis=0,
            )
            lhs_ref[2 * OWN_ROWS * pair : 2 * OWN_ROWS * (pair + 1), :] = both.astype(jnp.bfloat16)
        block = 64
        lanes = lax.broadcasted_iota(jnp.int32, (block, CX), 1).astype(jnp.float32)
        for part in range(CHUNK // block):
            held = columns_ref[part * block : (part + 1) * block, 0:8]
            tap = lanes - held[:, 0:1]
            distance = tap + held[:, 1:2]
            shape_x = jnp.where(jnp.abs(tap) < 3.5, jnp.exp(-0.5 * distance * distance), 0.0)
            for field in range(4):
                rhs_ref[part * block : (part + 1) * block, field * CX : (field + 1) * CX] = (
                    shape_x * held[:, 2 + field : 3 + field]
                ).astype(jnp.bfloat16)
        for pair in range(planes // 2):
            product = jnp.dot(
                lhs_ref[2 * OWN_ROWS * pair : 2 * OWN_ROWS * (pair + 1), :],
                rhs_ref[...],
                preferred_element_type=jnp.float32,
            )
            acc_ref[plane_first + 2 * pair, 0:OWN_ROWS, :] += product[:OWN_ROWS]
            acc_ref[plane_first + 2 * pair + 1, 0:OWN_ROWS, :] += product[OWN_ROWS:]
        return carry

    lax.fori_loop(0, lax.shift_right_logical(total + (CHUNK - 1), CHUNK.bit_length() - 1), chunk_step, 0)


def deposit_flat(parcels_ref, base, row_first, grid_rows, shift_z, shift_y, planes, plane_first, window, acc_ref, lhs_ref, rhs_ref, columns_ref):
    total = used_slots(parcels_ref[base + 4 : base + 5, :])

    def chunk_step(index, carry):
        start = pl.multiple_of(index * CHUNK, CHUNK)
        parcels = parcels_ref[base : base + 8, pl.ds(start, CHUNK)]
        home_z, home_y, home_x, inv_z, inv_y, inv_x = chunk_values(
            parcels, start, grid_rows, row_first, float(shift_y)
        )
        bundle = jnp.concatenate([home_x, 0.5 - parcels[3:4], inv_x], axis=0)
        x_columns(columns_ref, bundle)
        weight_y, place_y = axis_rows(
            8, float(window - REACH - shift_y), home_y, parcels[2:3], inv_y
        )
        place_y = place_y + (row_first + shift_y)
        weight_y = jnp.where((place_y >= 0.0) & (place_y < grid_rows), weight_y, 0.0)
        rows_z = -(-planes // 8) * 8
        weight_z, unused = axis_rows(
            rows_z, float(plane_first - REACH - shift_z), home_z, parcels[1:2], inv_z
        )
        for field in range(4):
            load = parcels[4:5] if field == 0 else parcels[4:5] * parcels[4 + field : 5 + field]
            loaded = weight_z * load
            for pair in range(planes // 2):
                both = jnp.concatenate(
                    [loaded[2 * pair : 2 * pair + 1] * weight_y, loaded[2 * pair + 1 : 2 * pair + 2] * weight_y],
                    axis=0,
                )
                first = (field * planes + 2 * pair) * 8
                lhs_ref[first : first + 16, :] = both.astype(jnp.bfloat16)
        block = 64
        lanes = lax.broadcasted_iota(jnp.int32, (block, CX), 1).astype(jnp.float32)
        for part in range(CHUNK // block):
            held = columns_ref[part * block : (part + 1) * block, 0:8]
            tap = lanes - held[:, 0:1]
            distance = tap + held[:, 1:2]
            shape_x = jnp.where(jnp.abs(tap) < 3.5, jnp.exp(-0.5 * distance * distance), 0.0)
            rhs_ref[part * block : (part + 1) * block, 0:CX] = (shape_x * held[:, 2:3]).astype(
                jnp.bfloat16
            )
        for field in range(4):
            product = jnp.dot(
                lhs_ref[field * planes * 8 : (field + 1) * planes * 8, :],
                rhs_ref[:, 0:CX],
                preferred_element_type=jnp.float32,
            )
            for plane in range(planes):
                acc_ref[
                    plane_first + plane, window : window + 8, field * CX : (field + 1) * CX
                ] += product[plane * 8 : (plane + 1) * 8]
        return carry

    lax.fori_loop(0, lax.shift_right_logical(total + (CHUNK - 1), CHUNK.bit_length() - 1), chunk_step, 0)


def own_kernel(grid_rows, row_ref, parcels_ref, acc_ref, lhs_ref, rhs_ref, columns_ref):
    row_first = row_ref[0].astype(jnp.float32)
    acc_ref[...] = jnp.zeros_like(acc_ref)
    deposit_tall(parcels_ref, 0, row_first, grid_rows, 0, 14, 2, acc_ref, lhs_ref, rhs_ref, columns_ref)


def z_kernel(grid_rows, row_ref, below_ref, above_ref, held_ref, acc_ref, lhs_ref, rhs_ref, columns_ref):
    row_first = row_ref[0].astype(jnp.float32)
    acc_ref[...] = held_ref[...]
    deposit_tall(below_ref, 0, row_first, grid_rows, -CZ, 8, 0, acc_ref, lhs_ref, rhs_ref, columns_ref)
    deposit_tall(above_ref, 0, row_first, grid_rows, CZ, 8, 10, acc_ref, lhs_ref, rhs_ref, columns_ref)


def y_kernel(grid_rows, row_ref, south_ref, north_ref, held_ref, acc_ref, lhs_ref, rhs_ref, columns_ref):
    row_first = row_ref[0].astype(jnp.float32)
    acc_ref[...] = held_ref[...]
    for parcels_ref, shift_y, window in ((south_ref, -CY, 0), (north_ref, CY, CY + 2)):
        for part, (shift_z, planes, plane_first) in enumerate(((0, 14, 2), (-CZ, 8, 0), (CZ, 8, 10))):
            deposit_flat(
                parcels_ref, 8 * part, row_first, grid_rows, shift_z, shift_y, planes, plane_first,
                window, acc_ref, lhs_ref, rhs_ref, columns_ref,
            )


def x_pair(values, first_lane, last_lane):
    west = jnp.where(first_lane, 0.0, pltpu.roll(values, 1, 1))
    east = jnp.where(last_lane, 0.0, pltpu.roll(values, CX - 1, 1))
    return west + east


def y_pair(values):
    rows = values.shape[0]
    return pltpu.roll(values, 1, 0) + pltpu.roll(values, rows - 1, 0)


def plane_masks(row_first, grid_rows):
    row = lax.broadcasted_iota(jnp.int32, (YE, CX), 0).astype(jnp.float32) + (row_first - REACH)
    lane = lax.broadcasted_iota(jnp.int32, (YE, CX), 1)
    return row, lane == 0, lane == CX - 1


def field_kernel(
    grid_rows,
    row_ref,
    acc_ref,
    density_ref,
    guess_ref,
    diverge_ref,
    fraction_ref,
    momentum_ref,
    residual_ref,
    direction_ref,
    mapped_ref,
    scaled_ref,
    mobility_ref,
    diagonal_ref,
    dots_ref,
    first_ref,
    second_ref,
    mob_ref,
    wide_ref,
):
    row_first = row_ref[0].astype(jnp.float32)
    row, first_lane, last_lane = plane_masks(row_first, grid_rows)
    within = (row >= 0.0) & (row < grid_rows)
    inside = within.astype(jnp.float32)
    known = within & (row >= row_first - 2.0) & (row < row_first + (CY + 2.0))
    count_y = (row >= 1.0).astype(jnp.float32) + (row < grid_rows - 1.0).astype(jnp.float32)
    count_x = 2.0 - first_lane.astype(jnp.float32) - last_lane.astype(jnp.float32)
    keep = inside * (1.0 - smooth_rate * (2.0 + count_y + count_x))
    spread_rate = inside * smooth_rate

    for sweep, (source, target) in enumerate(
        ((acc_ref, first_ref), (first_ref, second_ref), (second_ref, first_ref))
    ):

        def sweep_step(plane, carry, source=source, target=target):
            for field in range(4):
                cut = slice(field * CX, (field + 1) * CX)
                values = source[plane, :, cut]
                beside = source[plane - 1, :, cut] + source[plane + 1, :, cut]
                beside = beside + y_pair(values) + x_pair(values, first_lane, last_lane)
                target[plane, :, cut] = keep * values + spread_rate * beside
            return carry

        lax.fori_loop(sweep + 1, ZE - 1 - sweep, sweep_step, 0)

    filtered = first_ref
    own = slice(REACH, REACH + CY)

    def mobility_step(plane, carry):
        fraction = 1.0 / (1.0 + filtered[plane + 3, :, 0:CX])
        mob_ref[plane] = jnp.where(known, fraction / density_ref[plane], 0.0)
        return carry

    lax.fori_loop(0, CZ + 4, mobility_step, 0)

    def output_step(plane, carry):
        fraction_ref[plane] = 1.0 / (1.0 + filtered[plane + REACH, own, 0:CX])
        for part in range(3):
            momentum_ref[plane, part] = filtered[plane + REACH, own, (part + 1) * CX : (part + 2) * CX]
        return carry

    lax.fori_loop(0, CZ, output_step, 0)

    def beside_of(ref, plane):
        values = ref[plane]
        return ref[plane - 1] + ref[plane + 1] + y_pair(values) + x_pair(values, first_lane, last_lane)

    def product_step(plane, carry):
        wide_ref[plane] = mob_ref[plane] * guess_ref[plane]
        return carry

    lax.fori_loop(0, CZ + 4, product_step, 0)

    def first_residual(plane, carry):
        at = plane + 1
        mobility = mob_ref[at]
        diagonal = (3.0 + stiffness) * mobility + 0.5 * beside_of(mob_ref, at)
        operated = diagonal * guess_ref[at] - 0.5 * (
            mobility * beside_of(guess_ref, at) + beside_of(wide_ref, at)
        )
        along_y = filtered[at + 3, :, 2 * CX : 3 * CX]
        along_x = filtered[at + 3, :, 3 * CX : 4 * CX]
        spread = 0.5 * (filtered[at + 4, :, CX : 2 * CX] - filtered[at + 2, :, CX : 2 * CX])
        spread = spread + 0.5 * (pltpu.roll(along_y, YE - 1, 0) - pltpu.roll(along_y, 1, 0))
        spread = spread + 0.5 * (
            jnp.where(last_lane, 0.0, pltpu.roll(along_x, CX - 1, 1))
            - jnp.where(first_lane, 0.0, pltpu.roll(along_x, 1, 1))
        )
        residual = jnp.where(known, diverge_ref[plane] - spread - operated, 0.0)
        direction = jnp.where(known, residual / diagonal, 0.0)
        second_ref[plane, :, 0:CX] = residual
        second_ref[plane, :, CX : 2 * CX] = direction
        second_ref[plane, :, 2 * CX : 3 * CX] = direction * mobility
        diagonal_ref[plane] = diagonal
        mobility_ref[plane] = mobility
        return carry

    lax.fori_loop(0, CZ + 2, first_residual, 0)

    def beside_cut(plane, cut):
        values = second_ref[plane, :, cut]
        return (
            second_ref[plane - 1, :, cut]
            + second_ref[plane + 1, :, cut]
            + y_pair(values)
            + x_pair(values, first_lane, last_lane)
        )

    scaled_ref[0] = jnp.zeros((YE, CX), jnp.float32)
    scaled_ref[CZ + 1] = jnp.zeros((YE, CX), jnp.float32)
    row_own = (row >= row_first) & (row < row_first + CY)

    def map_step(plane, sums):
        at = plane + 1
        residual = second_ref[at, :, 0:CX]
        direction = second_ref[at, :, CX : 2 * CX]
        diagonal = diagonal_ref[at]
        mapped = diagonal * direction - 0.5 * (
            mobility_ref[at] * beside_cut(at, slice(CX, 2 * CX)) + beside_cut(at, slice(2 * CX, 3 * CX))
        )
        mapped = jnp.where(row_own, mapped, 0.0)
        scaled = jnp.where(row_own, mapped / diagonal, 0.0)
        scaled_ref[at] = scaled
        residual_ref[plane] = residual[own]
        direction_ref[plane] = direction[own]
        mapped_ref[plane] = mapped[own]
        sum_rz, sum_dw, sum_uw = sums
        return (
            sum_rz + jnp.where(row_own, residual * direction, 0.0),
            sum_dw + direction * mapped,
            sum_uw + scaled * mapped,
        )

    zero = jnp.zeros((YE, CX), jnp.float32)
    sums = lax.fori_loop(0, CZ, map_step, (zero, zero, zero))
    for index in range(3):
        dots_ref[index] = jnp.sum(sums[index])


def second_kernel(scaled_ref, below_ref, above_ref, south_ref, north_ref, mobility_ref, diagonal_ref, twice_ref, dot_ref, held_ref, product_ref):
    own = slice(REACH, REACH + CY)
    lane = lax.broadcasted_iota(jnp.int32, (YE, CX), 1)
    first_lane, last_lane = lane == 0, lane == CX - 1
    held_ref[...] = scaled_ref[...]
    held_ref[0, own, :] = below_ref[...]
    held_ref[CZ + 1, own, :] = above_ref[...]
    for plane in range(CZ):
        held_ref[plane + 1, REACH - 1 : REACH, :] = south_ref[plane : plane + 1]
        held_ref[plane + 1, REACH + CY : REACH + CY + 1, :] = north_ref[plane : plane + 1]

    def product_step(plane, carry):
        product_ref[plane] = held_ref[plane] * mobility_ref[plane]
        return carry

    lax.fori_loop(0, CZ + 2, product_step, 0)

    def beside_of(ref, plane):
        values = ref[plane]
        return ref[plane - 1] + ref[plane + 1] + y_pair(values) + x_pair(values, first_lane, last_lane)

    def map_step(plane, total):
        at = plane + 1
        twice = diagonal_ref[at] * held_ref[at] - 0.5 * (
            mobility_ref[at] * beside_of(held_ref, at) + beside_of(product_ref, at)
        )
        twice_ref[plane] = twice[own]
        return total + (held_ref[at] * twice)[own]

    total = lax.fori_loop(0, CZ, map_step, jnp.zeros((CY, CX), jnp.float32))
    dot_ref[0] = jnp.sum(total)


def vmem_spec():
    return pl.BlockSpec(memory_space=pltpu.VMEM)


def smem_spec():
    return pl.BlockSpec(memory_space=pltpu.SMEM)


def f32(*shape):
    return jax.ShapeDtypeStruct(shape, jnp.float32)


def params():
    return pltpu.CompilerParams(vmem_limit_bytes=VMEM_LIMIT)


def deposit_scratch():
    return [
        pltpu.VMEM((14 * OWN_ROWS, CHUNK), jnp.bfloat16),
        pltpu.VMEM((CHUNK, 4 * CX), jnp.bfloat16),
        pltpu.VMEM((CHUNK, 128), jnp.float32),
    ]


def on_device(
    parcel_cell,
    parcel_offset,
    parcel_volume,
    parcel_force,
    brick_counts,
    divergence,
    pressure_prev,
    gas_density,
):
    size_z = lax.axis_size("gz")
    size_y = lax.axis_size("gy")
    grid_rows = float(size_y * CY)
    row_first = (lax.axis_index("gy") * CY).astype(jnp.int32)[None]
    up_z = [(i, (i + 1) % size_z) for i in range(size_z)]
    down_z = [((i + 1) % size_z, i) for i in range(size_z)]
    up_y = [(i, i + 1) for i in range(size_y - 1)]
    down_y = [(i + 1, i) for i in range(size_y - 1)]

    live = (jnp.arange(PCAP, dtype=jnp.int32) < brick_counts[0, 0]).astype(jnp.float32)
    parcels = jnp.concatenate(
        [parcel_cell.astype(jnp.float32)[None], parcel_offset, (parcel_volume * live)[None], parcel_force],
        axis=0,
    )
    parcels_below = lax.ppermute(parcels, "gz", up_z)
    parcels_above = lax.ppermute(parcels, "gz", down_z)
    stack_z_head = jnp.concatenate([pressure_prev[:2], gas_density[:2], divergence[:1]], axis=0)
    stack_z_tail = jnp.concatenate([pressure_prev[-2:], gas_density[-2:], divergence[-1:]], axis=0)
    below = lax.ppermute(stack_z_tail, "gz", up_z)
    above = lax.ppermute(stack_z_head, "gz", down_z)
    trio = jnp.concatenate([parcels, parcels_below, parcels_above], axis=0)
    trio_south = lax.ppermute(trio, "gy", up_y)
    trio_north = lax.ppermute(trio, "gy", down_y)

    guess = jnp.concatenate([below[0:2], pressure_prev, above[0:2]], axis=0)
    density = jnp.concatenate([below[2:4], gas_density, above[2:4]], axis=0)
    diverge = jnp.concatenate([below[4:5], divergence, above[4:5]], axis=0)
    stack_y_head = jnp.concatenate([guess[:, :2], density[:, :2], jnp.pad(diverge[:, :1], ((1, 1), (0, 0), (0, 0)))], axis=1)
    stack_y_tail = jnp.concatenate([guess[:, -2:], density[:, -2:], jnp.pad(diverge[:, -1:], ((1, 1), (0, 0), (0, 0)))], axis=1)
    south = lax.ppermute(stack_y_tail, "gy", up_y)
    north = lax.ppermute(stack_y_head, "gy", down_y)

    def widened(values, low, high):
        depth = low.shape[1]
        return jnp.pad(
            jnp.concatenate([low, values, high], axis=1),
            ((0, 0), (REACH - depth, YE - REACH - CY - depth), (0, 0)),
        )

    guess = widened(guess, south[:, 0:2], north[:, 0:2])
    density = widened(density, south[:, 2:4], north[:, 2:4])
    diverge = widened(diverge, south[1:-1, 4:5], north[1:-1, 4:5])

    acc = pl.pallas_call(
        functools.partial(own_kernel, grid_rows),
        out_shape=f32(ZE, YE, 4 * CX),
        in_specs=[smem_spec(), vmem_spec()],
        out_specs=vmem_spec(),
        scratch_shapes=deposit_scratch(),
        compiler_params=params(),
        cost_estimate=pl.CostEstimate(flops=8_000_000_000, bytes_accessed=6_000_000, transcendentals=0),
        name="own",
    )(row_first, parcels)
    acc = pl.pallas_call(
        functools.partial(z_kernel, grid_rows),
        out_shape=f32(ZE, YE, 4 * CX),
        in_specs=[smem_spec(), vmem_spec(), vmem_spec(), vmem_spec()],
        out_specs=vmem_spec(),
        scratch_shapes=deposit_scratch(),
        compiler_params=params(),
        cost_estimate=pl.CostEstimate(flops=8_000_000_000, bytes_accessed=6_000_000, transcendentals=0),
        name="beside_z",
    )(row_first, parcels_below, parcels_above, acc)
    acc = pl.pallas_call(
        functools.partial(y_kernel, grid_rows),
        out_shape=f32(ZE, YE, 4 * CX),
        in_specs=[smem_spec(), vmem_spec(), vmem_spec(), vmem_spec()],
        out_specs=vmem_spec(),
        scratch_shapes=deposit_scratch(),
        compiler_params=params(),
        cost_estimate=pl.CostEstimate(flops=4_000_000_000, bytes_accessed=6_000_000, transcendentals=0),
        name="beside_y",
    )(row_first, trio_south, trio_north, acc)
    fraction, momentum, residual, direction, mapped, scaled, mobility, diagonal, dots = pl.pallas_call(
        functools.partial(field_kernel, grid_rows),
        out_shape=(
            f32(CZ, CY, CX),
            f32(CZ, 3, CY, CX),
            f32(CZ, CY, CX),
            f32(CZ, CY, CX),
            f32(CZ, CY, CX),
            f32(CZ + 2, YE, CX),
            f32(CZ + 2, YE, CX),
            f32(CZ + 2, YE, CX),
            f32(3),
        ),
        in_specs=[smem_spec()] + [vmem_spec()] * 4,
        out_specs=tuple([vmem_spec()] * 8 + [smem_spec()]),
        scratch_shapes=[
            pltpu.VMEM((ZE, YE, 4 * CX), jnp.float32),
            pltpu.VMEM((ZE, YE, 4 * CX), jnp.float32),
            pltpu.VMEM((CZ + 4, YE, CX), jnp.float32),
            pltpu.VMEM((CZ + 4, YE, CX), jnp.float32),
        ],
        compiler_params=params(),
        name="fields",
    )(row_first, acc, density, guess, diverge)

    own = slice(REACH, REACH + CY)
    scaled_below = lax.ppermute(scaled[CZ, own], "gz", up_z)
    scaled_above = lax.ppermute(scaled[1, own], "gz", down_z)
    scaled_south = lax.ppermute(scaled[1:-1, REACH + CY - 1], "gy", up_y)
    scaled_north = lax.ppermute(scaled[1:-1, REACH], "gy", down_y)
    twice, last_dot = pl.pallas_call(
        second_kernel,
        out_shape=(f32(CZ, CY, CX), f32(1)),
        in_specs=[vmem_spec()] * 7,
        out_specs=(vmem_spec(), smem_spec()),
        scratch_shapes=[
            pltpu.VMEM((CZ + 2, YE, CX), jnp.float32),
            pltpu.VMEM((CZ + 2, YE, CX), jnp.float32),
        ],
        compiler_params=params(),
        name="second",
    )(scaled, scaled_below, scaled_above, scaled_south, scaled_north, mobility, diagonal)

    every = size_z * size_y
    partial = jnp.concatenate([dots, last_dot])
    sent = jnp.broadcast_to(partial[None], (every, 4))
    sums = jnp.sum(lax.all_to_all(sent, ("gz", "gy"), 0, 0), axis=0)
    sum_rz, sum_dw, sum_uw, sum_uv = sums[0], sums[1], sums[2], sums[3]
    step = sum_rz / sum_dw
    next_rz = sum_rz - 2.0 * step * sum_dw + step * step * sum_uw
    ratio = next_rz / sum_rz
    along = 1.0 + ratio
    curvature = along * along * sum_dw - 2.0 * step * along * sum_uw + step * step * sum_uv
    next_step = next_rz / curvature
    scaled_own = scaled[1:-1, own]
    pressure = pressure_prev + (step + next_step * along) * direction - (next_step * step) * scaled_own
    final = residual - (step + next_step * along) * mapped + (next_step * step) * twice
    return (fraction, momentum, pressure, final)


def solution(mesh):
    return jax.shard_map(
        on_device,
        mesh=mesh,
        in_specs=(
            P(("gz", "gy")),
            P(None, ("gz", "gy")),
            P(("gz", "gy")),
            P(None, ("gz", "gy")),
            P("gz", "gy"),
            P("gz", "gy", None),
            P("gz", "gy", None),
            P("gz", "gy", None),
        ),
        out_specs=(
            P("gz", "gy", None),
            P("gz", None, "gy", None),
            P("gz", "gy", None),
            P("gz", "gy", None),
        ),
        check_vma=False,
    )
```

```python
import functools

import jax
import jax.numpy as jnp
from jax import lax
from jax.experimental import pallas as pl
from jax.experimental.pallas import tpu as pltpu
from jax.sharding import PartitionSpec as P

CZ = 8
CY = 64
CX = 256
PCAP = 4096
ITERS = 2
REACH = 5
ZE = CZ + 2 * REACH
YE = 80
LEAD = 8
HALF = 128
CHUNK = 256
TALL = 24

smooth_rate = 0.15
stiffness = 0.002

VMEM_LIMIT = 48 * 1024 * 1024


def chunk_values(parcels, grid_rows, row_first, shift_y):
    cell = parcels[0:1].astype(jnp.int32)
    home_z = lax.shift_right_logical(cell, 14).astype(jnp.float32)
    home_y = (lax.shift_right_logical(cell, 8) & 63).astype(jnp.float32)
    home_x = (cell & 255).astype(jnp.float32)
    count = parcels.shape[1]
    taps = lax.broadcasted_iota(jnp.int32, (8, count), 0).astype(jnp.float32) - 3.0

    def tap_sum(offset, inside):
        distance = taps + 0.5 - offset
        weight = jnp.where(inside, jnp.exp(-0.5 * distance * distance), 0.0)
        return 1.0 / jnp.sum(weight, axis=0, keepdims=True)

    seven = taps < 3.5
    place_y = taps + (home_y + (row_first + shift_y))
    place_x = taps + home_x
    inv_z = tap_sum(parcels[1:2], seven)
    inv_y = tap_sum(parcels[2:3], seven & (place_y >= 0.0) & (place_y < grid_rows))
    inv_x = tap_sum(parcels[3:4], seven & (place_x >= 0.0) & (place_x < float(CX)))
    return home_z, home_y, home_x, inv_z, inv_y, inv_x


def axis_rows(rows, first, home, offset, inverse):
    place = lax.broadcasted_iota(jnp.int32, (rows, home.shape[1]), 0).astype(jnp.float32) + first
    tap = place - home
    distance = tap + 0.5 - offset
    weight = jnp.exp(-0.5 * distance * distance) * inverse
    return jnp.where(jnp.abs(tap) < 3.5, weight, 0.0), place


def row_of(cell):
    return lax.shift_right_logical(cell.astype(jnp.int32), 8) & 63


def count_where(condition):
    return jnp.sum(condition.astype(jnp.float32)).astype(jnp.int32)


def deposit(parcels_ref, base, row_first, grid_rows, shift_z, shift_y, planes, plane_first, window, acc_ref, lhs_ref, rhs_ref):
    rows = TALL if window is None else 8
    volume = parcels_ref[base + 4 : base + 5, :]
    begin = 0
    if shift_y == 0:
        total = count_where(volume != 0.0)
    else:
        home_row = row_of(parcels_ref[base : base + 1, :])
        if shift_y < 0:
            total = count_where(volume != 0.0)
            begin = lax.shift_right_logical(
                count_where((volume != 0.0) & (home_row < CY - 3 - REACH)), CHUNK.bit_length() - 1
            )
        else:
            total = count_where((volume != 0.0) & (home_row < 3 + REACH))

    def chunk_step(index, carry):
        start = pl.multiple_of(index * CHUNK, CHUNK)
        parcels = parcels_ref[base : base + 8, pl.ds(start, CHUNK)]
        home_z, home_y, home_x, inv_z, inv_y, inv_x = chunk_values(
            parcels, grid_rows, row_first, float(shift_y)
        )
        block = 64
        for part in range(CX // block):
            weight_x, unused = axis_rows(block, float(part * block), home_x, parcels[3:4], inv_x)
            rhs_ref[part * block : (part + 1) * block, :] = weight_x.astype(jnp.bfloat16)
        rows_z = -(-planes // 8) * 8
        weight_z, unused = axis_rows(
            rows_z, float(plane_first - REACH - shift_z), home_z, parcels[1:2], inv_z
        )
        loaded = [
            weight_z * (parcels[4:5] if field == 0 else parcels[4:5] * parcels[4 + field : 5 + field])
            for field in range(4)
        ]

        def spread_window(first, least):
            weight_y, place_y = axis_rows(
                rows, first - (LEAD + shift_y), home_y, parcels[2:3], inv_y
            )
            global_y = place_y + (row_first + shift_y)
            inside = (global_y >= 0.0) & (global_y < grid_rows)
            if least is not None:
                inside = inside & (place_y >= least - LEAD)
            weight_y = jnp.where(inside, weight_y, 0.0)
            for field in range(4):
                for pair in range(planes // 2):
                    both = jnp.concatenate(
                        [
                            loaded[field][2 * pair : 2 * pair + 1] * weight_y,
                            loaded[field][2 * pair + 1 : 2 * pair + 2] * weight_y,
                        ],
                        axis=0,
                    )
                    at = (field * planes + 2 * pair) * rows
                    lhs_ref[at : at + 2 * rows, :] = both.astype(jnp.bfloat16)

        def add_window(first):
            for field in range(4):
                product = lax.dot_general(
                    lhs_ref[field * planes * rows : (field + 1) * planes * rows, :],
                    rhs_ref[...],
                    (((1,), (1,)), ((), ())),
                    preferred_element_type=jnp.float32,
                )
                for plane in range(planes):
                    for half in range(2):
                        acc_ref[field, plane_first + plane, half, pl.ds(first, rows), :] += product[
                            plane * rows : (plane + 1) * rows, half * HALF : (half + 1) * HALF
                        ]

        if window is not None:
            spread_window(float(window), None)
            add_window(window)
            return carry

        slot = lax.broadcasted_iota(jnp.int32, (1, CHUNK), 1) + start
        lowest = jnp.min(jnp.where(slot < total, home_y, float(CY))).astype(jnp.int32)
        highest = jnp.max(jnp.where(slot < total, home_y, 0.0)).astype(jnp.int32)
        row_low = lax.shift_right_logical(lowest + (LEAD - 3), 3) * 8
        row_high = highest + (LEAD + 4)

        def window_step(carried):
            logical = carried
            first = pl.multiple_of(jnp.minimum(logical, YE - TALL), 8)
            spread_window(first.astype(jnp.float32), logical.astype(jnp.float32))
            add_window(first)
            return logical + TALL

        lax.while_loop(lambda carried: carried < row_high, window_step, row_low)
        return carry

    end = lax.shift_right_logical(total + (CHUNK - 1), CHUNK.bit_length() - 1)
    lax.fori_loop(begin, end, chunk_step, 0)


def sort_kernel(count_ref, cell_ref, offset_ref, volume_ref, force_ref, out_ref, data_ref, hot_ref, prefix_ref, dest_ref, lhs_ref, total_ref):
    data_ref[0:1, :] = cell_ref[...].astype(jnp.float32)
    data_ref[1:4, :] = offset_ref[...]
    data_ref[4:5, :] = volume_ref[...]
    data_ref[5:8, :] = force_ref[...]
    live_count = count_ref[0, 0]
    block = 256
    blocks = PCAP // block
    bins = lax.broadcasted_iota(jnp.int32, (CY, block), 0)
    slots = lax.broadcasted_iota(jnp.int32, (1, block), 1)

    def hot_of(index):
        cut = slice(index * block, (index + 1) * block)
        home_row = lax.shift_right_logical(cell_ref[:, cut], 8) & 63
        return (bins == home_row) & (slots + index * block < live_count)

    for index in range(blocks):
        hot_ref[index * CY : (index + 1) * CY, :] = hot_of(index).astype(jnp.float32).astype(jnp.bfloat16)
    before = lax.broadcasted_iota(jnp.int32, (block, block), 0)
    after = lax.broadcasted_iota(jnp.int32, (block, block), 1)
    upto = (before <= after).astype(jnp.float32).astype(jnp.bfloat16)
    prefix_ref[...] = jnp.dot(hot_ref[...], upto, preferred_element_type=jnp.float32)
    carry = jnp.zeros((CY, 1), jnp.float32)
    carries = []
    for index in range(blocks):
        carries.append(carry)
        carry = carry + prefix_ref[index * CY : (index + 1) * CY, block - 1 : block]
    total = jnp.broadcast_to(carry, (CY, 128))
    row = lax.broadcasted_iota(jnp.int32, (CY, 128), 0)
    summed = total
    for shift in (1, 2, 4, 8, 16, 32):
        summed = summed + jnp.where(row >= shift, pltpu.roll(summed, shift, 0), 0.0)
    first = (summed - total)[:, 0:1]
    for index in range(blocks):
        cut = slice(index * block, (index + 1) * block)
        place = prefix_ref[index * CY : (index + 1) * CY, :] + (first + carries[index])
        hot = hot_of(index)
        dest = jnp.sum(jnp.where(hot, place, 0.0), axis=0, keepdims=True) - 1.0
        dest_ref[:, cut] = dest.astype(jnp.int32)

    total_ref[...] = jnp.zeros_like(total_ref)
    width = 512

    def route(index, unused):
        start = pl.multiple_of(index * width, width)
        dest = dest_ref[:, pl.ds(start, width)]
        high = lax.shift_right_arithmetic(dest, 8)
        low = dest & 255
        data = data_ref[:, pl.ds(start, width)]
        top = data.astype(jnp.bfloat16).astype(jnp.float32)
        rest = data - top
        middle = rest.astype(jnp.bfloat16).astype(jnp.float32)
        lanes = lax.broadcasted_iota(jnp.int32, (256, width), 0)
        rhs = (lanes == low).astype(jnp.float32).astype(jnp.bfloat16)
        wide = jnp.broadcast_to(high, (8, width))
        for split, values in enumerate((top, middle, rest - middle)):
            for pair in range(8):
                both = jnp.concatenate(
                    [
                        jnp.where(wide == 2 * pair, values, 0.0),
                        jnp.where(wide == 2 * pair + 1, values, 0.0),
                    ],
                    axis=0,
                )
                at = split * 128 + pair * 16
                lhs_ref[at : at + 16, :] = both.astype(jnp.bfloat16)
        total_ref[...] += lax.dot_general(
            lhs_ref[...], rhs, (((1,), (1,)), ((), ())), preferred_element_type=jnp.float32
        )
        return unused

    steps = lax.shift_right_logical(live_count + (width - 1), 9)
    lax.fori_loop(0, steps, route, 0)
    for part in range(16):
        at = part * 8
        out_ref[:, part * 256 : (part + 1) * 256] = (
            total_ref[at : at + 8, :] + total_ref[128 + at : 136 + at, :]
        ) + total_ref[256 + at : 264 + at, :]


def own_kernel(grid_rows, row_ref, parcels_ref, acc_ref, lhs_ref, rhs_ref):
    row_first = row_ref[0].astype(jnp.float32)
    acc_ref[...] = jnp.zeros_like(acc_ref)
    deposit(parcels_ref, 0, row_first, grid_rows, 0, 0, 14, 2, None, acc_ref, lhs_ref, rhs_ref)


def z_kernel(grid_rows, row_ref, below_ref, above_ref, held_ref, acc_ref, lhs_ref, rhs_ref):
    row_first = row_ref[0].astype(jnp.float32)
    acc_ref[...] = held_ref[...]
    deposit(below_ref, 0, row_first, grid_rows, -CZ, 0, 8, 0, None, acc_ref, lhs_ref, rhs_ref)
    deposit(above_ref, 0, row_first, grid_rows, CZ, 0, 8, 10, None, acc_ref, lhs_ref, rhs_ref)


def beside_y(row_first, grid_rows, south_ref, north_ref, acc_ref, lhs_ref, rhs_ref):
    for parcels_ref, shift_y, window in (
        (south_ref, -CY, LEAD - REACH),
        (north_ref, CY, LEAD + CY - 3),
    ):
        for part, (shift_z, planes, plane_first) in enumerate(((0, 14, 2), (-CZ, 8, 0), (CZ, 8, 10))):
            deposit(
                parcels_ref, 8 * part, row_first, grid_rows, shift_z, shift_y, planes, plane_first,
                window, acc_ref, lhs_ref, rhs_ref,
            )


MID = slice(4, 76)
LOW = slice(3, 75)
HIGH = slice(5, 77)
OWN = slice(LEAD, LEAD + CY)


def x_pair(left, right):
    lane = lax.broadcasted_iota(jnp.int32, left.shape, 1)
    start, stop = lane == 0, lane == HALF - 1
    left_west, right_west = pltpu.roll(left, 1, 1), pltpu.roll(right, 1, 1)
    left_east, right_east = pltpu.roll(left, HALF - 1, 1), pltpu.roll(right, HALF - 1, 1)
    return (
        jnp.where(start, 0.0, left_west) + jnp.where(stop, right_east, left_east),
        jnp.where(start, left_west, right_west) + jnp.where(stop, 0.0, right_east),
    )


def x_slope(left, right):
    lane = lax.broadcasted_iota(jnp.int32, left.shape, 1)
    start, stop = lane == 0, lane == HALF - 1
    left_west, right_west = pltpu.roll(left, 1, 1), pltpu.roll(right, 1, 1)
    left_east, right_east = pltpu.roll(left, HALF - 1, 1), pltpu.roll(right, HALF - 1, 1)
    return (
        jnp.where(stop, right_east, left_east) - jnp.where(start, 0.0, left_west),
        jnp.where(stop, 0.0, right_east) - jnp.where(start, left_west, right_west),
    )


def beside_of(ref, plane):
    centre = [ref[plane, half, MID, :] for half in range(2)]
    pairs = x_pair(*centre)
    sums = [
        (ref[plane - 1, half, MID, :] + ref[plane + 1, half, MID, :])
        + (ref[plane, half, LOW, :] + ref[plane, half, HIGH, :])
        + pairs[half]
        for half in range(2)
    ]
    return centre, sums


def field_kernel(
    grid_rows,
    row_ref,
    south_ref,
    north_ref,
    held_ref,
    density_ref,
    guess_ref,
    diverge_ref,
    fraction_ref,
    momentum_ref,
    residual_ref,
    direction_ref,
    mapped_ref,
    scaled_ref,
    mobility_ref,
    diagonal_ref,
    dots_ref,
    first_ref,
    second_ref,
    mob_ref,
    held_guess_ref,
    wide_ref,
    rate_ref,
    lhs_ref,
    rhs_ref,
):
    row_first = row_ref[0].astype(jnp.float32)
    first_ref[...] = held_ref[...]
    beside_y(row_first, grid_rows, south_ref, north_ref, first_ref, lhs_ref, rhs_ref)

    row = lax.broadcasted_iota(jnp.int32, (YE, HALF), 0).astype(jnp.float32) + (row_first - LEAD)
    lane = lax.broadcasted_iota(jnp.int32, (YE, HALF), 1)
    within = (row >= 0.0) & (row < grid_rows)
    inside = within.astype(jnp.float32)
    count_y = (row >= 1.0).astype(jnp.float32) + (row < grid_rows - 1.0).astype(jnp.float32)
    for half in range(2):
        count_x = 2.0 - (lane == (0, HALF - 1)[half]).astype(jnp.float32)
        rate_ref[half] = inside * (1.0 - smooth_rate * (2.0 + count_y + count_x))
    rate_ref[2] = inside * smooth_rate
    for index, reach in enumerate((2.0, 1.0, 0.0)):
        near = within & (row >= row_first - reach) & (row < row_first + (CY + reach))
        rate_ref[3 + index] = near.astype(jnp.float32)

    for sweep, (source, target) in enumerate(
        ((first_ref, second_ref), (second_ref, first_ref), (first_ref, second_ref))
    ):

        def sweep_step(plane, carry, source=source, target=target):
            for field in range(4):
                centre, sums = beside_of(source.at[field], plane)
                for half in range(2):
                    target[field, plane, half, MID, :] = (
                        rate_ref[half, MID, :] * centre[half] + rate_ref[2, MID, :] * sums[half]
                    )
            return carry

        lax.fori_loop(sweep + 1, ZE - 1 - sweep, sweep_step, 0)

    filtered = second_ref

    def mobility_step(plane, carry):
        known = rate_ref[3] > 0.5
        for half in range(2):
            cut = slice(half * HALF, (half + 1) * HALF)
            fraction = 1.0 / (1.0 + filtered[0, plane + 3, half])
            mobility = jnp.where(known, fraction / density_ref[plane, :, cut], 0.0)
            guess = guess_ref[plane, :, cut]
            mob_ref[plane, half] = mobility
            held_guess_ref[plane, half] = guess
            wide_ref[plane, half] = mobility * guess
        return carry

    lax.fori_loop(0, CZ + 4, mobility_step, 0)

    def output_step(plane, carry):
        for half in range(2):
            cut = slice(half * HALF, (half + 1) * HALF)
            fraction_ref[plane, :, cut] = 1.0 / (1.0 + filtered[0, plane + REACH, half, OWN, :])
            for part in range(3):
                momentum_ref[plane, part, :, cut] = filtered[part + 1, plane + REACH, half, OWN, :]
        return carry

    lax.fori_loop(0, CZ, output_step, 0)

    direct_ref, product_ref, remain_ref = first_ref.at[0], first_ref.at[1], first_ref.at[2]

    def first_residual(plane, carry):
        at = plane + 1
        near = rate_ref[4, MID, :] > 0.5
        mobility, beside_mobility = beside_of(mob_ref, at)
        guess, beside_guess = beside_of(held_guess_ref, at)
        unused, beside_wide = beside_of(wide_ref, at)
        slope = x_slope(filtered[3, at + 3, 0, MID, :], filtered[3, at + 3, 1, MID, :])
        for half in range(2):
            cut = slice(half * HALF, (half + 1) * HALF)
            diagonal = (3.0 + stiffness) * mobility[half] + 0.5 * beside_mobility[half]
            operated = diagonal * guess[half] - 0.5 * (
                mobility[half] * beside_guess[half] + beside_wide[half]
            )
            spread = 0.5 * (filtered[1, at + 4, half, MID, :] - filtered[1, at + 2, half, MID, :])
            spread = spread + 0.5 * (
                filtered[2, at + 3, half, HIGH, :] - filtered[2, at + 3, half, LOW, :]
            )
            spread = spread + 0.5 * slope[half]
            residual = jnp.where(near, diverge_ref[plane, MID, cut] - spread - operated, 0.0)
            direction = jnp.where(near, residual / diagonal, 0.0)
            remain_ref[plane, half, MID, :] = residual
            direct_ref[plane, half, MID, :] = direction
            product_ref[plane, half, MID, :] = direction * mobility[half]
            diagonal_ref[plane, half, MID, :] = diagonal
            mobility_ref[plane, half, MID, :] = mobility[half]
        return carry

    lax.fori_loop(0, CZ + 2, first_residual, 0)

    scaled_ref[...] = jnp.zeros_like(scaled_ref)

    def map_step(plane, sums):
        at = plane + 1
        own = rate_ref[5, MID, :] > 0.5
        directions, beside_direction = beside_of(direct_ref, at)
        unused, beside_product = beside_of(product_ref, at)
        sum_rz, sum_dw, sum_uw = sums
        for half in range(2):
            residual = jnp.where(own, remain_ref[at, half, MID, :], 0.0)
            diagonal = diagonal_ref[at, half, MID, :]
            mapped = diagonal * directions[half] - 0.5 * (
                mobility_ref[at, half, MID, :] * beside_direction[half] + beside_product[half]
            )
            mapped = jnp.where(own, mapped, 0.0)
            scaled = jnp.where(own, mapped / diagonal, 0.0)
            scaled_ref[at, half, MID, :] = scaled
            residual_ref[plane, half] = residual[4:68]
            direction_ref[plane, half] = directions[half][4:68]
            mapped_ref[plane, half] = mapped[4:68]
            sum_rz = sum_rz + residual * directions[half]
            sum_dw = sum_dw + directions[half] * mapped
            sum_uw = sum_uw + scaled * mapped
        return sum_rz, sum_dw, sum_uw

    zero = jnp.zeros((72, HALF), jnp.float32)
    sums = lax.fori_loop(0, CZ, map_step, (zero, zero, zero))
    for index in range(3):
        dots_ref[index] = jnp.sum(sums[index])


def second_kernel(dots_ref, scaled_ref, below_ref, above_ref, south_ref, north_ref, mobility_ref, diagonal_ref, twice_ref, sent_ref, held_ref, product_ref):
    held_ref[...] = scaled_ref[...]
    held_ref[0, :, OWN, :] = below_ref[...]
    held_ref[CZ + 1, :, OWN, :] = above_ref[...]
    for plane in range(CZ):
        for half in range(2):
            held_ref[plane + 1, half, LEAD - 1 : LEAD, :] = south_ref[plane, half : half + 1]
            held_ref[plane + 1, half, LEAD + CY : LEAD + CY + 1, :] = north_ref[plane, half : half + 1]

    def product_step(plane, carry):
        for half in range(2):
            product_ref[plane, half] = held_ref[plane, half] * mobility_ref[plane, half]
        return carry

    lax.fori_loop(0, CZ + 2, product_step, 0)

    def map_step(plane, total):
        at = plane + 1
        centre, beside = beside_of(held_ref, at)
        unused, beside_product = beside_of(product_ref, at)
        for half in range(2):
            twice = diagonal_ref[at, half, MID, :] * centre[half] - 0.5 * (
                mobility_ref[at, half, MID, :] * beside[half] + beside_product[half]
            )
            twice_ref[plane, half] = twice[4:68]
            total = total + (centre[half] * twice)[4:68]
        return total

    total = lax.fori_loop(0, CZ, map_step, jnp.zeros((CY, HALF), jnp.float32))
    values = (dots_ref[0], dots_ref[1], dots_ref[2], jnp.sum(total))
    column = lax.broadcasted_iota(jnp.int32, sent_ref.shape, 1)
    sent = jnp.zeros(sent_ref.shape, jnp.float32)
    for index, value in enumerate(values):
        sent = jnp.where(column == index, value, sent)
    sent_ref[...] = sent


def final_kernel(got_ref, guess_ref, residual_ref, direction_ref, mapped_ref, scaled_ref, twice_ref, pressure_ref, final_ref):
    sums = jnp.sum(got_ref[...], axis=0, keepdims=True)
    sum_rz, sum_dw, sum_uw, sum_uv = (sums[:, index : index + 1] for index in range(4))
    step = sum_rz / sum_dw
    next_rz = sum_rz - 2.0 * step * sum_dw + step * step * sum_uw
    along = 1.0 + next_rz / sum_rz
    curvature = along * along * sum_dw - 2.0 * step * along * sum_uw + step * step * sum_uv
    next_step = next_rz / curvature
    first = step + next_step * along
    last = next_step * step

    def write_step(plane, carry):
        for half in range(2):
            cut = slice(half * HALF, (half + 1) * HALF)
            pressure_ref[plane, :, cut] = (
                guess_ref[plane, :, cut]
                + first * direction_ref[plane, half]
                - last * scaled_ref[plane + 1, half, OWN, :]
            )
            final_ref[plane, :, cut] = (
                residual_ref[plane, half] - first * mapped_ref[plane, half] + last * twice_ref[plane, half]
            )
        return carry

    lax.fori_loop(0, CZ, write_step, 0)


def vmem_spec():
    return pl.BlockSpec(memory_space=pltpu.VMEM)


def smem_spec():
    return pl.BlockSpec(memory_space=pltpu.SMEM)


def f32(*shape):
    return jax.ShapeDtypeStruct(shape, jnp.float32)


def params():
    return pltpu.CompilerParams(vmem_limit_bytes=VMEM_LIMIT)


def deposit_scratch():
    return [
        pltpu.VMEM((4 * 14 * TALL, CHUNK), jnp.bfloat16),
        pltpu.VMEM((CX, CHUNK), jnp.bfloat16),
    ]


def on_device(
    parcel_cell,
    parcel_offset,
    parcel_volume,
    parcel_force,
    brick_counts,
    divergence,
    pressure_prev,
    gas_density,
):
    size_z = lax.axis_size("gz")
    size_y = lax.axis_size("gy")
    grid_rows = float(size_y * CY)
    row_first = (lax.axis_index("gy") * CY).astype(jnp.int32)[None]
    up_z = [(i, (i + 1) % size_z) for i in range(size_z)]
    down_z = [((i + 1) % size_z, i) for i in range(size_z)]
    up_y = [(i, i + 1) for i in range(size_y - 1)]
    down_y = [(i + 1, i) for i in range(size_y - 1)]

    parcels = pl.pallas_call(
        sort_kernel,
        out_shape=f32(8, PCAP),
        in_specs=[smem_spec()] + [vmem_spec()] * 4,
        out_specs=vmem_spec(),
        scratch_shapes=[
            pltpu.VMEM((8, PCAP), jnp.float32),
            pltpu.VMEM((PCAP // 256 * CY, 256), jnp.bfloat16),
            pltpu.VMEM((PCAP // 256 * CY, 256), jnp.float32),
            pltpu.VMEM((1, PCAP), jnp.int32),
            pltpu.VMEM((384, 512), jnp.bfloat16),
            pltpu.VMEM((384, 256), jnp.float32),
        ],
        compiler_params=params(),
        name="order",
    )(brick_counts, parcel_cell[None], parcel_offset, parcel_volume[None], parcel_force)
    parcels_below = lax.ppermute(parcels, "gz", up_z)
    parcels_above = lax.ppermute(parcels, "gz", down_z)
    stack_z_head = jnp.concatenate([pressure_prev[:2], gas_density[:2], divergence[:1]], axis=0)
    stack_z_tail = jnp.concatenate([pressure_prev[-2:], gas_density[-2:], divergence[-1:]], axis=0)
    below = lax.ppermute(stack_z_tail, "gz", up_z)
    above = lax.ppermute(stack_z_head, "gz", down_z)
    trio = jnp.concatenate([parcels, parcels_below, parcels_above], axis=0)
    trio_south = lax.ppermute(trio, "gy", up_y)
    trio_north = lax.ppermute(trio, "gy", down_y)

    guess = jnp.concatenate([below[0:2], pressure_prev, above[0:2]], axis=0)
    density = jnp.concatenate([below[2:4], gas_density, above[2:4]], axis=0)
    diverge = jnp.concatenate([below[4:5], divergence, above[4:5]], axis=0)
    stack_y_head = jnp.concatenate([guess[:, :2], density[:, :2], jnp.pad(diverge[:, :1], ((1, 1), (0, 0), (0, 0)))], axis=1)
    stack_y_tail = jnp.concatenate([guess[:, -2:], density[:, -2:], jnp.pad(diverge[:, -1:], ((1, 1), (0, 0), (0, 0)))], axis=1)
    south = lax.ppermute(stack_y_tail, "gy", up_y)
    north = lax.ppermute(stack_y_head, "gy", down_y)

    def widened(values, low, high):
        depth = low.shape[1]
        return jnp.pad(
            jnp.concatenate([low, values, high], axis=1),
            ((0, 0), (LEAD - depth, YE - LEAD - CY - depth), (0, 0)),
        )

    guess = widened(guess, south[:, 0:2], north[:, 0:2])
    density = widened(density, south[:, 2:4], north[:, 2:4])
    diverge = widened(diverge, south[1:-1, 4:5], north[1:-1, 4:5])

    acc = pl.pallas_call(
        functools.partial(own_kernel, grid_rows),
        out_shape=f32(4, ZE, 2, YE, HALF),
        in_specs=[smem_spec(), vmem_spec()],
        out_specs=vmem_spec(),
        scratch_shapes=deposit_scratch(),
        compiler_params=params(),
        cost_estimate=pl.CostEstimate(flops=8_000_000_000, bytes_accessed=6_000_000, transcendentals=0),
        name="own",
    )(row_first, parcels)
    acc = pl.pallas_call(
        functools.partial(z_kernel, grid_rows),
        out_shape=f32(4, ZE, 2, YE, HALF),
        in_specs=[smem_spec(), vmem_spec(), vmem_spec(), vmem_spec()],
        out_specs=vmem_spec(),
        scratch_shapes=deposit_scratch(),
        compiler_params=params(),
        cost_estimate=pl.CostEstimate(flops=8_000_000_000, bytes_accessed=6_000_000, transcendentals=0),
        name="beside_z",
    )(row_first, parcels_below, parcels_above, acc)
    halves = f32(CZ, 2, CY, HALF)
    wider = f32(CZ + 2, 2, YE, HALF)
    fraction, momentum, residual, direction, mapped, scaled, mobility, diagonal, dots = pl.pallas_call(
        functools.partial(field_kernel, grid_rows),
        out_shape=(
            f32(CZ, CY, CX),
            f32(CZ, 3, CY, CX),
            halves,
            halves,
            halves,
            wider,
            wider,
            wider,
            f32(3),
        ),
        in_specs=[smem_spec()] + [vmem_spec()] * 6,
        out_specs=tuple([vmem_spec()] * 8 + [smem_spec()]),
        scratch_shapes=[
            pltpu.VMEM((4, ZE, 2, YE, HALF), jnp.float32),
            pltpu.VMEM((4, ZE, 2, YE, HALF), jnp.float32),
            pltpu.VMEM((CZ + 4, 2, YE, HALF), jnp.float32),
            pltpu.VMEM((CZ + 4, 2, YE, HALF), jnp.float32),
            pltpu.VMEM((CZ + 4, 2, YE, HALF), jnp.float32),
            pltpu.VMEM((6, YE, HALF), jnp.float32),
        ]
        + deposit_scratch(),
        compiler_params=params(),
        name="fields",
    )(row_first, trio_south, trio_north, acc, density, guess, diverge)

    scaled_below = lax.ppermute(scaled[CZ, :, OWN], "gz", up_z)
    scaled_above = lax.ppermute(scaled[1, :, OWN], "gz", down_z)
    scaled_south = lax.ppermute(scaled[1:-1, :, LEAD + CY - 1], "gy", up_y)
    scaled_north = lax.ppermute(scaled[1:-1, :, LEAD], "gy", down_y)
    every = size_z * size_y
    twice, sent = pl.pallas_call(
        second_kernel,
        out_shape=(halves, f32(every, 128)),
        in_specs=[smem_spec()] + [vmem_spec()] * 7,
        out_specs=(vmem_spec(), vmem_spec()),
        scratch_shapes=[
            pltpu.VMEM((CZ + 2, 2, YE, HALF), jnp.float32),
            pltpu.VMEM((CZ + 2, 2, YE, HALF), jnp.float32),
        ],
        compiler_params=params(),
        name="second",
    )(dots, scaled, scaled_below, scaled_above, scaled_south, scaled_north, mobility, diagonal)
    got = lax.all_to_all(sent, ("gz", "gy"), 0, 0, tiled=True)
    pressure, final = pl.pallas_call(
        final_kernel,
        out_shape=(f32(CZ, CY, CX), f32(CZ, CY, CX)),
        in_specs=[vmem_spec()] * 7,
        out_specs=(vmem_spec(), vmem_spec()),
        compiler_params=params(),
        name="final",
    )(got, pressure_prev, residual, direction, mapped, scaled, twice)
    return (fraction, momentum, pressure, final)


def solution(mesh):
    return jax.shard_map(
        on_device,
        mesh=mesh,
        in_specs=(
            P(("gz", "gy")),
            P(None, ("gz", "gy")),
            P(("gz", "gy")),
            P(None, ("gz", "gy")),
            P("gz", "gy"),
            P("gz", "gy", None),
            P("gz", "gy", None),
            P("gz", "gy", None),
        ),
        out_specs=(
            P("gz", "gy", None),
            P("gz", None, "gy", None),
            P("gz", "gy", None),
            P("gz", "gy", None),
        ),
        check_vma=False,
    )
```

```python
import functools

import jax
import jax.numpy as jnp
from jax import lax
from jax.experimental import pallas as pl
from jax.experimental.pallas import tpu as pltpu
from jax.sharding import PartitionSpec as P

CZ = 8
CY = 64
CX = 256
PCAP = 4096
ITERS = 2
REACH = 5
ZE = CZ + 2 * REACH
YE = 88
LEAD = 12
LIST = PCAP // 256
TILES = CY // 8
HALF = 128
CHUNK = 256
TALL = 24

smooth_rate = 0.15
stiffness = 0.002

VMEM_LIMIT = 48 * 1024 * 1024


def chunk_values(parcels, grid_rows, row_first, shift_y):
    cell = parcels[0:1].astype(jnp.int32)
    home_z = lax.shift_right_logical(cell, 14).astype(jnp.float32)
    home_y = (lax.shift_right_logical(cell, 8) & 63).astype(jnp.float32)
    home_x = (cell & 255).astype(jnp.float32)
    count = parcels.shape[1]
    taps = lax.broadcasted_iota(jnp.int32, (8, count), 0).astype(jnp.float32) - 3.0

    def tap_sum(offset, inside):
        distance = taps + 0.5 - offset
        weight = jnp.where(inside, jnp.exp(-0.5 * distance * distance), 0.0)
        return 1.0 / jnp.sum(weight, axis=0, keepdims=True)

    seven = taps < 3.5
    place_y = taps + (home_y + (row_first + shift_y))
    place_x = taps + home_x
    inv_z = tap_sum(parcels[1:2], seven)
    inv_y = tap_sum(parcels[2:3], seven & (place_y >= 0.0) & (place_y < grid_rows))
    inv_x = tap_sum(parcels[3:4], seven & (place_x >= 0.0) & (place_x < float(CX)))
    return home_z, home_y, home_x, inv_z, inv_y, inv_x


def axis_rows(rows, first, home, offset, inverse):
    place = lax.broadcasted_iota(jnp.int32, (rows, home.shape[1]), 0).astype(jnp.float32) + first
    tap = place - home
    distance = tap + 0.5 - offset
    weight = jnp.exp(-0.5 * distance * distance) * inverse
    return jnp.where(jnp.abs(tap) < 3.5, weight, 0.0), place


def row_of(cell):
    return lax.shift_right_logical(cell.astype(jnp.int32), 8) & 63


def count_where(condition):
    return jnp.sum(condition.astype(jnp.float32)).astype(jnp.int32)


def deposit(parcels_ref, base, row_first, grid_rows, shift_z, shift_y, planes, plane_first, window, acc_ref, lhs_ref, rhs_ref):
    rows = TALL if window is None else 8
    volume = parcels_ref[base : base + LIST, 4, :]
    begin = 0
    if shift_y == 0:
        total = count_where(volume != 0.0)
    else:
        home_row = row_of(parcels_ref[base : base + LIST, 0, :])
        if shift_y < 0:
            total = count_where(volume != 0.0)
            begin = lax.shift_right_logical(
                count_where((volume != 0.0) & (home_row < CY - 3 - REACH)), CHUNK.bit_length() - 1
            )
        else:
            total = count_where((volume != 0.0) & (home_row < 3 + REACH))

    def chunk_step(index, carry):
        start = index * CHUNK
        parcels = parcels_ref[base + index]
        home_z, home_y, home_x, inv_z, inv_y, inv_x = chunk_values(
            parcels, grid_rows, row_first, float(shift_y)
        )
        block = 64
        for part in range(CX // block):
            weight_x, unused = axis_rows(block, float(part * block), home_x, parcels[3:4], inv_x)
            rhs_ref[part * block : (part + 1) * block, :] = weight_x.astype(jnp.bfloat16)
        rows_z = -(-planes // 8) * 8
        weight_z, unused = axis_rows(
            rows_z, float(plane_first - REACH - shift_z), home_z, parcels[1:2], inv_z
        )
        loaded = [
            weight_z * (parcels[4:5] if field == 0 else parcels[4:5] * parcels[4 + field : 5 + field])
            for field in range(4)
        ]

        def spread_window(first, least):
            weight_y, place_y = axis_rows(
                rows, first - (LEAD + shift_y), home_y, parcels[2:3], inv_y
            )
            global_y = place_y + (row_first + shift_y)
            inside = (global_y >= 0.0) & (global_y < grid_rows)
            if least is not None:
                inside = inside & (place_y >= least - LEAD)
            weight_y = jnp.where(inside, weight_y, 0.0)
            for field in range(4):
                for pair in range(planes // 2):
                    both = jnp.concatenate(
                        [
                            loaded[field][2 * pair : 2 * pair + 1] * weight_y,
                            loaded[field][2 * pair + 1 : 2 * pair + 2] * weight_y,
                        ],
                        axis=0,
                    )
                    at = (field * planes + 2 * pair) * rows
                    lhs_ref[at : at + 2 * rows, :] = both.astype(jnp.bfloat16)

        def add_window(first):
            for field in range(4):
                product = lax.dot_general(
                    lhs_ref[field * planes * rows : (field + 1) * planes * rows, :],
                    rhs_ref[...],
                    (((1,), (1,)), ((), ())),
                    preferred_element_type=jnp.float32,
                )
                for plane in range(planes):
                    for half in range(2):
                        acc_ref[field, plane_first + plane, half, pl.ds(first, rows), :] += product[
                            plane * rows : (plane + 1) * rows, half * HALF : (half + 1) * HALF
                        ]

        if window is not None:
            spread_window(float(window), None)
            add_window(window)
            return carry

        slot = lax.broadcasted_iota(jnp.int32, (1, CHUNK), 1) + start
        lowest = jnp.min(jnp.where(slot < total, home_y, float(CY))).astype(jnp.int32)
        highest = jnp.max(jnp.where(slot < total, home_y, 0.0)).astype(jnp.int32)
        row_low = lax.shift_right_logical(lowest + (LEAD - 3), 3) * 8
        row_high = highest + (LEAD + 4)

        def window_step(carried):
            logical = carried
            first = pl.multiple_of(jnp.minimum(logical, YE - TALL), 8)
            spread_window(first.astype(jnp.float32), logical.astype(jnp.float32))
            add_window(first)
            return logical + TALL

        lax.while_loop(lambda carried: carried < row_high, window_step, row_low)
        return carry

    end = lax.shift_right_logical(total + (CHUNK - 1), CHUNK.bit_length() - 1)
    lax.fori_loop(begin, end, chunk_step, 0)


def sort_kernel(count_ref, cell_ref, offset_ref, volume_ref, force_ref, guess_head_ref, guess_tail_ref, density_head_ref, density_tail_ref, diverge_head_ref, diverge_tail_ref, up_ref, down_ref, data_ref, hot_ref, prefix_ref, dest_ref, lhs_ref, total_ref):
    data_ref[0:1, :] = cell_ref[...].astype(jnp.float32)
    data_ref[1:4, :] = offset_ref[...]
    data_ref[4:5, :] = volume_ref[...]
    data_ref[5:8, :] = force_ref[...]
    edges = (
        (up_ref, (guess_tail_ref, density_tail_ref, diverge_tail_ref)),
        (down_ref, (guess_head_ref, density_head_ref, diverge_head_ref)),
    )
    for out_ref, sources in edges:
        at = LIST
        for source in sources:
            for plane in range(source.shape[0]):
                for tile in range(TILES):
                    out_ref[at] = source[plane, tile * 8 : (tile + 1) * 8, :]
                    at += 1
    live_count = count_ref[0, 0]
    block = 256
    blocks = PCAP // block
    bins = lax.broadcasted_iota(jnp.int32, (CY, block), 0)
    slots = lax.broadcasted_iota(jnp.int32, (1, block), 1)

    def hot_of(index):
        cut = slice(index * block, (index + 1) * block)
        home_row = lax.shift_right_logical(cell_ref[:, cut], 8) & 63
        return (bins == home_row) & (slots + index * block < live_count)

    for index in range(blocks):
        hot_ref[index * CY : (index + 1) * CY, :] = hot_of(index).astype(jnp.float32).astype(jnp.bfloat16)
    before = lax.broadcasted_iota(jnp.int32, (block, block), 0)
    after = lax.broadcasted_iota(jnp.int32, (block, block), 1)
    upto = (before <= after).astype(jnp.float32).astype(jnp.bfloat16)
    prefix_ref[...] = jnp.dot(hot_ref[...], upto, preferred_element_type=jnp.float32)
    carry = jnp.zeros((CY, 1), jnp.float32)
    carries = []
    for index in range(blocks):
        carries.append(carry)
        carry = carry + prefix_ref[index * CY : (index + 1) * CY, block - 1 : block]
    total = jnp.broadcast_to(carry, (CY, 128))
    row = lax.broadcasted_iota(jnp.int32, (CY, 128), 0)
    summed = total
    for shift in (1, 2, 4, 8, 16, 32):
        summed = summed + jnp.where(row >= shift, pltpu.roll(summed, shift, 0), 0.0)
    first = (summed - total)[:, 0:1]
    for index in range(blocks):
        cut = slice(index * block, (index + 1) * block)
        place = prefix_ref[index * CY : (index + 1) * CY, :] + (first + carries[index])
        hot = hot_of(index)
        dest = jnp.sum(jnp.where(hot, place, 0.0), axis=0, keepdims=True) - 1.0
        dest_ref[:, cut] = dest.astype(jnp.int32)

    total_ref[...] = jnp.zeros_like(total_ref)
    width = 512

    def route(index, unused):
        start = pl.multiple_of(index * width, width)
        dest = dest_ref[:, pl.ds(start, width)]
        high = lax.shift_right_arithmetic(dest, 8)
        low = dest & 255
        data = data_ref[:, pl.ds(start, width)]
        top = data.astype(jnp.bfloat16).astype(jnp.float32)
        rest = data - top
        middle = rest.astype(jnp.bfloat16).astype(jnp.float32)
        lanes = lax.broadcasted_iota(jnp.int32, (256, width), 0)
        rhs = (lanes == low).astype(jnp.float32).astype(jnp.bfloat16)
        wide = jnp.broadcast_to(high, (8, width))
        for split, values in enumerate((top, middle, rest - middle)):
            for pair in range(8):
                both = jnp.concatenate(
                    [
                        jnp.where(wide == 2 * pair, values, 0.0),
                        jnp.where(wide == 2 * pair + 1, values, 0.0),
                    ],
                    axis=0,
                )
                at = split * 128 + pair * 16
                lhs_ref[at : at + 16, :] = both.astype(jnp.bfloat16)
        total_ref[...] += lax.dot_general(
            lhs_ref[...], rhs, (((1,), (1,)), ((), ())), preferred_element_type=jnp.float32
        )
        return unused

    steps = lax.shift_right_logical(live_count + (width - 1), 9)
    lax.fori_loop(0, steps, route, 0)
    for part in range(LIST):
        at = part * 8
        sorted_part = (
            total_ref[at : at + 8, :] + total_ref[128 + at : 136 + at, :]
        ) + total_ref[256 + at : 264 + at, :]
        up_ref[part] = sorted_part
        down_ref[part] = sorted_part


def extended_row(own_ref, below_ref, above_ref, part, depth, plane, row):
    first = (0, 2, 4)[part]
    if depth <= plane < CZ + depth:
        return own_ref[plane - depth, row : row + 1, :]
    ref, inner = (below_ref, plane) if plane < depth else (above_ref, plane - CZ - depth)
    tile = LIST + (first + inner) * TILES + row // 8
    return ref[tile, row % 8 : row % 8 + 1, :]


FIELDS = ((2, 2), (2, 2), (1, 1))


def pack_kernel(sorted_ref, below_ref, above_ref, guess_ref, density_ref, diverge_ref, north_ref, south_ref):
    for out_ref, last in ((north_ref, True), (south_ref, False)):
        for index, source in enumerate((sorted_ref, below_ref, above_ref)):
            out_ref[index * LIST : (index + 1) * LIST] = source[0:LIST]
        slot = 0
        for part, (own_ref, (depth, wide)) in enumerate(zip((guess_ref, density_ref, diverge_ref), FIELDS)):
            for plane in range(CZ + 2 * depth):
                for row in range(wide):
                    place = CY - wide + row if last else row
                    out_ref[3 * LIST + slot // 8, slot % 8 : slot % 8 + 1, :] = extended_row(
                        own_ref, below_ref, above_ref, part, depth, plane, place
                    )
                    slot += 1
        out_ref[3 * LIST + 7, 2:8, :] = jnp.zeros((6, CX), jnp.float32)


def own_kernel(grid_rows, row_ref, parcels_ref, acc_ref, lhs_ref, rhs_ref):
    row_first = row_ref[0].astype(jnp.float32)
    acc_ref[...] = jnp.zeros_like(acc_ref)
    deposit(parcels_ref, 0, row_first, grid_rows, 0, 0, 14, 2, None, acc_ref, lhs_ref, rhs_ref)


def gather_fields(south_ref, north_ref, below_ref, above_ref, sources, targets):
    slot = 0
    for part, (own_ref, out_ref, (depth, wide)) in enumerate(zip(sources, targets, FIELDS)):
        first = (0, 2, 4)[part]
        for plane in range(CZ + 2 * depth):
            for half in range(2):
                cut = slice(half * HALF, (half + 1) * HALF)
                if depth <= plane < CZ + depth:
                    out_ref[plane, half, OWN, :] = own_ref[plane - depth, :, cut]
                else:
                    ref, inner = (below_ref, plane) if plane < depth else (above_ref, plane - CZ - depth)
                    at = LIST + (first + inner) * TILES
                    for tile in range(TILES):
                        out_ref[plane, half, LEAD + 8 * tile : LEAD + 8 * tile + 8, :] = ref[at + tile, :, cut]
                edge = 3 * LIST + slot // 8
                inner_rows = slice(slot % 8, slot % 8 + wide)
                out_ref[plane, half, LEAD - wide : LEAD, :] = south_ref[edge, inner_rows, cut]
                out_ref[plane, half, LEAD + CY : LEAD + CY + wide, :] = north_ref[edge, inner_rows, cut]
            slot += wide


def beside_y(row_first, grid_rows, south_ref, north_ref, acc_ref, lhs_ref, rhs_ref):
    for parcels_ref, shift_y, window in (
        (south_ref, -CY, LEAD - REACH),
        (north_ref, CY, LEAD + CY - 3),
    ):
        for part, (shift_z, planes, plane_first) in enumerate(((0, 14, 2), (-CZ, 8, 0), (CZ, 8, 10))):
            deposit(
                parcels_ref, LIST * part, row_first, grid_rows, shift_z, shift_y, planes, plane_first,
                window, acc_ref, lhs_ref, rhs_ref,
            )


MID = slice(8, 80)
LOW = slice(7, 79)
HIGH = slice(9, 81)
OWN = slice(LEAD, LEAD + CY)


def x_pair(left, right):
    lane = lax.broadcasted_iota(jnp.int32, left.shape, 1)
    start, stop = lane == 0, lane == HALF - 1
    left_west, right_west = pltpu.roll(left, 1, 1), pltpu.roll(right, 1, 1)
    left_east, right_east = pltpu.roll(left, HALF - 1, 1), pltpu.roll(right, HALF - 1, 1)
    return (
        jnp.where(start, 0.0, left_west) + jnp.where(stop, right_east, left_east),
        jnp.where(start, left_west, right_west) + jnp.where(stop, 0.0, right_east),
    )


def x_slope(left, right):
    lane = lax.broadcasted_iota(jnp.int32, left.shape, 1)
    start, stop = lane == 0, lane == HALF - 1
    left_west, right_west = pltpu.roll(left, 1, 1), pltpu.roll(right, 1, 1)
    left_east, right_east = pltpu.roll(left, HALF - 1, 1), pltpu.roll(right, HALF - 1, 1)
    return (
        jnp.where(stop, right_east, left_east) - jnp.where(start, 0.0, left_west),
        jnp.where(stop, 0.0, right_east) - jnp.where(start, left_west, right_west),
    )


def beside_of(ref, plane):
    centre = [ref[plane, half, MID, :] for half in range(2)]
    pairs = x_pair(*centre)
    sums = [
        (ref[plane - 1, half, MID, :] + ref[plane + 1, half, MID, :])
        + (ref[plane, half, LOW, :] + ref[plane, half, HIGH, :])
        + pairs[half]
        for half in range(2)
    ]
    return centre, sums


def field_kernel(
    grid_rows,
    row_ref,
    below_ref,
    above_ref,
    south_ref,
    north_ref,
    acc_ref,
    density_own_ref,
    guess_own_ref,
    diverge_own_ref,
    fraction_ref,
    momentum_ref,
    residual_ref,
    direction_ref,
    mapped_ref,
    scaled_ref,
    mobility_ref,
    diagonal_ref,
    dots_ref,
    first_ref,
    second_ref,
    mob_ref,
    guess_ref,
    wide_ref,
    density_ref,
    diverge_ref,
    rate_ref,
    lhs_ref,
    rhs_ref,
    load_sem,
):
    row_first = row_ref[0].astype(jnp.float32)
    load = pltpu.make_async_copy(acc_ref, first_ref, load_sem)
    load.start()
    gather_fields(
        south_ref,
        north_ref,
        below_ref,
        above_ref,
        (guess_own_ref, density_own_ref, diverge_own_ref),
        (guess_ref, density_ref, diverge_ref),
    )
    load.wait()
    deposit(below_ref, 0, row_first, grid_rows, -CZ, 0, 8, 0, None, first_ref, lhs_ref, rhs_ref)
    deposit(above_ref, 0, row_first, grid_rows, CZ, 0, 8, 10, None, first_ref, lhs_ref, rhs_ref)
    beside_y(row_first, grid_rows, south_ref, north_ref, first_ref, lhs_ref, rhs_ref)

    row = lax.broadcasted_iota(jnp.int32, (YE, HALF), 0).astype(jnp.float32) + (row_first - LEAD)
    lane = lax.broadcasted_iota(jnp.int32, (YE, HALF), 1)
    within = (row >= 0.0) & (row < grid_rows)
    inside = within.astype(jnp.float32)
    count_y = (row >= 1.0).astype(jnp.float32) + (row < grid_rows - 1.0).astype(jnp.float32)
    for half in range(2):
        count_x = 2.0 - (lane == (0, HALF - 1)[half]).astype(jnp.float32)
        rate_ref[half] = inside * (1.0 - smooth_rate * (2.0 + count_y + count_x))
    rate_ref[2] = inside * smooth_rate
    for index, reach in enumerate((2.0, 1.0, 0.0)):
        near = within & (row >= row_first - reach) & (row < row_first + (CY + reach))
        rate_ref[3 + index] = near.astype(jnp.float32)

    for sweep, (source, target) in enumerate(
        ((first_ref, second_ref), (second_ref, first_ref), (first_ref, second_ref))
    ):

        def sweep_step(plane, carry, source=source, target=target):
            for field in range(4):
                centre, sums = beside_of(source.at[field], plane)
                for half in range(2):
                    target[field, plane, half, MID, :] = (
                        rate_ref[half, MID, :] * centre[half] + rate_ref[2, MID, :] * sums[half]
                    )
            return carry

        lax.fori_loop(sweep + 1, ZE - 1 - sweep, sweep_step, 0)

    filtered = second_ref

    def mobility_step(plane, carry):
        known = rate_ref[3] > 0.5
        for half in range(2):
            fraction = 1.0 / (1.0 + filtered[0, plane + 3, half])
            mobility = jnp.where(known, fraction / density_ref[plane, half], 0.0)
            mob_ref[plane, half] = mobility
            wide_ref[plane, half] = mobility * guess_ref[plane, half]
        return carry

    lax.fori_loop(0, CZ + 4, mobility_step, 0)

    def output_step(plane, carry):
        for half in range(2):
            cut = slice(half * HALF, (half + 1) * HALF)
            fraction_ref[plane, :, cut] = 1.0 / (1.0 + filtered[0, plane + REACH, half, OWN, :])
            for part in range(3):
                momentum_ref[plane, part, :, cut] = filtered[part + 1, plane + REACH, half, OWN, :]
        return carry

    lax.fori_loop(0, CZ, output_step, 0)

    direct_ref, product_ref, remain_ref = first_ref.at[0], first_ref.at[1], first_ref.at[2]

    def first_residual(plane, carry):
        at = plane + 1
        near = rate_ref[4, MID, :] > 0.5
        mobility, beside_mobility = beside_of(mob_ref, at)
        guess, beside_guess = beside_of(guess_ref, at)
        unused, beside_wide = beside_of(wide_ref, at)
        slope = x_slope(filtered[3, at + 3, 0, MID, :], filtered[3, at + 3, 1, MID, :])
        for half in range(2):
            diagonal = (3.0 + stiffness) * mobility[half] + 0.5 * beside_mobility[half]
            operated = diagonal * guess[half] - 0.5 * (
                mobility[half] * beside_guess[half] + beside_wide[half]
            )
            spread = 0.5 * (filtered[1, at + 4, half, MID, :] - filtered[1, at + 2, half, MID, :])
            spread = spread + 0.5 * (
                filtered[2, at + 3, half, HIGH, :] - filtered[2, at + 3, half, LOW, :]
            )
            spread = spread + 0.5 * slope[half]
            residual = jnp.where(near, diverge_ref[plane, half, MID, :] - spread - operated, 0.0)
            direction = jnp.where(near, residual / diagonal, 0.0)
            remain_ref[plane, half, MID, :] = residual
            direct_ref[plane, half, MID, :] = direction
            product_ref[plane, half, MID, :] = direction * mobility[half]
            diagonal_ref[plane, half, MID, :] = diagonal
            mobility_ref[plane, half, MID, :] = mobility[half]
        return carry

    lax.fori_loop(0, CZ + 2, first_residual, 0)

    scaled_ref[...] = jnp.zeros_like(scaled_ref)

    def map_step(plane, sums):
        at = plane + 1
        own = rate_ref[5, MID, :] > 0.5
        directions, beside_direction = beside_of(direct_ref, at)
        unused, beside_product = beside_of(product_ref, at)
        sum_rz, sum_dw, sum_uw = sums
        for half in range(2):
            residual = jnp.where(own, remain_ref[at, half, MID, :], 0.0)
            diagonal = diagonal_ref[at, half, MID, :]
            mapped = diagonal * directions[half] - 0.5 * (
                mobility_ref[at, half, MID, :] * beside_direction[half] + beside_product[half]
            )
            mapped = jnp.where(own, mapped, 0.0)
            scaled = jnp.where(own, mapped / diagonal, 0.0)
            scaled_ref[at, half, MID, :] = scaled
            residual_ref[plane, half] = residual[4:68]
            direction_ref[plane, half] = directions[half][4:68]
            mapped_ref[plane, half] = mapped[4:68]
            sum_rz = sum_rz + residual * directions[half]
            sum_dw = sum_dw + directions[half] * mapped
            sum_uw = sum_uw + scaled * mapped
        return sum_rz, sum_dw, sum_uw

    zero = jnp.zeros((72, HALF), jnp.float32)
    sums = lax.fori_loop(0, CZ, map_step, (zero, zero, zero))
    for index in range(3):
        dots_ref[index] = jnp.sum(sums[index])


def second_kernel(dots_ref, scaled_ref, below_ref, above_ref, south_ref, north_ref, mobility_ref, diagonal_ref, twice_ref, sent_ref, held_ref, product_ref):
    held_ref[...] = scaled_ref[...]
    held_ref[0, :, OWN, :] = below_ref[...]
    held_ref[CZ + 1, :, OWN, :] = above_ref[...]
    for plane in range(CZ):
        for half in range(2):
            held_ref[plane + 1, half, LEAD - 1 : LEAD, :] = south_ref[plane, half : half + 1]
            held_ref[plane + 1, half, LEAD + CY : LEAD + CY + 1, :] = north_ref[plane, half : half + 1]

    def product_step(plane, carry):
        for half in range(2):
            product_ref[plane, half] = held_ref[plane, half] * mobility_ref[plane, half]
        return carry

    lax.fori_loop(0, CZ + 2, product_step, 0)

    def map_step(plane, total):
        at = plane + 1
        centre, beside = beside_of(held_ref, at)
        unused, beside_product = beside_of(product_ref, at)
        for half in range(2):
            twice = diagonal_ref[at, half, MID, :] * centre[half] - 0.5 * (
                mobility_ref[at, half, MID, :] * beside[half] + beside_product[half]
            )
            twice_ref[plane, half] = twice[4:68]
            total = total + (centre[half] * twice)[4:68]
        return total

    total = lax.fori_loop(0, CZ, map_step, jnp.zeros((CY, HALF), jnp.float32))
    values = (dots_ref[0], dots_ref[1], dots_ref[2], jnp.sum(total))
    column = lax.broadcasted_iota(jnp.int32, sent_ref.shape, 1)
    sent = jnp.zeros(sent_ref.shape, jnp.float32)
    for index, value in enumerate(values):
        sent = jnp.where(column == index, value, sent)
    sent_ref[...] = sent


def final_kernel(got_ref, guess_ref, residual_ref, direction_ref, mapped_ref, scaled_ref, twice_ref, pressure_ref, final_ref):
    sums = jnp.sum(got_ref[...], axis=0, keepdims=True)
    sum_rz, sum_dw, sum_uw, sum_uv = (sums[:, index : index + 1] for index in range(4))
    step = sum_rz / sum_dw
    next_rz = sum_rz - 2.0 * step * sum_dw + step * step * sum_uw
    along = 1.0 + next_rz / sum_rz
    curvature = along * along * sum_dw - 2.0 * step * along * sum_uw + step * step * sum_uv
    next_step = next_rz / curvature
    first = step + next_step * along
    last = next_step * step

    def write_step(plane, carry):
        for half in range(2):
            cut = slice(half * HALF, (half + 1) * HALF)
            pressure_ref[plane, :, cut] = (
                guess_ref[plane, :, cut]
                + first * direction_ref[plane, half]
                - last * scaled_ref[plane + 1, half, OWN, :]
            )
            final_ref[plane, :, cut] = (
                residual_ref[plane, half] - first * mapped_ref[plane, half] + last * twice_ref[plane, half]
            )
        return carry

    lax.fori_loop(0, CZ, write_step, 0)


def vmem_spec():
    return pl.BlockSpec(memory_space=pltpu.VMEM)


def smem_spec():
    return pl.BlockSpec(memory_space=pltpu.SMEM)


def f32(*shape):
    return jax.ShapeDtypeStruct(shape, jnp.float32)


def params():
    return pltpu.CompilerParams(vmem_limit_bytes=VMEM_LIMIT)


def deposit_scratch():
    return [
        pltpu.VMEM((4 * 14 * TALL, CHUNK), jnp.bfloat16),
        pltpu.VMEM((CX, CHUNK), jnp.bfloat16),
    ]


def on_device(
    parcel_cell,
    parcel_offset,
    parcel_volume,
    parcel_force,
    brick_counts,
    divergence,
    pressure_prev,
    gas_density,
):
    size_z = lax.axis_size("gz")
    size_y = lax.axis_size("gy")
    grid_rows = float(size_y * CY)
    row_first = (lax.axis_index("gy") * CY).astype(jnp.int32)[None]
    up_z = [(i, (i + 1) % size_z) for i in range(size_z)]
    down_z = [((i + 1) % size_z, i) for i in range(size_z)]
    up_y = [(i, i + 1) for i in range(size_y - 1)]
    down_y = [(i + 1, i) for i in range(size_y - 1)]

    message = f32(LIST + 5 * TILES, 8, CX)
    whole = [
        pl.BlockSpec(shape, lambda step, rank=len(shape): (0,) * rank)
        for shape in ((1, PCAP), (3, PCAP), (1, PCAP), (3, PCAP))
    ]
    edge_specs = []
    for depth in (2, 2, 1):
        for block in (0, CZ // depth - 1):
            edge_specs.append(pl.BlockSpec((depth, CY, CX), lambda step, block=block: (block, 0, 0)))
    to_up, to_down = pl.pallas_call(
        sort_kernel,
        grid=(1,),
        out_shape=(message, message),
        in_specs=[smem_spec()] + whole + edge_specs,
        out_specs=(vmem_spec(), vmem_spec()),
        scratch_shapes=[
            pltpu.VMEM((8, PCAP), jnp.float32),
            pltpu.VMEM((PCAP // 256 * CY, 256), jnp.bfloat16),
            pltpu.VMEM((PCAP // 256 * CY, 256), jnp.float32),
            pltpu.VMEM((1, PCAP), jnp.int32),
            pltpu.VMEM((384, 512), jnp.bfloat16),
            pltpu.VMEM((384, 256), jnp.float32),
        ],
        compiler_params=params(),
        name="order",
    )(
        brick_counts, parcel_cell[None], parcel_offset, parcel_volume[None], parcel_force,
        pressure_prev, pressure_prev, gas_density, gas_density, divergence, divergence,
    )
    below = lax.ppermute(to_up, "gz", up_z)
    above = lax.ppermute(to_down, "gz", down_z)
    edge_rows = f32(3 * LIST + 8, 8, CX)
    to_north, to_south = pl.pallas_call(
        pack_kernel,
        out_shape=(edge_rows, edge_rows),
        in_specs=[vmem_spec()] * 6,
        out_specs=(vmem_spec(), vmem_spec()),
        compiler_params=params(),
        name="pack",
    )(to_up, below, above, pressure_prev, gas_density, divergence)
    south = lax.ppermute(to_north, "gy", up_y)
    north = lax.ppermute(to_south, "gy", down_y)
    acc = pl.pallas_call(
        functools.partial(own_kernel, grid_rows),
        out_shape=f32(4, ZE, 2, YE, HALF),
        in_specs=[smem_spec(), vmem_spec()],
        out_specs=vmem_spec(),
        scratch_shapes=deposit_scratch(),
        compiler_params=params(),
        cost_estimate=pl.CostEstimate(flops=8_000_000_000, bytes_accessed=8_000_000, transcendentals=0),
        name="own",
    )(row_first, to_up)
    halves = f32(CZ, 2, CY, HALF)
    wider = f32(CZ + 2, 2, YE, HALF)
    fraction, momentum, residual, direction, mapped, scaled, mobility, diagonal, dots = pl.pallas_call(
        functools.partial(field_kernel, grid_rows),
        out_shape=(
            f32(CZ, CY, CX),
            f32(CZ, 3, CY, CX),
            halves,
            halves,
            halves,
            wider,
            wider,
            wider,
            f32(3),
        ),
        in_specs=[smem_spec()] + [vmem_spec()] * 4 + [pl.BlockSpec(memory_space=pl.ANY)] + [vmem_spec()] * 3,
        out_specs=tuple([vmem_spec()] * 8 + [smem_spec()]),
        scratch_shapes=[
            pltpu.VMEM((4, ZE, 2, YE, HALF), jnp.float32),
            pltpu.VMEM((4, ZE, 2, YE, HALF), jnp.float32),
            pltpu.VMEM((CZ + 4, 2, YE, HALF), jnp.float32),
            pltpu.VMEM((CZ + 4, 2, YE, HALF), jnp.float32),
            pltpu.VMEM((CZ + 4, 2, YE, HALF), jnp.float32),
            pltpu.VMEM((CZ + 4, 2, YE, HALF), jnp.float32),
            pltpu.VMEM((CZ + 2, 2, YE, HALF), jnp.float32),
            pltpu.VMEM((6, YE, HALF), jnp.float32),
        ]
        + deposit_scratch()
        + [pltpu.SemaphoreType.DMA],
        compiler_params=params(),
        name="fields",
    )(row_first, below, above, south, north, acc, gas_density, pressure_prev, divergence)

    scaled_below = lax.ppermute(scaled[CZ, :, OWN], "gz", up_z)
    scaled_above = lax.ppermute(scaled[1, :, OWN], "gz", down_z)
    scaled_south = lax.ppermute(scaled[1:-1, :, LEAD + CY - 1], "gy", up_y)
    scaled_north = lax.ppermute(scaled[1:-1, :, LEAD], "gy", down_y)
    every = size_z * size_y
    twice, sent = pl.pallas_call(
        second_kernel,
        out_shape=(halves, f32(every, 128)),
        in_specs=[smem_spec()] + [vmem_spec()] * 7,
        out_specs=(vmem_spec(), vmem_spec()),
        scratch_shapes=[
            pltpu.VMEM((CZ + 2, 2, YE, HALF), jnp.float32),
            pltpu.VMEM((CZ + 2, 2, YE, HALF), jnp.float32),
        ],
        compiler_params=params(),
        name="second",
    )(dots, scaled, scaled_below, scaled_above, scaled_south, scaled_north, mobility, diagonal)
    got = lax.all_to_all(sent, ("gz", "gy"), 0, 0, tiled=True)
    pressure, final = pl.pallas_call(
        final_kernel,
        out_shape=(f32(CZ, CY, CX), f32(CZ, CY, CX)),
        in_specs=[vmem_spec()] * 7,
        out_specs=(vmem_spec(), vmem_spec()),
        compiler_params=params(),
        name="final",
    )(got, pressure_prev, residual, direction, mapped, scaled, twice)
    return (fraction, momentum, pressure, final)


def solution(mesh):
    return jax.shard_map(
        on_device,
        mesh=mesh,
        in_specs=(
            P(("gz", "gy")),
            P(None, ("gz", "gy")),
            P(("gz", "gy")),
            P(None, ("gz", "gy")),
            P("gz", "gy"),
            P("gz", "gy", None),
            P("gz", "gy", None),
            P("gz", "gy", None),
        ),
        out_specs=(
            P("gz", "gy", None),
            P("gz", None, "gy", None),
            P("gz", "gy", None),
            P("gz", "gy", None),
        ),
        check_vma=False,
    )
```

```python
import functools

import jax
import jax.numpy as jnp
from jax import lax
from jax.experimental import pallas as pl
from jax.experimental.pallas import tpu as pltpu
from jax.sharding import PartitionSpec as P

CZ = 8
CY = 64
CX = 256
PCAP = 4096
ITERS = 2
REACH = 5
ZE = CZ + 2 * REACH
YE = 88
LEAD = 12
LIST = PCAP // 256
TILES = CY // 8
HALF = 128
CHUNK = 256
TALL = 24

smooth_rate = 0.15
stiffness = 0.002

VMEM_LIMIT = 48 * 1024 * 1024


def chunk_values(parcels, grid_rows, row_first, shift_y):
    cell = parcels[0:1].astype(jnp.int32)
    home_z = lax.shift_right_logical(cell, 14)
    home_y = lax.shift_right_logical(cell, 8) & 63
    home_x = cell & 255
    count = parcels.shape[1]
    taps = lax.broadcasted_iota(jnp.int32, (8, count), 0).astype(jnp.float32) - 3.0

    def tap_table(offset, inside):
        distance = taps + 0.5 - offset
        weight = jnp.where(inside, jnp.exp(-0.5 * distance * distance), 0.0)
        return weight * (1.0 / jnp.sum(weight, axis=0, keepdims=True))

    seven = taps < 3.5
    place_y = taps + (home_y.astype(jnp.float32) + (row_first + shift_y))
    place_x = taps + home_x.astype(jnp.float32)
    table_z = tap_table(parcels[1:2], seven)
    table_y = tap_table(parcels[2:3], seven & (place_y >= 0.0) & (place_y < grid_rows))
    table_x = tap_table(parcels[3:4], seven & (place_x >= 0.0) & (place_x < float(CX)))
    return home_z, home_y, home_x, table_z, table_y, table_x


def axis_rows(rows, first, home, table, least=None):
    count = home.shape[1]
    lane_row = lax.broadcasted_iota(jnp.int32, (8, count), 0)
    tap_base = lane_row - (home - 3)
    tiles = []
    for tile in range(rows // 8):
        at = first + 8 * tile
        tap = tap_base + at
        fits = (tap & -8) == 0
        if least is not None:
            fits = fits & (lane_row >= least - at)
        tiles.append(jnp.take_along_axis(table, jnp.where(fits, tap, 7), axis=0))
    return tiles[0] if len(tiles) == 1 else jnp.concatenate(tiles, axis=0)


def row_of(cell):
    return lax.shift_right_logical(cell.astype(jnp.int32), 8) & 63


def count_where(condition):
    return jnp.sum(condition.astype(jnp.float32)).astype(jnp.int32)


def deposit(parcels_ref, base, row_first, grid_rows, shift_z, shift_y, planes, plane_first, window, acc_ref, lhs_ref, rhs_ref):
    rows = TALL if window is None else 8
    volume = parcels_ref[base : base + LIST, 4, :]
    begin = 0
    if shift_y == 0:
        total = count_where(volume != 0.0)
    else:
        home_row = row_of(parcels_ref[base : base + LIST, 0, :])
        if shift_y < 0:
            total = count_where(volume != 0.0)
            begin = lax.shift_right_logical(
                count_where((volume != 0.0) & (home_row < CY - 3 - REACH)), CHUNK.bit_length() - 1
            )
        else:
            total = count_where((volume != 0.0) & (home_row < 3 + REACH))

    def chunk_step(index, carry):
        start = index * CHUNK
        parcels = parcels_ref[base + index]
        home_z, home_y, home_x, table_z, table_y, table_x = chunk_values(
            parcels, grid_rows, row_first, float(shift_y)
        )
        block = 64
        for part in range(CX // block):
            weight_x = axis_rows(block, part * block, home_x, table_x)
            rhs_ref[part * block : (part + 1) * block, :] = weight_x.astype(jnp.bfloat16)
        rows_z = -(-planes // 8) * 8
        weight_z = axis_rows(rows_z, plane_first - REACH - shift_z, home_z, table_z)
        loaded = [
            weight_z * (parcels[4:5] if field == 0 else parcels[4:5] * parcels[4 + field : 5 + field])
            for field in range(4)
        ]

        def spread_window(first, least):
            weight_y = axis_rows(
                rows, first - (LEAD + shift_y), home_y, table_y,
                None if least is None else least - LEAD,
            )
            for field in range(4):
                for pair in range(planes // 2):
                    both = jnp.concatenate(
                        [
                            loaded[field][2 * pair : 2 * pair + 1] * weight_y,
                            loaded[field][2 * pair + 1 : 2 * pair + 2] * weight_y,
                        ],
                        axis=0,
                    )
                    at = (field * planes + 2 * pair) * rows
                    lhs_ref[at : at + 2 * rows, :] = both.astype(jnp.bfloat16)

        def add_window(first):
            for field in range(4):
                product = lax.dot_general(
                    lhs_ref[field * planes * rows : (field + 1) * planes * rows, :],
                    rhs_ref[...],
                    (((1,), (1,)), ((), ())),
                    preferred_element_type=jnp.float32,
                )
                for plane in range(planes):
                    for half in range(2):
                        acc_ref[field, plane_first + plane, half, pl.ds(first, rows), :] += product[
                            plane * rows : (plane + 1) * rows, half * HALF : (half + 1) * HALF
                        ]

        if window is not None:
            spread_window(window, None)
            add_window(window)
            return carry

        slot = lax.broadcasted_iota(jnp.int32, (1, CHUNK), 1) + start
        row_home = home_y.astype(jnp.float32)
        lowest = jnp.min(jnp.where(slot < total, row_home, float(CY))).astype(jnp.int32)
        highest = jnp.max(jnp.where(slot < total, row_home, 0.0)).astype(jnp.int32)
        row_low = lax.shift_right_logical(lowest + (LEAD - 3), 3) * 8
        row_high = highest + (LEAD + 4)

        def window_step(carried):
            logical = carried
            first = pl.multiple_of(jnp.minimum(logical, YE - TALL), 8)
            spread_window(first, logical)
            add_window(first)
            return logical + TALL

        lax.while_loop(lambda carried: carried < row_high, window_step, row_low)
        return carry

    end = lax.shift_right_logical(total + (CHUNK - 1), CHUNK.bit_length() - 1)
    lax.fori_loop(begin, end, chunk_step, 0)


def sort_kernel(count_ref, cell_ref, offset_ref, volume_ref, force_ref, guess_ref, density_ref, diverge_ref, up_ref, down_ref, rows_ref, cell_held_ref, data_ref, hot_ref, prefix_ref, dest_ref, lhs_ref, total_ref, sems):
    lists = [
        pltpu.make_async_copy(cell_ref, cell_held_ref, sems.at[0]),
        pltpu.make_async_copy(offset_ref, data_ref.at[1:4], sems.at[1]),
        pltpu.make_async_copy(volume_ref, data_ref.at[4:5], sems.at[2]),
        pltpu.make_async_copy(force_ref, data_ref.at[5:8], sems.at[3]),
    ]
    edges = []
    for out_ref, upper in ((up_ref, True), (down_ref, False)):
        at = LIST
        for source, depth in ((guess_ref, 2), (density_ref, 2), (diverge_ref, 1)):
            for plane in range(depth):
                edges.append(
                    pltpu.make_async_copy(
                        source.at[CZ - depth + plane if upper else plane],
                        out_ref.at[at : at + TILES],
                        sems.at[4 + len(edges)],
                    )
                )
                at += TILES
    for part, source in enumerate((guess_ref, density_ref, diverge_ref)):
        for side in range(2):
            edges.append(
                pltpu.make_async_copy(
                    source.at[:, side * (TILES - 1)], rows_ref.at[2 * part + side], sems.at[4 + len(edges)]
                )
            )
    for copy in lists + edges:
        copy.start()
    for copy in lists:
        copy.wait()
    data_ref[0:1, :] = cell_held_ref[...].astype(jnp.float32)
    live_count = count_ref[0, 0]
    block = 256
    blocks = PCAP // block
    bins = lax.broadcasted_iota(jnp.int32, (CY, block), 0)
    slots = lax.broadcasted_iota(jnp.int32, (1, block), 1)

    def hot_of(index):
        cut = slice(index * block, (index + 1) * block)
        home_row = lax.shift_right_logical(cell_held_ref[:, cut], 8) & 63
        return (bins == home_row) & (slots + index * block < live_count)

    for index in range(blocks):
        hot_ref[index * CY : (index + 1) * CY, :] = hot_of(index).astype(jnp.float32).astype(jnp.bfloat16)
    before = lax.broadcasted_iota(jnp.int32, (block, block), 0)
    after = lax.broadcasted_iota(jnp.int32, (block, block), 1)
    upto = (before <= after).astype(jnp.float32).astype(jnp.bfloat16)
    prefix_ref[...] = jnp.dot(hot_ref[...], upto, preferred_element_type=jnp.float32)
    carry = jnp.zeros((CY, 1), jnp.float32)
    carries = []
    for index in range(blocks):
        carries.append(carry)
        carry = carry + prefix_ref[index * CY : (index + 1) * CY, block - 1 : block]
    total = jnp.broadcast_to(carry, (CY, 128))
    row = lax.broadcasted_iota(jnp.int32, (CY, 128), 0)
    summed = total
    for shift in (1, 2, 4, 8, 16, 32):
        summed = summed + jnp.where(row >= shift, pltpu.roll(summed, shift, 0), 0.0)
    first = (summed - total)[:, 0:1]
    for index in range(blocks):
        cut = slice(index * block, (index + 1) * block)
        place = prefix_ref[index * CY : (index + 1) * CY, :] + (first + carries[index])
        hot = hot_of(index)
        dest = jnp.sum(jnp.where(hot, place, 0.0), axis=0, keepdims=True) - 1.0
        dest_ref[:, cut] = dest.astype(jnp.int32)

    total_ref[...] = jnp.zeros_like(total_ref)
    width = 512

    def route(index, unused):
        start = pl.multiple_of(index * width, width)
        dest = dest_ref[:, pl.ds(start, width)]
        high = lax.shift_right_arithmetic(dest, 8)
        low = dest & 255
        data = data_ref[:, pl.ds(start, width)]
        top = data.astype(jnp.bfloat16).astype(jnp.float32)
        rest = data - top
        middle = rest.astype(jnp.bfloat16).astype(jnp.float32)
        lanes = lax.broadcasted_iota(jnp.int32, (256, width), 0)
        rhs = (lanes == low).astype(jnp.float32).astype(jnp.bfloat16)
        wide = jnp.broadcast_to(high, (8, width))
        for split, values in enumerate((top, middle, rest - middle)):
            for pair in range(8):
                both = jnp.concatenate(
                    [
                        jnp.where(wide == 2 * pair, values, 0.0),
                        jnp.where(wide == 2 * pair + 1, values, 0.0),
                    ],
                    axis=0,
                )
                at = split * 128 + pair * 16
                lhs_ref[at : at + 16, :] = both.astype(jnp.bfloat16)
        total_ref[...] += lax.dot_general(
            lhs_ref[...], rhs, (((1,), (1,)), ((), ())), preferred_element_type=jnp.float32
        )
        return unused

    steps = lax.shift_right_logical(live_count + (width - 1), 9)
    lax.fori_loop(0, steps, route, 0)
    for part in range(LIST):
        at = part * 8
        sorted_part = (
            total_ref[at : at + 8, :] + total_ref[128 + at : 136 + at, :]
        ) + total_ref[256 + at : 264 + at, :]
        up_ref[part] = sorted_part
        down_ref[part] = sorted_part
    for copy in edges:
        copy.wait()


FIELDS = ((2, 2), (2, 2), (1, 1))


def pack_kernel(sorted_ref, below_ref, above_ref, edge_ref, north_ref, south_ref):
    for out_ref in (north_ref, south_ref):
        for index, source in enumerate((sorted_ref, below_ref, above_ref)):
            out_ref[index * LIST : (index + 1) * LIST] = source[0:LIST]
        out_ref[3 * LIST + 7, 2:8, :] = jnp.zeros((6, CX), jnp.float32)
    for side, out_ref in ((1, north_ref), (0, south_ref)):
        slot = 0
        for part, (depth, wide) in enumerate(FIELDS):
            first = (0, 2, 4)[part]
            rows = slice(8 - wide, 8) if side else slice(0, wide)
            for plane in range(CZ + 2 * depth):
                if depth <= plane < CZ + depth:
                    values = edge_ref[2 * part + side, plane - depth, rows, :]
                else:
                    ref, inner = (below_ref, plane) if plane < depth else (above_ref, plane - CZ - depth)
                    values = ref[LIST + (first + inner) * TILES + side * (TILES - 1), rows, :]
                out_ref[3 * LIST + slot // 8, slot % 8 : slot % 8 + wide, :] = values
                slot += wide


def own_kernel(grid_rows, row_ref, parcels_ref, acc_ref, lhs_ref, rhs_ref):
    row_first = row_ref[0].astype(jnp.float32)
    acc_ref[...] = jnp.zeros_like(acc_ref)
    deposit(parcels_ref, 0, row_first, grid_rows, 0, 0, 14, 2, None, acc_ref, lhs_ref, rhs_ref)


def gather_fields(south_ref, north_ref, below_ref, above_ref, sources, targets):
    slot = 0
    for part, (own_ref, out_ref, (depth, wide)) in enumerate(zip(sources, targets, FIELDS)):
        first = (0, 2, 4)[part]
        for plane in range(CZ + 2 * depth):
            for half in range(2):
                cut = slice(half * HALF, (half + 1) * HALF)
                if depth <= plane < CZ + depth:
                    out_ref[plane, half, OWN, :] = own_ref[plane - depth, :, cut]
                else:
                    ref, inner = (below_ref, plane) if plane < depth else (above_ref, plane - CZ - depth)
                    at = LIST + (first + inner) * TILES
                    for tile in range(TILES):
                        out_ref[plane, half, LEAD + 8 * tile : LEAD + 8 * tile + 8, :] = ref[at + tile, :, cut]
                edge = 3 * LIST + slot // 8
                inner_rows = slice(slot % 8, slot % 8 + wide)
                out_ref[plane, half, LEAD - wide : LEAD, :] = south_ref[edge, inner_rows, cut]
                out_ref[plane, half, LEAD + CY : LEAD + CY + wide, :] = north_ref[edge, inner_rows, cut]
            slot += wide


def beside_y(row_first, grid_rows, south_ref, north_ref, acc_ref, lhs_ref, rhs_ref):
    for parcels_ref, shift_y, window in (
        (south_ref, -CY, LEAD - REACH),
        (north_ref, CY, LEAD + CY - 3),
    ):
        for part, (shift_z, planes, plane_first) in enumerate(((0, 14, 2), (-CZ, 8, 0), (CZ, 8, 10))):
            deposit(
                parcels_ref, LIST * part, row_first, grid_rows, shift_z, shift_y, planes, plane_first,
                window, acc_ref, lhs_ref, rhs_ref,
            )


MID = slice(8, 80)
LOW = slice(7, 79)
HIGH = slice(9, 81)
OWN = slice(LEAD, LEAD + CY)


def x_pair(left, right):
    lane = lax.broadcasted_iota(jnp.int32, left.shape, 1)
    start, stop = lane == 0, lane == HALF - 1
    left_west, right_west = pltpu.roll(left, 1, 1), pltpu.roll(right, 1, 1)
    left_east, right_east = pltpu.roll(left, HALF - 1, 1), pltpu.roll(right, HALF - 1, 1)
    return (
        jnp.where(start, 0.0, left_west) + jnp.where(stop, right_east, left_east),
        jnp.where(start, left_west, right_west) + jnp.where(stop, 0.0, right_east),
    )


def x_slope(left, right):
    lane = lax.broadcasted_iota(jnp.int32, left.shape, 1)
    start, stop = lane == 0, lane == HALF - 1
    left_west, right_west = pltpu.roll(left, 1, 1), pltpu.roll(right, 1, 1)
    left_east, right_east = pltpu.roll(left, HALF - 1, 1), pltpu.roll(right, HALF - 1, 1)
    return (
        jnp.where(stop, right_east, left_east) - jnp.where(start, 0.0, left_west),
        jnp.where(stop, 0.0, right_east) - jnp.where(start, left_west, right_west),
    )


def beside_of(ref, plane):
    centre = [ref[plane, half, MID, :] for half in range(2)]
    pairs = x_pair(*centre)
    sums = [
        (ref[plane - 1, half, MID, :] + ref[plane + 1, half, MID, :])
        + (ref[plane, half, LOW, :] + ref[plane, half, HIGH, :])
        + pairs[half]
        for half in range(2)
    ]
    return centre, sums


def field_kernel(
    grid_rows,
    row_ref,
    below_ref,
    above_ref,
    south_ref,
    north_ref,
    acc_ref,
    density_own_ref,
    guess_own_ref,
    diverge_own_ref,
    fraction_ref,
    momentum_ref,
    residual_ref,
    direction_ref,
    mapped_ref,
    scaled_own_ref,
    twice_ref,
    high_ref,
    low_ref,
    north_edge_ref,
    south_edge_ref,
    high_face_ref,
    low_face_ref,
    north_face_ref,
    south_face_ref,
    dots_ref,
    scaled_ref,
    mobility_ref,
    diagonal_ref,
    first_ref,
    second_ref,
    mob_ref,
    guess_ref,
    wide_ref,
    density_ref,
    diverge_ref,
    rate_ref,
    lhs_ref,
    rhs_ref,
    load_sem,
):
    row_first = row_ref[0].astype(jnp.float32)
    load = pltpu.make_async_copy(acc_ref, first_ref, load_sem)
    load.start()
    gather_fields(
        south_ref,
        north_ref,
        below_ref,
        above_ref,
        (guess_own_ref, density_own_ref, diverge_own_ref),
        (guess_ref, density_ref, diverge_ref),
    )
    load.wait()
    deposit(below_ref, 0, row_first, grid_rows, -CZ, 0, 8, 0, None, first_ref, lhs_ref, rhs_ref)
    deposit(above_ref, 0, row_first, grid_rows, CZ, 0, 8, 10, None, first_ref, lhs_ref, rhs_ref)
    beside_y(row_first, grid_rows, south_ref, north_ref, first_ref, lhs_ref, rhs_ref)

    row = lax.broadcasted_iota(jnp.int32, (YE, HALF), 0).astype(jnp.float32) + (row_first - LEAD)
    lane = lax.broadcasted_iota(jnp.int32, (YE, HALF), 1)
    within = (row >= 0.0) & (row < grid_rows)
    inside = within.astype(jnp.float32)
    count_y = (row >= 1.0).astype(jnp.float32) + (row < grid_rows - 1.0).astype(jnp.float32)
    for half in range(2):
        count_x = 2.0 - (lane == (0, HALF - 1)[half]).astype(jnp.float32)
        rate_ref[half] = inside * (1.0 - smooth_rate * (2.0 + count_y + count_x))
    rate_ref[2] = inside * smooth_rate
    for index, reach in enumerate((2.0, 1.0, 0.0)):
        near = within & (row >= row_first - reach) & (row < row_first + (CY + reach))
        rate_ref[3 + index] = near.astype(jnp.float32)

    for sweep, (source, target) in enumerate(
        ((first_ref, second_ref), (second_ref, first_ref), (first_ref, second_ref))
    ):

        def sweep_step(plane, carry, source=source, target=target):
            for field in range(4):
                centre, sums = beside_of(source.at[field], plane)
                for half in range(2):
                    target[field, plane, half, MID, :] = (
                        rate_ref[half, MID, :] * centre[half] + rate_ref[2, MID, :] * sums[half]
                    )
            return carry

        lax.fori_loop(sweep + 1, ZE - 1 - sweep, sweep_step, 0)

    filtered = second_ref

    def mobility_step(plane, carry):
        known = rate_ref[3] > 0.5
        for half in range(2):
            fraction = 1.0 / (1.0 + filtered[0, plane + 3, half])
            mobility = jnp.where(known, fraction / density_ref[plane, half], 0.0)
            mob_ref[plane, half] = mobility
            wide_ref[plane, half] = mobility * guess_ref[plane, half]
        return carry

    lax.fori_loop(0, CZ + 4, mobility_step, 0)

    def output_step(plane, carry):
        for half in range(2):
            cut = slice(half * HALF, (half + 1) * HALF)
            fraction_ref[plane, :, cut] = 1.0 / (1.0 + filtered[0, plane + REACH, half, OWN, :])
            for part in range(3):
                momentum_ref[plane, part, :, cut] = filtered[part + 1, plane + REACH, half, OWN, :]
        return carry

    lax.fori_loop(0, CZ, output_step, 0)

    direct_ref, product_ref, remain_ref = first_ref.at[0], first_ref.at[1], first_ref.at[2]

    def first_residual(plane, carry):
        at = plane + 1
        near = rate_ref[4, MID, :] > 0.5
        mobility, beside_mobility = beside_of(mob_ref, at)
        guess, beside_guess = beside_of(guess_ref, at)
        unused, beside_wide = beside_of(wide_ref, at)
        slope = x_slope(filtered[3, at + 3, 0, MID, :], filtered[3, at + 3, 1, MID, :])
        for half in range(2):
            diagonal = (3.0 + stiffness) * mobility[half] + 0.5 * beside_mobility[half]
            operated = diagonal * guess[half] - 0.5 * (
                mobility[half] * beside_guess[half] + beside_wide[half]
            )
            spread = 0.5 * (filtered[1, at + 4, half, MID, :] - filtered[1, at + 2, half, MID, :])
            spread = spread + 0.5 * (
                filtered[2, at + 3, half, HIGH, :] - filtered[2, at + 3, half, LOW, :]
            )
            spread = spread + 0.5 * slope[half]
            residual = jnp.where(near, diverge_ref[plane, half, MID, :] - spread - operated, 0.0)
            direction = jnp.where(near, residual / diagonal, 0.0)
            remain_ref[plane, half, MID, :] = residual
            direct_ref[plane, half, MID, :] = direction
            product_ref[plane, half, MID, :] = direction * mobility[half]
            diagonal_ref[plane, half, MID, :] = diagonal
            mobility_ref[plane, half, MID, :] = mobility[half]
        return carry

    lax.fori_loop(0, CZ + 2, first_residual, 0)

    scaled_ref[...] = jnp.zeros_like(scaled_ref)
    again_ref = first_ref.at[3]
    for plane in (0, CZ + 1):
        again_ref[plane] = jnp.zeros((2, YE, HALF), jnp.float32)

    def map_step(plane, sums):
        at = plane + 1
        own = rate_ref[5, MID, :] > 0.5
        directions, beside_direction = beside_of(direct_ref, at)
        unused, beside_product = beside_of(product_ref, at)
        sum_rz, sum_dw, sum_uw = sums
        for half in range(2):
            residual = jnp.where(own, remain_ref[at, half, MID, :], 0.0)
            diagonal = diagonal_ref[at, half, MID, :]
            mapped = diagonal * directions[half] - 0.5 * (
                mobility_ref[at, half, MID, :] * beside_direction[half] + beside_product[half]
            )
            mapped = jnp.where(own, mapped, 0.0)
            scaled = jnp.where(own, mapped / diagonal, 0.0)
            scaled_ref[at, half, MID, :] = scaled
            again_ref[at, half, MID, :] = scaled * mobility_ref[at, half, MID, :]
            scaled_own_ref[plane, half] = scaled[4:68]
            residual_ref[plane, half] = residual[4:68]
            direction_ref[plane, half] = directions[half][4:68]
            mapped_ref[plane, half] = mapped[4:68]
            sum_rz = sum_rz + residual * directions[half]
            sum_dw = sum_dw + directions[half] * mapped
            sum_uw = sum_uw + scaled * mapped
        return sum_rz, sum_dw, sum_uw

    zero = jnp.zeros((72, HALF), jnp.float32)
    sums = lax.fori_loop(0, CZ, map_step, (zero, zero, zero))
    for index in range(3):
        dots_ref[index] = jnp.sum(sums[index])
    def again_step(plane, total):
        at = plane + 1
        centre, beside = beside_of(scaled_ref, at)
        unused, beside_again = beside_of(again_ref, at)
        for half in range(2):
            twice = diagonal_ref[at, half, MID, :] * centre[half] - 0.5 * (
                mobility_ref[at, half, MID, :] * beside[half] + beside_again[half]
            )
            twice_ref[plane, half] = twice[4:68]
            total = total + (centre[half] * twice)[4:68]
        return total

    total = lax.fori_loop(0, CZ, again_step, jnp.zeros((CY, HALF), jnp.float32))
    dots_ref[3] = jnp.sum(total)
    high_face_ref[...] = 0.5 * (mobility_ref[CZ, :, OWN, :] + mobility_ref[CZ + 1, :, OWN, :])
    low_face_ref[...] = 0.5 * (mobility_ref[1, :, OWN, :] + mobility_ref[0, :, OWN, :])
    for face_ref, inner in ((north_face_ref, LEAD + CY - 1), (south_face_ref, LEAD - 1)):
        for plane in range(CZ):
            for half in range(2):
                face_ref[plane, half : half + 1] = 0.5 * (
                    mobility_ref[plane + 1, half, inner : inner + 1, :]
                    + mobility_ref[plane + 1, half, inner + 1 : inner + 2, :]
                )
    high_ref[...] = scaled_ref[CZ, :, OWN, :]
    low_ref[...] = scaled_ref[1, :, OWN, :]
    for plane in range(CZ):
        for half in range(2):
            north_edge_ref[plane, half : half + 1] = scaled_ref[plane + 1, half, LEAD + CY - 1 : LEAD + CY, :]
            south_edge_ref[plane, half : half + 1] = scaled_ref[plane + 1, half, LEAD : LEAD + 1, :]


def second_kernel(dots_ref, *refs):
    received, own_edges, faces, sent_ref = refs[0:4], refs[4:8], refs[8:12], refs[12]
    missing = jnp.float32(0.0)
    for got_ref, own_ref, face_ref in zip(received, own_edges, faces):
        missing = missing + jnp.sum(got_ref[...] * own_ref[...] * face_ref[...])
    values = (dots_ref[0], dots_ref[1], dots_ref[2], dots_ref[3] - missing)
    column = lax.broadcasted_iota(jnp.int32, sent_ref.shape, 1)
    sent = jnp.zeros(sent_ref.shape, jnp.float32)
    for index, value in enumerate(values):
        sent = jnp.where(column == index, value, sent)
    sent_ref[...] = sent


def final_kernel(got_ref, guess_ref, residual_ref, direction_ref, mapped_ref, scaled_ref, twice_ref, below_ref, above_ref, south_ref, north_ref, low_face_ref, high_face_ref, south_face_ref, north_face_ref, pressure_ref, final_ref):
    sums = jnp.sum(got_ref[...], axis=0, keepdims=True)
    sum_rz, sum_dw, sum_uw, sum_uv = (sums[:, index : index + 1] for index in range(4))
    step = sum_rz / sum_dw
    next_rz = sum_rz - 2.0 * step * sum_dw + step * step * sum_uw
    along = 1.0 + next_rz / sum_rz
    curvature = along * along * sum_dw - 2.0 * step * along * sum_uw + step * step * sum_uv
    next_step = next_rz / curvature
    first = step + next_step * along
    last = next_step * step

    row = lax.broadcasted_iota(jnp.int32, (CY, HALF), 0)
    for plane in range(CZ):
        for half in range(2):
            cut = slice(half * HALF, (half + 1) * HALF)
            south = south_ref[plane, half : half + 1] * south_face_ref[plane, half : half + 1]
            north = north_ref[plane, half : half + 1] * north_face_ref[plane, half : half + 1]
            past = jnp.where(row == 0, south, 0.0) + jnp.where(row == CY - 1, north, 0.0)
            if plane == 0:
                past = past + below_ref[half] * low_face_ref[half]
            if plane == CZ - 1:
                past = past + above_ref[half] * high_face_ref[half]
            twice = twice_ref[plane, half] - past
            pressure_ref[plane, :, cut] = (
                guess_ref[plane, :, cut]
                + first * direction_ref[plane, half]
                - last * scaled_ref[plane, half]
            )
            final_ref[plane, :, cut] = (
                residual_ref[plane, half] - first * mapped_ref[plane, half] + last * twice
            )


def vmem_spec():
    return pl.BlockSpec(memory_space=pltpu.VMEM)


def smem_spec():
    return pl.BlockSpec(memory_space=pltpu.SMEM)


def f32(*shape):
    return jax.ShapeDtypeStruct(shape, jnp.float32)


def params():
    return pltpu.CompilerParams(vmem_limit_bytes=VMEM_LIMIT)


def hbm_spec():
    return pl.BlockSpec(memory_space=pltpu.HBM)


def deposit_scratch():
    return [
        pltpu.VMEM((4 * 14 * TALL, CHUNK), jnp.bfloat16),
        pltpu.VMEM((CX, CHUNK), jnp.bfloat16),
    ]


def on_device(
    parcel_cell,
    parcel_offset,
    parcel_volume,
    parcel_force,
    brick_counts,
    divergence,
    pressure_prev,
    gas_density,
):
    size_z = lax.axis_size("gz")
    size_y = lax.axis_size("gy")
    grid_rows = float(size_y * CY)
    row_first = (lax.axis_index("gy") * CY).astype(jnp.int32)[None]
    up_z = [(i, (i + 1) % size_z) for i in range(size_z)]
    down_z = [((i + 1) % size_z, i) for i in range(size_z)]
    up_y = [(i, i + 1) for i in range(size_y - 1)]
    down_y = [(i + 1, i) for i in range(size_y - 1)]

    message = f32(LIST + 5 * TILES, 8, CX)
    tiled = [values.reshape(CZ, TILES, 8, CX) for values in (pressure_prev, gas_density, divergence)]
    to_up, to_down, brick_rows = pl.pallas_call(
        sort_kernel,
        out_shape=(message, message, f32(6, CZ, 8, CX)),
        in_specs=[smem_spec()] + [hbm_spec()] * 7,
        out_specs=(vmem_spec(), vmem_spec(), vmem_spec()),
        scratch_shapes=[
            pltpu.VMEM((1, PCAP), jnp.int32),
            pltpu.VMEM((8, PCAP), jnp.float32),
            pltpu.VMEM((PCAP // 256 * CY, 256), jnp.bfloat16),
            pltpu.VMEM((PCAP // 256 * CY, 256), jnp.float32),
            pltpu.VMEM((1, PCAP), jnp.int32),
            pltpu.VMEM((384, 512), jnp.bfloat16),
            pltpu.VMEM((384, 256), jnp.float32),
            pltpu.SemaphoreType.DMA((20,)),
        ],
        compiler_params=pltpu.CompilerParams(vmem_limit_bytes=60 * 1024 * 1024),
        name="order",
    )(brick_counts, parcel_cell[None], parcel_offset, parcel_volume[None], parcel_force, *tiled)
    below = lax.ppermute(to_up, "gz", up_z)
    above = lax.ppermute(to_down, "gz", down_z)
    edge_rows = f32(3 * LIST + 8, 8, CX)
    to_north, to_south = pl.pallas_call(
        pack_kernel,
        out_shape=(edge_rows, edge_rows),
        in_specs=[vmem_spec()] * 4,
        out_specs=(vmem_spec(), vmem_spec()),
        compiler_params=params(),
        name="pack",
    )(to_up, below, above, brick_rows)
    south = lax.ppermute(to_north, "gy", up_y)
    north = lax.ppermute(to_south, "gy", down_y)
    acc = pl.pallas_call(
        functools.partial(own_kernel, grid_rows),
        out_shape=f32(4, ZE, 2, YE, HALF),
        in_specs=[smem_spec(), vmem_spec()],
        out_specs=vmem_spec(),
        scratch_shapes=deposit_scratch(),
        compiler_params=params(),
        cost_estimate=pl.CostEstimate(flops=8_000_000_000, bytes_accessed=8_000_000, transcendentals=0),
        name="own",
    )(row_first, to_up)
    halves = f32(CZ, 2, CY, HALF)
    face_z, face_y = f32(2, CY, HALF), f32(CZ, 2, HALF)
    (
        fraction, momentum, residual, direction, mapped, scaled, twice,
        high, low, north_edge, south_edge, high_face, low_face, north_face, south_face, dots,
    ) = pl.pallas_call(
        functools.partial(field_kernel, grid_rows),
        out_shape=(f32(CZ, CY, CX), f32(CZ, 3, CY, CX))
        + (halves,) * 5
        + (face_z, face_z, face_y, face_y) * 2
        + (f32(4),),
        in_specs=[smem_spec()] + [vmem_spec()] * 4 + [pl.BlockSpec(memory_space=pl.ANY)] + [vmem_spec()] * 3,
        out_specs=tuple([vmem_spec()] * 15 + [smem_spec()]),
        scratch_shapes=[pltpu.VMEM((CZ + 2, 2, YE, HALF), jnp.float32)] * 3
        + [
            pltpu.VMEM((4, ZE, 2, YE, HALF), jnp.float32),
            pltpu.VMEM((4, ZE, 2, YE, HALF), jnp.float32),
            pltpu.VMEM((CZ + 4, 2, YE, HALF), jnp.float32),
            pltpu.VMEM((CZ + 4, 2, YE, HALF), jnp.float32),
            pltpu.VMEM((CZ + 4, 2, YE, HALF), jnp.float32),
            pltpu.VMEM((CZ + 4, 2, YE, HALF), jnp.float32),
            pltpu.VMEM((CZ + 2, 2, YE, HALF), jnp.float32),
            pltpu.VMEM((6, YE, HALF), jnp.float32),
        ]
        + deposit_scratch()
        + [pltpu.SemaphoreType.DMA],
        compiler_params=params(),
        name="fields",
    )(row_first, below, above, south, north, acc, gas_density, pressure_prev, divergence)

    scaled_below = lax.ppermute(high, "gz", up_z)
    scaled_above = lax.ppermute(low, "gz", down_z)
    scaled_south = lax.ppermute(north_edge, "gy", up_y)
    scaled_north = lax.ppermute(south_edge, "gy", down_y)
    every = size_z * size_y
    received = (scaled_below, scaled_above, scaled_south, scaled_north)
    faces = (low_face, high_face, south_face, north_face)
    sent = pl.pallas_call(
        second_kernel,
        out_shape=f32(every, 128),
        in_specs=[smem_spec()] + [vmem_spec()] * 12,
        out_specs=vmem_spec(),
        compiler_params=params(),
        name="second",
    )(dots, *received, low, high, south_edge, north_edge, *faces)
    got = lax.all_to_all(sent, ("gz", "gy"), 0, 0, tiled=True)
    pressure, final = pl.pallas_call(
        final_kernel,
        out_shape=(f32(CZ, CY, CX), f32(CZ, CY, CX)),
        in_specs=[vmem_spec()] * 15,
        out_specs=(vmem_spec(), vmem_spec()),
        compiler_params=params(),
        name="final",
    )(got, pressure_prev, residual, direction, mapped, scaled, twice, *received, *faces)
    return (fraction, momentum, pressure, final)


def solution(mesh):
    return jax.shard_map(
        on_device,
        mesh=mesh,
        in_specs=(
            P(("gz", "gy")),
            P(None, ("gz", "gy")),
            P(("gz", "gy")),
            P(None, ("gz", "gy")),
            P("gz", "gy"),
            P("gz", "gy", None),
            P("gz", "gy", None),
            P("gz", "gy", None),
        ),
        out_specs=(
            P("gz", "gy", None),
            P("gz", None, "gy", None),
            P("gz", "gy", None),
            P("gz", "gy", None),
        ),
        check_vma=False,
    )
```

```python
import functools

import jax
import jax.numpy as jnp
from jax import lax
from jax.experimental import pallas as pl
from jax.experimental.pallas import tpu as pltpu
from jax.sharding import PartitionSpec as P

CZ = 8
CY = 64
CX = 256
PCAP = 4096
ITERS = 2
REACH = 5
ZE = CZ + 2 * REACH
YE = 88
LEAD = 12
LIST = PCAP // 256
TILES = CY // 8
HALF = 128
CHUNK = 256
TALL = 16

smooth_rate = 0.15
stiffness = 0.002

VMEM_LIMIT = 48 * 1024 * 1024


def chunk_values(parcels, grid_rows, row_first, shift_y):
    cell = parcels[0:1].astype(jnp.int32)
    home_z = lax.shift_right_logical(cell, 14)
    home_y = lax.shift_right_logical(cell, 8) & 63
    home_x = cell & 255
    count = parcels.shape[1]
    taps = lax.broadcasted_iota(jnp.int32, (8, count), 0).astype(jnp.float32) - 3.0

    def tap_table(offset, inside):
        distance = taps + 0.5 - offset
        weight = jnp.where(inside, jnp.exp(-0.5 * distance * distance), 0.0)
        return weight * (1.0 / jnp.sum(weight, axis=0, keepdims=True))

    seven = taps < 3.5
    place_y = taps + (home_y.astype(jnp.float32) + (row_first + shift_y))
    place_x = taps + home_x.astype(jnp.float32)
    table_z = tap_table(parcels[1:2], seven)
    table_y = tap_table(parcels[2:3], seven & (place_y >= 0.0) & (place_y < grid_rows))
    table_x = tap_table(parcels[3:4], seven & (place_x >= 0.0) & (place_x < float(CX)))
    return home_z, home_y, home_x, table_z, table_y, table_x


def axis_rows(rows, first, home, table, least=None):
    count = home.shape[1]
    lane_row = lax.broadcasted_iota(jnp.int32, (8, count), 0)
    tap_base = lane_row - (home - 3)
    tiles = []
    for tile in range(rows // 8):
        at = first + 8 * tile
        tap = tap_base + at
        fits = (tap & -8) == 0
        if least is not None:
            fits = fits & (lane_row >= least - at)
        tiles.append(jnp.take_along_axis(table, jnp.where(fits, tap, 7), axis=0))
    return tiles[0] if len(tiles) == 1 else jnp.concatenate(tiles, axis=0)


def row_of(cell):
    return lax.shift_right_logical(cell.astype(jnp.int32), 8) & 63


def count_where(condition):
    return jnp.sum(condition.astype(jnp.float32)).astype(jnp.int32)


def deposit(parcels_ref, base, row_first, grid_rows, shift_z, shift_y, planes, plane_first, window, lead, acc_ref, lhs_ref, rhs_ref):
    rows = TALL if window is None else 8
    volume = parcels_ref[base : base + LIST, 4, :]
    begin = 0
    if shift_y == 0:
        total = count_where(volume != 0.0)
    else:
        home_row = row_of(parcels_ref[base : base + LIST, 0, :])
        if shift_y < 0:
            total = count_where(volume != 0.0)
            begin = lax.shift_right_logical(
                count_where((volume != 0.0) & (home_row < CY - 3 - REACH)), CHUNK.bit_length() - 1
            )
        else:
            total = count_where((volume != 0.0) & (home_row < 3 + REACH))

    def chunk_step(index, carry):
        start = index * CHUNK
        parcels = parcels_ref[base + index]
        home_z, home_y, home_x, table_z, table_y, table_x = chunk_values(
            parcels, grid_rows, row_first, float(shift_y)
        )
        block = 64
        for part in range(CX // block):
            weight_x = axis_rows(block, part * block, home_x, table_x)
            rhs_ref[part * block : (part + 1) * block, :] = weight_x.astype(jnp.bfloat16)
        rows_z = -(-planes // 8) * 8
        weight_z = axis_rows(rows_z, plane_first - REACH - shift_z, home_z, table_z)
        loaded = [
            weight_z * (parcels[4:5] if field == 0 else parcels[4:5] * parcels[4 + field : 5 + field])
            for field in range(4)
        ]

        def spread_window(first, least):
            weight_y = axis_rows(
                rows, first - (lead + shift_y), home_y, table_y,
                None if least is None else least - lead,
            )
            for field in range(4):
                for pair in range(planes // 2):
                    both = jnp.concatenate(
                        [
                            loaded[field][2 * pair : 2 * pair + 1] * weight_y,
                            loaded[field][2 * pair + 1 : 2 * pair + 2] * weight_y,
                        ],
                        axis=0,
                    )
                    at = (field * planes + 2 * pair) * rows
                    lhs_ref[at : at + 2 * rows, :] = both.astype(jnp.bfloat16)

        def add_window(first):
            for field in range(4):
                product = lax.dot_general(
                    lhs_ref[field * planes * rows : (field + 1) * planes * rows, :],
                    rhs_ref[...],
                    (((1,), (1,)), ((), ())),
                    preferred_element_type=jnp.float32,
                )
                for plane in range(planes):
                    for half in range(2):
                        acc_ref[field, plane_first + plane, half, pl.ds(first, rows), :] += product[
                            plane * rows : (plane + 1) * rows, half * HALF : (half + 1) * HALF
                        ]

        if window is not None:
            spread_window(window, None)
            add_window(window)
            return carry

        slot = lax.broadcasted_iota(jnp.int32, (1, CHUNK), 1) + start
        row_home = home_y.astype(jnp.float32)
        lowest = jnp.min(jnp.where(slot < total, row_home, float(CY))).astype(jnp.int32)
        highest = jnp.max(jnp.where(slot < total, row_home, 0.0)).astype(jnp.int32)
        row_low = lowest + (lead - 3)
        row_high = highest + (lead + 4)

        def window_step(carried):
            logical = carried
            first = jnp.minimum(logical, acc_ref.shape[3] - TALL)
            spread_window(first, logical)
            add_window(first)
            return logical + TALL

        lax.while_loop(lambda carried: carried < row_high, window_step, row_low)
        return carry

    end = lax.shift_right_logical(total + (CHUNK - 1), CHUNK.bit_length() - 1)
    lax.fori_loop(begin, end, chunk_step, 0)


def sort_kernel(count_ref, cell_ref, offset_ref, volume_ref, force_ref, guess_ref, density_ref, diverge_ref, up_ref, down_ref, rows_ref, cell_held_ref, data_ref, hot_ref, prefix_ref, dest_ref, lhs_ref, total_ref, sems):
    lists = [
        pltpu.make_async_copy(cell_ref, cell_held_ref, sems.at[0]),
        pltpu.make_async_copy(offset_ref, data_ref.at[1:4], sems.at[1]),
        pltpu.make_async_copy(volume_ref, data_ref.at[4:5], sems.at[2]),
        pltpu.make_async_copy(force_ref, data_ref.at[5:8], sems.at[3]),
    ]
    edges = []
    for out_ref, upper in ((up_ref, True), (down_ref, False)):
        at = LIST
        for source, depth in ((guess_ref, 2), (density_ref, 2), (diverge_ref, 1)):
            for plane in range(depth):
                edges.append(
                    pltpu.make_async_copy(
                        source.at[CZ - depth + plane if upper else plane],
                        out_ref.at[at : at + TILES],
                        sems.at[4 + len(edges)],
                    )
                )
                at += TILES
    for part, source in enumerate((guess_ref, density_ref, diverge_ref)):
        for side in range(2):
            edges.append(
                pltpu.make_async_copy(
                    source.at[:, side * (TILES - 1)], rows_ref.at[2 * part + side], sems.at[4 + len(edges)]
                )
            )
    for copy in lists + edges:
        copy.start()
    for copy in lists:
        copy.wait()
    data_ref[0:1, :] = cell_held_ref[...].astype(jnp.float32)
    live_count = count_ref[0, 0]
    block = 256
    blocks = PCAP // block
    bins = lax.broadcasted_iota(jnp.int32, (CY, block), 0)
    slots = lax.broadcasted_iota(jnp.int32, (1, block), 1)

    def hot_of(index):
        cut = slice(index * block, (index + 1) * block)
        home_row = lax.shift_right_logical(cell_held_ref[:, cut], 8) & 63
        return (bins == home_row) & (slots + index * block < live_count)

    for index in range(blocks):
        hot_ref[index * CY : (index + 1) * CY, :] = hot_of(index).astype(jnp.float32).astype(jnp.bfloat16)
    before = lax.broadcasted_iota(jnp.int32, (block, block), 0)
    after = lax.broadcasted_iota(jnp.int32, (block, block), 1)
    upto = (before <= after).astype(jnp.float32).astype(jnp.bfloat16)
    prefix_ref[...] = jnp.dot(hot_ref[...], upto, preferred_element_type=jnp.float32)
    carry = jnp.zeros((CY, 1), jnp.float32)
    carries = []
    for index in range(blocks):
        carries.append(carry)
        carry = carry + prefix_ref[index * CY : (index + 1) * CY, block - 1 : block]
    total = jnp.broadcast_to(carry, (CY, 128))
    row = lax.broadcasted_iota(jnp.int32, (CY, 128), 0)
    summed = total
    for shift in (1, 2, 4, 8, 16, 32):
        summed = summed + jnp.where(row >= shift, pltpu.roll(summed, shift, 0), 0.0)
    first = (summed - total)[:, 0:1]
    for index in range(blocks):
        cut = slice(index * block, (index + 1) * block)
        place = prefix_ref[index * CY : (index + 1) * CY, :] + (first + carries[index])
        hot = hot_of(index)
        dest = jnp.sum(jnp.where(hot, place, 0.0), axis=0, keepdims=True) - 1.0
        dest_ref[:, cut] = dest.astype(jnp.int32)

    total_ref[...] = jnp.zeros_like(total_ref)
    width = 512

    def route(index, unused):
        start = pl.multiple_of(index * width, width)
        dest = dest_ref[:, pl.ds(start, width)]
        high = lax.shift_right_arithmetic(dest, 8)
        low = dest & 255
        data = data_ref[:, pl.ds(start, width)]
        top = data.astype(jnp.bfloat16).astype(jnp.float32)
        rest = data - top
        middle = rest.astype(jnp.bfloat16).astype(jnp.float32)
        lanes = lax.broadcasted_iota(jnp.int32, (256, width), 0)
        rhs = (lanes == low).astype(jnp.float32).astype(jnp.bfloat16)
        wide = jnp.broadcast_to(high, (8, width))
        for split, values in enumerate((top, middle, rest - middle)):
            for pair in range(8):
                both = jnp.concatenate(
                    [
                        jnp.where(wide == 2 * pair, values, 0.0),
                        jnp.where(wide == 2 * pair + 1, values, 0.0),
                    ],
                    axis=0,
                )
                at = split * 128 + pair * 16
                lhs_ref[at : at + 16, :] = both.astype(jnp.bfloat16)
        total_ref[...] += lax.dot_general(
            lhs_ref[...], rhs, (((1,), (1,)), ((), ())), preferred_element_type=jnp.float32
        )
        return unused

    steps = lax.shift_right_logical(live_count + (width - 1), 9)
    lax.fori_loop(0, steps, route, 0)
    for part in range(LIST):
        at = part * 8
        sorted_part = (
            total_ref[at : at + 8, :] + total_ref[128 + at : 136 + at, :]
        ) + total_ref[256 + at : 264 + at, :]
        up_ref[part] = sorted_part
        down_ref[part] = sorted_part
    for copy in edges:
        copy.wait()


FIELDS = ((2, 2), (2, 2), (1, 1))


def pack_kernel(sorted_ref, below_ref, above_ref, edge_ref, north_ref, south_ref):
    for out_ref in (north_ref, south_ref):
        for index, source in enumerate((sorted_ref, below_ref, above_ref)):
            out_ref[index * LIST : (index + 1) * LIST] = source[0:LIST]
        out_ref[3 * LIST + 7, 2:8, :] = jnp.zeros((6, CX), jnp.float32)
    for side, out_ref in ((1, north_ref), (0, south_ref)):
        slot = 0
        for part, (depth, wide) in enumerate(FIELDS):
            first = (0, 2, 4)[part]
            rows = slice(8 - wide, 8) if side else slice(0, wide)
            for plane in range(CZ + 2 * depth):
                if depth <= plane < CZ + depth:
                    values = edge_ref[2 * part + side, plane - depth, rows, :]
                else:
                    ref, inner = (below_ref, plane) if plane < depth else (above_ref, plane - CZ - depth)
                    values = ref[LIST + (first + inner) * TILES + side * (TILES - 1), rows, :]
                out_ref[3 * LIST + slot // 8, slot % 8 : slot % 8 + wide, :] = values
                slot += wide


def own_kernel(grid_rows, row_ref, parcels_ref, below_ref, above_ref, acc_ref, lhs_ref, rhs_ref):
    row_first = row_ref[0].astype(jnp.float32)
    acc_ref[...] = jnp.zeros_like(acc_ref)
    for list_ref, shift_z, planes, plane_first in (
        (parcels_ref, 0, 14, 2),
        (below_ref, -CZ, 8, 0),
        (above_ref, CZ, 8, 10),
    ):
        deposit(
            list_ref, 0, row_first, grid_rows, shift_z, 0, planes, plane_first, None, LEAD - MID.start,
            acc_ref, lhs_ref, rhs_ref,
        )


def gather_fields(south_ref, north_ref, below_ref, above_ref, sources, targets):
    slot = 0
    for part, (own_ref, out_ref, (depth, wide)) in enumerate(zip(sources, targets, FIELDS)):
        first = (0, 2, 4)[part]
        for plane in range(CZ + 2 * depth):
            for half in range(2):
                cut = slice(half * HALF, (half + 1) * HALF)
                if depth <= plane < CZ + depth:
                    out_ref[plane, half, OWN, :] = own_ref[plane - depth, :, cut]
                else:
                    ref, inner = (below_ref, plane) if plane < depth else (above_ref, plane - CZ - depth)
                    at = LIST + (first + inner) * TILES
                    for tile in range(TILES):
                        out_ref[plane, half, LEAD + 8 * tile : LEAD + 8 * tile + 8, :] = ref[at + tile, :, cut]
                edge = 3 * LIST + slot // 8
                inner_rows = slice(slot % 8, slot % 8 + wide)
                out_ref[plane, half, LEAD - wide : LEAD, :] = south_ref[edge, inner_rows, cut]
                out_ref[plane, half, LEAD + CY : LEAD + CY + wide, :] = north_ref[edge, inner_rows, cut]
            slot += wide


def beside_y(row_first, grid_rows, south_ref, north_ref, acc_ref, lhs_ref, rhs_ref):
    for parcels_ref, shift_y, window in (
        (south_ref, -CY, LEAD - REACH),
        (north_ref, CY, LEAD + CY - 3),
    ):
        for part, (shift_z, planes, plane_first) in enumerate(((0, 14, 2), (-CZ, 8, 0), (CZ, 8, 10))):
            deposit(
                parcels_ref, LIST * part, row_first, grid_rows, shift_z, shift_y, planes, plane_first,
                window, LEAD, acc_ref, lhs_ref, rhs_ref,
            )


MID = slice(8, 80)
LOW = slice(7, 79)
HIGH = slice(9, 81)
OWN = slice(LEAD, LEAD + CY)


def x_pair(left, right):
    lane = lax.broadcasted_iota(jnp.int32, left.shape, 1)
    start, stop = lane == 0, lane == HALF - 1
    left_west, right_west = pltpu.roll(left, 1, 1), pltpu.roll(right, 1, 1)
    left_east, right_east = pltpu.roll(left, HALF - 1, 1), pltpu.roll(right, HALF - 1, 1)
    return (
        jnp.where(start, 0.0, left_west) + jnp.where(stop, right_east, left_east),
        jnp.where(start, left_west, right_west) + jnp.where(stop, 0.0, right_east),
    )


def x_slope(left, right):
    lane = lax.broadcasted_iota(jnp.int32, left.shape, 1)
    start, stop = lane == 0, lane == HALF - 1
    left_west, right_west = pltpu.roll(left, 1, 1), pltpu.roll(right, 1, 1)
    left_east, right_east = pltpu.roll(left, HALF - 1, 1), pltpu.roll(right, HALF - 1, 1)
    return (
        jnp.where(stop, right_east, left_east) - jnp.where(start, 0.0, left_west),
        jnp.where(stop, 0.0, right_east) - jnp.where(start, left_west, right_west),
    )


def beside_of(ref, plane):
    centre = [ref[plane, half, MID, :] for half in range(2)]
    pairs = x_pair(*centre)
    sums = [
        (ref[plane - 1, half, MID, :] + ref[plane + 1, half, MID, :])
        + (ref[plane, half, LOW, :] + ref[plane, half, HIGH, :])
        + pairs[half]
        for half in range(2)
    ]
    return centre, sums


def field_kernel(
    grid_rows,
    row_ref,
    below_ref,
    above_ref,
    south_ref,
    north_ref,
    acc_ref,
    density_own_ref,
    guess_own_ref,
    diverge_own_ref,
    fraction_ref,
    momentum_ref,
    residual_ref,
    direction_ref,
    mapped_ref,
    scaled_own_ref,
    twice_ref,
    high_ref,
    low_ref,
    north_edge_ref,
    south_edge_ref,
    high_face_ref,
    low_face_ref,
    north_face_ref,
    south_face_ref,
    dots_ref,
    scaled_ref,
    mobility_ref,
    diagonal_ref,
    first_ref,
    second_ref,
    mob_ref,
    guess_ref,
    wide_ref,
    density_ref,
    diverge_ref,
    rate_ref,
    lhs_ref,
    rhs_ref,
    load_sem,
):
    row_first = row_ref[0].astype(jnp.float32)
    load = pltpu.make_async_copy(acc_ref, first_ref.at[:, :, :, MID, :], load_sem)
    load.start()
    for field in range(4):
        edge = jnp.zeros((ZE, 2, 8, HALF), jnp.float32)
        first_ref[field, :, :, 0 : MID.start, :] = edge
        first_ref[field, :, :, MID.stop : YE, :] = edge
    gather_fields(
        south_ref,
        north_ref,
        below_ref,
        above_ref,
        (guess_own_ref, density_own_ref, diverge_own_ref),
        (guess_ref, density_ref, diverge_ref),
    )
    load.wait()
    beside_y(row_first, grid_rows, south_ref, north_ref, first_ref, lhs_ref, rhs_ref)

    row = lax.broadcasted_iota(jnp.int32, (YE, HALF), 0).astype(jnp.float32) + (row_first - LEAD)
    lane = lax.broadcasted_iota(jnp.int32, (YE, HALF), 1)
    within = (row >= 0.0) & (row < grid_rows)
    inside = within.astype(jnp.float32)
    count_y = (row >= 1.0).astype(jnp.float32) + (row < grid_rows - 1.0).astype(jnp.float32)
    for half in range(2):
        count_x = 2.0 - (lane == (0, HALF - 1)[half]).astype(jnp.float32)
        rate_ref[half] = inside * (1.0 - smooth_rate * (2.0 + count_y + count_x))
    rate_ref[2] = inside * smooth_rate
    for index, reach in enumerate((2.0, 1.0, 0.0)):
        near = within & (row >= row_first - reach) & (row < row_first + (CY + reach))
        rate_ref[3 + index] = near.astype(jnp.float32)

    for sweep, (source, target) in enumerate(
        ((first_ref, second_ref), (second_ref, first_ref), (first_ref, second_ref))
    ):

        def sweep_plane(plane, fields, source=source, target=target):
            for field in fields:
                centre, sums = beside_of(source.at[field], plane)
                for half in range(2):
                    target[field, plane, half, MID, :] = (
                        rate_ref[half, MID, :] * centre[half] + rate_ref[2, MID, :] * sums[half]
                    )

        def sweep_step(plane, carry, sweep_plane=sweep_plane):
            sweep_plane(plane, (0, 1, 2, 3))
            return carry

        sweep_plane(sweep + 1, (0, 1))
        lax.fori_loop(sweep + 2, ZE - 2 - sweep, sweep_step, 0)
        sweep_plane(ZE - 2 - sweep, (0, 1))

    filtered = second_ref

    def mobility_step(plane, carry):
        known = rate_ref[3] > 0.5
        for half in range(2):
            fraction = 1.0 / (1.0 + filtered[0, plane + 3, half])
            mobility = jnp.where(known, fraction / density_ref[plane, half], 0.0)
            mob_ref[plane, half] = mobility
            wide_ref[plane, half] = mobility * guess_ref[plane, half]
        return carry

    lax.fori_loop(0, CZ + 4, mobility_step, 0)

    def output_step(plane, carry):
        for half in range(2):
            cut = slice(half * HALF, (half + 1) * HALF)
            fraction_ref[plane, :, cut] = 1.0 / (1.0 + filtered[0, plane + REACH, half, OWN, :])
            for part in range(3):
                momentum_ref[plane, part, :, cut] = filtered[part + 1, plane + REACH, half, OWN, :]
        return carry

    lax.fori_loop(0, CZ, output_step, 0)

    direct_ref, product_ref, remain_ref = first_ref.at[0], first_ref.at[1], first_ref.at[2]

    def first_residual(plane, carry):
        at = plane + 1
        near = rate_ref[4, MID, :] > 0.5
        mobility, beside_mobility = beside_of(mob_ref, at)
        guess, beside_guess = beside_of(guess_ref, at)
        unused, beside_wide = beside_of(wide_ref, at)
        slope = x_slope(filtered[3, at + 3, 0, MID, :], filtered[3, at + 3, 1, MID, :])
        for half in range(2):
            diagonal = (3.0 + stiffness) * mobility[half] + 0.5 * beside_mobility[half]
            operated = diagonal * guess[half] - 0.5 * (
                mobility[half] * beside_guess[half] + beside_wide[half]
            )
            spread = 0.5 * (filtered[1, at + 4, half, MID, :] - filtered[1, at + 2, half, MID, :])
            spread = spread + 0.5 * (
                filtered[2, at + 3, half, HIGH, :] - filtered[2, at + 3, half, LOW, :]
            )
            spread = spread + 0.5 * slope[half]
            residual = jnp.where(near, diverge_ref[plane, half, MID, :] - spread - operated, 0.0)
            direction = jnp.where(near, residual / diagonal, 0.0)
            remain_ref[plane, half, MID, :] = residual
            direct_ref[plane, half, MID, :] = direction
            product_ref[plane, half, MID, :] = direction * mobility[half]
            diagonal_ref[plane, half, MID, :] = diagonal
            mobility_ref[plane, half, MID, :] = mobility[half]
        return carry

    lax.fori_loop(0, CZ + 2, first_residual, 0)

    scaled_ref[...] = jnp.zeros_like(scaled_ref)
    again_ref = first_ref.at[3]
    for plane in (0, CZ + 1):
        again_ref[plane] = jnp.zeros((2, YE, HALF), jnp.float32)

    def map_step(plane, sums):
        at = plane + 1
        own = rate_ref[5, MID, :] > 0.5
        directions, beside_direction = beside_of(direct_ref, at)
        unused, beside_product = beside_of(product_ref, at)
        sum_rz, sum_dw, sum_uw = sums
        for half in range(2):
            residual = jnp.where(own, remain_ref[at, half, MID, :], 0.0)
            diagonal = diagonal_ref[at, half, MID, :]
            mapped = diagonal * directions[half] - 0.5 * (
                mobility_ref[at, half, MID, :] * beside_direction[half] + beside_product[half]
            )
            mapped = jnp.where(own, mapped, 0.0)
            scaled = jnp.where(own, mapped / diagonal, 0.0)
            scaled_ref[at, half, MID, :] = scaled
            again_ref[at, half, MID, :] = scaled * mobility_ref[at, half, MID, :]
            scaled_own_ref[plane, half] = scaled[4:68]
            residual_ref[plane, half] = residual[4:68]
            direction_ref[plane, half] = directions[half][4:68]
            mapped_ref[plane, half] = mapped[4:68]
            sum_rz = sum_rz + residual * directions[half]
            sum_dw = sum_dw + directions[half] * mapped
            sum_uw = sum_uw + scaled * mapped
        return sum_rz, sum_dw, sum_uw

    zero = jnp.zeros((72, HALF), jnp.float32)
    sums = lax.fori_loop(0, CZ, map_step, (zero, zero, zero))
    for index in range(3):
        dots_ref[index] = jnp.sum(sums[index])
    def again_step(plane, total):
        at = plane + 1
        centre, beside = beside_of(scaled_ref, at)
        unused, beside_again = beside_of(again_ref, at)
        for half in range(2):
            twice = diagonal_ref[at, half, MID, :] * centre[half] - 0.5 * (
                mobility_ref[at, half, MID, :] * beside[half] + beside_again[half]
            )
            twice_ref[plane, half] = twice[4:68]
            total = total + (centre[half] * twice)[4:68]
        return total

    total = lax.fori_loop(0, CZ, again_step, jnp.zeros((CY, HALF), jnp.float32))
    dots_ref[3] = jnp.sum(total)
    high_face_ref[...] = 0.5 * (mobility_ref[CZ, :, OWN, :] + mobility_ref[CZ + 1, :, OWN, :])
    low_face_ref[...] = 0.5 * (mobility_ref[1, :, OWN, :] + mobility_ref[0, :, OWN, :])
    for face_ref, inner in ((north_face_ref, LEAD + CY - 1), (south_face_ref, LEAD - 1)):
        for plane in range(CZ):
            for half in range(2):
                face_ref[plane, half : half + 1] = 0.5 * (
                    mobility_ref[plane + 1, half, inner : inner + 1, :]
                    + mobility_ref[plane + 1, half, inner + 1 : inner + 2, :]
                )
    high_ref[...] = scaled_ref[CZ, :, OWN, :]
    low_ref[...] = scaled_ref[1, :, OWN, :]
    for plane in range(CZ):
        for half in range(2):
            north_edge_ref[plane, half : half + 1] = scaled_ref[plane + 1, half, LEAD + CY - 1 : LEAD + CY, :]
            south_edge_ref[plane, half : half + 1] = scaled_ref[plane + 1, half, LEAD : LEAD + 1, :]


def second_kernel(dots_ref, *refs):
    received, own_edges, faces, sent_ref = refs[0:4], refs[4:8], refs[8:12], refs[12]
    missing = jnp.float32(0.0)
    for got_ref, own_ref, face_ref in zip(received, own_edges, faces):
        missing = missing + jnp.sum(got_ref[...] * own_ref[...] * face_ref[...])
    values = (dots_ref[0], dots_ref[1], dots_ref[2], dots_ref[3] - missing)
    column = lax.broadcasted_iota(jnp.int32, sent_ref.shape, 1)
    sent = jnp.zeros(sent_ref.shape, jnp.float32)
    for index, value in enumerate(values):
        sent = jnp.where(column == index, value, sent)
    sent_ref[...] = sent


def final_kernel(got_ref, guess_ref, residual_ref, direction_ref, mapped_ref, scaled_ref, twice_ref, below_ref, above_ref, south_ref, north_ref, low_face_ref, high_face_ref, south_face_ref, north_face_ref, pressure_ref, final_ref):
    sums = jnp.sum(got_ref[...], axis=0, keepdims=True)
    sum_rz, sum_dw, sum_uw, sum_uv = (sums[:, index : index + 1] for index in range(4))
    step = sum_rz / sum_dw
    next_rz = sum_rz - 2.0 * step * sum_dw + step * step * sum_uw
    along = 1.0 + next_rz / sum_rz
    curvature = along * along * sum_dw - 2.0 * step * along * sum_uw + step * step * sum_uv
    next_step = next_rz / curvature
    first = step + next_step * along
    last = next_step * step

    row = lax.broadcasted_iota(jnp.int32, (CY, HALF), 0)
    for plane in range(CZ):
        for half in range(2):
            cut = slice(half * HALF, (half + 1) * HALF)
            south = south_ref[plane, half : half + 1] * south_face_ref[plane, half : half + 1]
            north = north_ref[plane, half : half + 1] * north_face_ref[plane, half : half + 1]
            past = jnp.where(row == 0, south, 0.0) + jnp.where(row == CY - 1, north, 0.0)
            if plane == 0:
                past = past + below_ref[half] * low_face_ref[half]
            if plane == CZ - 1:
                past = past + above_ref[half] * high_face_ref[half]
            twice = twice_ref[plane, half] - past
            pressure_ref[plane, :, cut] = (
                guess_ref[plane, :, cut]
                + first * direction_ref[plane, half]
                - last * scaled_ref[plane, half]
            )
            final_ref[plane, :, cut] = (
                residual_ref[plane, half] - first * mapped_ref[plane, half] + last * twice
            )


def vmem_spec():
    return pl.BlockSpec(memory_space=pltpu.VMEM)


def smem_spec():
    return pl.BlockSpec(memory_space=pltpu.SMEM)


def f32(*shape):
    return jax.ShapeDtypeStruct(shape, jnp.float32)


def params():
    return pltpu.CompilerParams(vmem_limit_bytes=VMEM_LIMIT)


def hbm_spec():
    return pl.BlockSpec(memory_space=pltpu.HBM)


def deposit_scratch():
    return [
        pltpu.VMEM((4 * 14 * TALL, CHUNK), jnp.bfloat16),
        pltpu.VMEM((CX, CHUNK), jnp.bfloat16),
    ]


def on_device(
    parcel_cell,
    parcel_offset,
    parcel_volume,
    parcel_force,
    brick_counts,
    divergence,
    pressure_prev,
    gas_density,
):
    size_z = lax.axis_size("gz")
    size_y = lax.axis_size("gy")
    grid_rows = float(size_y * CY)
    row_first = (lax.axis_index("gy") * CY).astype(jnp.int32)[None]
    up_z = [(i, (i + 1) % size_z) for i in range(size_z)]
    down_z = [((i + 1) % size_z, i) for i in range(size_z)]
    up_y = [(i, i + 1) for i in range(size_y - 1)]
    down_y = [(i + 1, i) for i in range(size_y - 1)]

    message = f32(LIST + 5 * TILES, 8, CX)
    tiled = [values.reshape(CZ, TILES, 8, CX) for values in (pressure_prev, gas_density, divergence)]
    to_up, to_down, brick_rows = pl.pallas_call(
        sort_kernel,
        out_shape=(message, message, f32(6, CZ, 8, CX)),
        in_specs=[smem_spec()] + [hbm_spec()] * 7,
        out_specs=(vmem_spec(), vmem_spec(), vmem_spec()),
        scratch_shapes=[
            pltpu.VMEM((1, PCAP), jnp.int32),
            pltpu.VMEM((8, PCAP), jnp.float32),
            pltpu.VMEM((PCAP // 256 * CY, 256), jnp.bfloat16),
            pltpu.VMEM((PCAP // 256 * CY, 256), jnp.float32),
            pltpu.VMEM((1, PCAP), jnp.int32),
            pltpu.VMEM((384, 512), jnp.bfloat16),
            pltpu.VMEM((384, 256), jnp.float32),
            pltpu.SemaphoreType.DMA((20,)),
        ],
        compiler_params=pltpu.CompilerParams(vmem_limit_bytes=60 * 1024 * 1024),
        name="order",
    )(brick_counts, parcel_cell[None], parcel_offset, parcel_volume[None], parcel_force, *tiled)
    below = lax.ppermute(to_up, "gz", up_z)
    above = lax.ppermute(to_down, "gz", down_z)
    edge_rows = f32(3 * LIST + 8, 8, CX)
    to_north, to_south = pl.pallas_call(
        pack_kernel,
        out_shape=(edge_rows, edge_rows),
        in_specs=[vmem_spec()] * 4,
        out_specs=(vmem_spec(), vmem_spec()),
        compiler_params=params(),
        name="pack",
    )(to_up, below, above, brick_rows)
    south = lax.ppermute(to_north, "gy", up_y)
    north = lax.ppermute(to_south, "gy", down_y)
    acc = pl.pallas_call(
        functools.partial(own_kernel, grid_rows),
        out_shape=f32(4, ZE, 2, MID.stop - MID.start, HALF),
        in_specs=[smem_spec()] + [vmem_spec()] * 3,
        out_specs=vmem_spec(),
        scratch_shapes=deposit_scratch(),
        compiler_params=params(),
        cost_estimate=pl.CostEstimate(flops=8_000_000_000, bytes_accessed=8_000_000, transcendentals=0),
        name="own",
    )(row_first, to_up, below, above)
    halves = f32(CZ, 2, CY, HALF)
    face_z, face_y = f32(2, CY, HALF), f32(CZ, 2, HALF)
    (
        fraction, momentum, residual, direction, mapped, scaled, twice,
        high, low, north_edge, south_edge, high_face, low_face, north_face, south_face, dots,
    ) = pl.pallas_call(
        functools.partial(field_kernel, grid_rows),
        out_shape=(f32(CZ, CY, CX), f32(CZ, 3, CY, CX))
        + (halves,) * 5
        + (face_z, face_z, face_y, face_y) * 2
        + (f32(4),),
        in_specs=[smem_spec()] + [vmem_spec()] * 4 + [pl.BlockSpec(memory_space=pl.ANY)] + [vmem_spec()] * 3,
        out_specs=tuple([vmem_spec()] * 15 + [smem_spec()]),
        scratch_shapes=[pltpu.VMEM((CZ + 2, 2, YE, HALF), jnp.float32)] * 3
        + [
            pltpu.VMEM((4, ZE, 2, YE, HALF), jnp.float32),
            pltpu.VMEM((4, ZE, 2, YE, HALF), jnp.float32),
            pltpu.VMEM((CZ + 4, 2, YE, HALF), jnp.float32),
            pltpu.VMEM((CZ + 4, 2, YE, HALF), jnp.float32),
            pltpu.VMEM((CZ + 4, 2, YE, HALF), jnp.float32),
            pltpu.VMEM((CZ + 4, 2, YE, HALF), jnp.float32),
            pltpu.VMEM((CZ + 2, 2, YE, HALF), jnp.float32),
            pltpu.VMEM((6, YE, HALF), jnp.float32),
        ]
        + deposit_scratch()
        + [pltpu.SemaphoreType.DMA],
        compiler_params=params(),
        name="fields",
    )(row_first, below, above, south, north, acc, gas_density, pressure_prev, divergence)

    scaled_below = lax.ppermute(high, "gz", up_z)
    scaled_above = lax.ppermute(low, "gz", down_z)
    scaled_south = lax.ppermute(north_edge, "gy", up_y)
    scaled_north = lax.ppermute(south_edge, "gy", down_y)
    every = size_z * size_y
    received = (scaled_below, scaled_above, scaled_south, scaled_north)
    faces = (low_face, high_face, south_face, north_face)
    sent = pl.pallas_call(
        second_kernel,
        out_shape=f32(every, 128),
        in_specs=[smem_spec()] + [vmem_spec()] * 12,
        out_specs=vmem_spec(),
        compiler_params=params(),
        name="second",
    )(dots, *received, low, high, south_edge, north_edge, *faces)
    got = lax.all_to_all(sent, ("gz", "gy"), 0, 0, tiled=True)
    pressure, final = pl.pallas_call(
        final_kernel,
        out_shape=(f32(CZ, CY, CX), f32(CZ, CY, CX)),
        in_specs=[vmem_spec()] * 15,
        out_specs=(vmem_spec(), vmem_spec()),
        compiler_params=params(),
        name="final",
    )(got, pressure_prev, residual, direction, mapped, scaled, twice, *received, *faces)
    return (fraction, momentum, pressure, final)


def solution(mesh):
    return jax.shard_map(
        on_device,
        mesh=mesh,
        in_specs=(
            P(("gz", "gy")),
            P(None, ("gz", "gy")),
            P(("gz", "gy")),
            P(None, ("gz", "gy")),
            P("gz", "gy"),
            P("gz", "gy", None),
            P("gz", "gy", None),
            P("gz", "gy", None),
        ),
        out_specs=(
            P("gz", "gy", None),
            P("gz", None, "gy", None),
            P("gz", "gy", None),
            P("gz", "gy", None),
        ),
        check_vma=False,
    )
```

```python
import functools

import jax
import jax.numpy as jnp
from jax import lax
from jax.experimental import pallas as pl
from jax.experimental.pallas import tpu as pltpu
from jax.sharding import PartitionSpec as P

CZ = 8
CY = 64
CX = 256
PCAP = 4096
ITERS = 2
REACH = 5
ZE = CZ + 2 * REACH
YE = 88
LEAD = 12
LIST = PCAP // 256
TILES = CY // 8
HALF = 128
CHUNK = 256
TALL = 16

smooth_rate = 0.15
stiffness = 0.002

VMEM_LIMIT = 48 * 1024 * 1024


def chunk_values(parcels, grid_rows, row_first, shift_y):
    cell = parcels[0:1].astype(jnp.int32)
    home_z = lax.shift_right_logical(cell, 14)
    home_y = lax.shift_right_logical(cell, 8) & 63
    home_x = cell & 255
    count = parcels.shape[1]
    taps = lax.broadcasted_iota(jnp.int32, (8, count), 0).astype(jnp.float32) - 3.0

    def tap_table(offset, inside):
        distance = taps + 0.5 - offset
        weight = jnp.where(inside, jnp.exp(-0.5 * distance * distance), 0.0)
        return weight * (1.0 / jnp.sum(weight, axis=0, keepdims=True))

    seven = taps < 3.5
    place_y = taps + (home_y.astype(jnp.float32) + (row_first + shift_y))
    place_x = taps + home_x.astype(jnp.float32)
    table_z = tap_table(parcels[1:2], seven)
    table_y = tap_table(parcels[2:3], seven & (place_y >= 0.0) & (place_y < grid_rows))
    table_x = tap_table(parcels[3:4], seven & (place_x >= 0.0) & (place_x < float(CX)))
    return home_z, home_y, home_x, table_z, table_y, table_x


def axis_rows(rows, first, home, table, least=None):
    count = home.shape[1]
    lane_row = lax.broadcasted_iota(jnp.int32, (8, count), 0)
    tap_base = lane_row - (home - 3)
    tiles = []
    for tile in range(rows // 8):
        at = first + 8 * tile
        tap = tap_base + at
        fits = (tap & -8) == 0
        if least is not None:
            fits = fits & (lane_row >= least - at)
        tiles.append(jnp.take_along_axis(table, jnp.where(fits, tap, 7), axis=0))
    return tiles[0] if len(tiles) == 1 else jnp.concatenate(tiles, axis=0)


def row_of(cell):
    return lax.shift_right_logical(cell.astype(jnp.int32), 8) & 63


def count_where(condition):
    return jnp.sum(condition.astype(jnp.float32)).astype(jnp.int32)


def deposit(parcels_ref, base, row_first, grid_rows, shift_z, shift_y, planes, plane_first, window, lead, acc_first, acc_ref, lhs_ref, rhs_ref):
    rows = TALL if window is None else 8
    volume = parcels_ref[base : base + LIST, 4, :]
    begin = 0
    if shift_y == 0:
        total = count_where(volume != 0.0)
    else:
        home_row = row_of(parcels_ref[base : base + LIST, 0, :])
        if shift_y < 0:
            total = count_where(volume != 0.0)
            begin = lax.shift_right_logical(
                count_where((volume != 0.0) & (home_row < CY - 3 - REACH)), CHUNK.bit_length() - 1
            )
        else:
            total = count_where((volume != 0.0) & (home_row < 3 + REACH))

    def chunk_step(index, carry):
        start = index * CHUNK
        parcels = parcels_ref[base + index]
        home_z, home_y, home_x, table_z, table_y, table_x = chunk_values(
            parcels, grid_rows, row_first, float(shift_y)
        )
        block = 64
        for part in range(CX // block):
            weight_x = axis_rows(block, part * block, home_x, table_x)
            rhs_ref[part * block : (part + 1) * block, :] = weight_x.astype(jnp.bfloat16)
        rows_z = -(-planes // 8) * 8
        weight_z = axis_rows(rows_z, plane_first - REACH - shift_z, home_z, table_z)
        loaded = [
            weight_z * (parcels[4:5] if field == 0 else parcels[4:5] * parcels[4 + field : 5 + field])
            for field in range(4)
        ]

        def spread_window(first, least):
            weight_y = axis_rows(
                rows, first - (lead + shift_y), home_y, table_y,
                None if least is None else least - lead,
            )
            for field in range(4):
                for pair in range(planes // 2):
                    both = jnp.concatenate(
                        [
                            loaded[field][2 * pair : 2 * pair + 1] * weight_y,
                            loaded[field][2 * pair + 1 : 2 * pair + 2] * weight_y,
                        ],
                        axis=0,
                    )
                    at = (field * planes + 2 * pair) * rows
                    lhs_ref[at : at + 2 * rows, :] = both.astype(jnp.bfloat16)

        def add_window(first):
            for field in range(4):
                product = lax.dot_general(
                    lhs_ref[field * planes * rows : (field + 1) * planes * rows, :],
                    rhs_ref[...],
                    (((1,), (1,)), ((), ())),
                    preferred_element_type=jnp.float32,
                )
                for plane in range(planes):
                    for half in range(2):
                        acc_ref[field, plane_first - acc_first + plane, half, pl.ds(first, rows), :] += product[
                            plane * rows : (plane + 1) * rows, half * HALF : (half + 1) * HALF
                        ]

        if window is not None:
            spread_window(window, None)
            add_window(window)
            return carry

        slot = lax.broadcasted_iota(jnp.int32, (1, CHUNK), 1) + start
        row_home = home_y.astype(jnp.float32)
        lowest = jnp.min(jnp.where(slot < total, row_home, float(CY))).astype(jnp.int32)
        highest = jnp.max(jnp.where(slot < total, row_home, 0.0)).astype(jnp.int32)
        row_low = lowest + (lead - 3)
        row_high = highest + (lead + 4)

        def window_step(carried):
            logical = carried
            first = jnp.minimum(logical, acc_ref.shape[3] - TALL)
            spread_window(first, logical)
            add_window(first)
            return logical + TALL

        lax.while_loop(lambda carried: carried < row_high, window_step, row_low)
        return carry

    end = lax.shift_right_logical(total + (CHUNK - 1), CHUNK.bit_length() - 1)
    lax.fori_loop(begin, end, chunk_step, 0)


def sort_kernel(count_ref, cell_ref, offset_ref, volume_ref, force_ref, guess_ref, density_ref, diverge_ref, up_ref, down_ref, rows_ref, cell_held_ref, data_ref, hot_ref, prefix_ref, dest_ref, lhs_ref, total_ref, sems):
    lists = [
        pltpu.make_async_copy(cell_ref, cell_held_ref, sems.at[0]),
        pltpu.make_async_copy(offset_ref, data_ref.at[1:4], sems.at[1]),
        pltpu.make_async_copy(volume_ref, data_ref.at[4:5], sems.at[2]),
        pltpu.make_async_copy(force_ref, data_ref.at[5:8], sems.at[3]),
    ]
    edges = []
    for out_ref, upper in ((up_ref, True), (down_ref, False)):
        at = LIST
        for source, depth in ((guess_ref, 2), (density_ref, 2), (diverge_ref, 1)):
            for plane in range(depth):
                edges.append(
                    pltpu.make_async_copy(
                        source.at[CZ - depth + plane if upper else plane],
                        out_ref.at[at : at + TILES],
                        sems.at[4 + len(edges)],
                    )
                )
                at += TILES
    for part, source in enumerate((guess_ref, density_ref, diverge_ref)):
        for side in range(2):
            edges.append(
                pltpu.make_async_copy(
                    source.at[:, side * (TILES - 1)], rows_ref.at[2 * part + side], sems.at[4 + len(edges)]
                )
            )
    for copy in lists + edges:
        copy.start()
    for copy in lists:
        copy.wait()
    data_ref[0:1, :] = cell_held_ref[...].astype(jnp.float32)
    live_count = count_ref[0, 0]
    block = 256
    blocks = PCAP // block
    bins = lax.broadcasted_iota(jnp.int32, (CY, block), 0)
    slots = lax.broadcasted_iota(jnp.int32, (1, block), 1)

    def hot_of(index):
        cut = slice(index * block, (index + 1) * block)
        home_row = lax.shift_right_logical(cell_held_ref[:, cut], 8) & 63
        return (bins == home_row) & (slots + index * block < live_count)

    for index in range(blocks):
        hot_ref[index * CY : (index + 1) * CY, :] = hot_of(index).astype(jnp.float32).astype(jnp.bfloat16)
    before = lax.broadcasted_iota(jnp.int32, (block, block), 0)
    after = lax.broadcasted_iota(jnp.int32, (block, block), 1)
    upto = (before <= after).astype(jnp.float32).astype(jnp.bfloat16)
    prefix_ref[...] = jnp.dot(hot_ref[...], upto, preferred_element_type=jnp.float32)
    carry = jnp.zeros((CY, 1), jnp.float32)
    carries = []
    for index in range(blocks):
        carries.append(carry)
        carry = carry + prefix_ref[index * CY : (index + 1) * CY, block - 1 : block]
    total = jnp.broadcast_to(carry, (CY, 128))
    row = lax.broadcasted_iota(jnp.int32, (CY, 128), 0)
    summed = total
    for shift in (1, 2, 4, 8, 16, 32):
        summed = summed + jnp.where(row >= shift, pltpu.roll(summed, shift, 0), 0.0)
    first = (summed - total)[:, 0:1]
    for index in range(blocks):
        cut = slice(index * block, (index + 1) * block)
        place = prefix_ref[index * CY : (index + 1) * CY, :] + (first + carries[index])
        hot = hot_of(index)
        dest = jnp.sum(jnp.where(hot, place, 0.0), axis=0, keepdims=True) - 1.0
        dest_ref[:, cut] = dest.astype(jnp.int32)

    total_ref[...] = jnp.zeros_like(total_ref)
    width = 512

    def route(index, unused):
        start = pl.multiple_of(index * width, width)
        dest = dest_ref[:, pl.ds(start, width)]
        high = lax.shift_right_arithmetic(dest, 8)
        low = dest & 255
        data = data_ref[:, pl.ds(start, width)]
        top = data.astype(jnp.bfloat16).astype(jnp.float32)
        rest = data - top
        middle = rest.astype(jnp.bfloat16).astype(jnp.float32)
        lanes = lax.broadcasted_iota(jnp.int32, (256, width), 0)
        rhs = (lanes == low).astype(jnp.float32).astype(jnp.bfloat16)
        wide = jnp.broadcast_to(high, (8, width))
        for split, values in enumerate((top, middle, rest - middle)):
            for pair in range(8):
                both = jnp.concatenate(
                    [
                        jnp.where(wide == 2 * pair, values, 0.0),
                        jnp.where(wide == 2 * pair + 1, values, 0.0),
                    ],
                    axis=0,
                )
                at = split * 128 + pair * 16
                lhs_ref[at : at + 16, :] = both.astype(jnp.bfloat16)
        total_ref[...] += lax.dot_general(
            lhs_ref[...], rhs, (((1,), (1,)), ((), ())), preferred_element_type=jnp.float32
        )
        return unused

    steps = lax.shift_right_logical(live_count + (width - 1), 9)
    lax.fori_loop(0, steps, route, 0)
    for part in range(LIST):
        at = part * 8
        sorted_part = (
            total_ref[at : at + 8, :] + total_ref[128 + at : 136 + at, :]
        ) + total_ref[256 + at : 264 + at, :]
        up_ref[part] = sorted_part
        down_ref[part] = sorted_part
    for copy in edges:
        copy.wait()


FIELDS = ((2, 2), (2, 2), (1, 1))


def pack_kernel(sorted_ref, below_ref, above_ref, edge_ref, north_ref, south_ref):
    for out_ref in (north_ref, south_ref):
        for index, source in enumerate((sorted_ref, below_ref, above_ref)):
            out_ref[index * LIST : (index + 1) * LIST] = source[0:LIST]
        out_ref[3 * LIST + 7, 2:8, :] = jnp.zeros((6, CX), jnp.float32)
    for side, out_ref in ((1, north_ref), (0, south_ref)):
        slot = 0
        for part, (depth, wide) in enumerate(FIELDS):
            first = (0, 2, 4)[part]
            rows = slice(8 - wide, 8) if side else slice(0, wide)
            for plane in range(CZ + 2 * depth):
                if depth <= plane < CZ + depth:
                    values = edge_ref[2 * part + side, plane - depth, rows, :]
                else:
                    ref, inner = (below_ref, plane) if plane < depth else (above_ref, plane - CZ - depth)
                    values = ref[LIST + (first + inner) * TILES + side * (TILES - 1), rows, :]
                out_ref[3 * LIST + slot // 8, slot % 8 : slot % 8 + wide, :] = values
                slot += wide


def middle_deposit(list_ref, row_first, grid_rows, shift_z, planes, plane_first, acc_first, acc_ref, lhs_ref, rhs_ref):
    deposit(
        list_ref, 0, row_first, grid_rows, shift_z, 0, planes, plane_first, None, LEAD - MID.start,
        acc_first, acc_ref, lhs_ref, rhs_ref,
    )


def own_kernel(grid_rows, row_ref, parcels_ref, acc_ref, lhs_ref, rhs_ref):
    row_first = row_ref[0].astype(jnp.float32)
    acc_ref[...] = jnp.zeros_like(acc_ref)
    middle_deposit(parcels_ref, row_first, grid_rows, 0, 14, 2, 2, acc_ref, lhs_ref, rhs_ref)


def z_kernel(grid_rows, row_ref, below_ref, above_ref, acc_ref, lhs_ref, rhs_ref):
    row_first = row_ref[0].astype(jnp.float32)
    acc_ref[...] = jnp.zeros_like(acc_ref)
    middle_deposit(below_ref, row_first, grid_rows, -CZ, 8, 0, 0, acc_ref, lhs_ref, rhs_ref)
    middle_deposit(above_ref, row_first, grid_rows, CZ, 8, 10, 2, acc_ref, lhs_ref, rhs_ref)


def gather_fields(south_ref, north_ref, below_ref, above_ref, sources, targets):
    slot = 0
    for part, (own_ref, out_ref, (depth, wide)) in enumerate(zip(sources, targets, FIELDS)):
        first = (0, 2, 4)[part]
        for plane in range(CZ + 2 * depth):
            for half in range(2):
                cut = slice(half * HALF, (half + 1) * HALF)
                if depth <= plane < CZ + depth:
                    out_ref[plane, half, OWN, :] = own_ref[plane - depth, :, cut]
                else:
                    ref, inner = (below_ref, plane) if plane < depth else (above_ref, plane - CZ - depth)
                    at = LIST + (first + inner) * TILES
                    for tile in range(TILES):
                        out_ref[plane, half, LEAD + 8 * tile : LEAD + 8 * tile + 8, :] = ref[at + tile, :, cut]
                edge = 3 * LIST + slot // 8
                inner_rows = slice(slot % 8, slot % 8 + wide)
                out_ref[plane, half, LEAD - wide : LEAD, :] = south_ref[edge, inner_rows, cut]
                out_ref[plane, half, LEAD + CY : LEAD + CY + wide, :] = north_ref[edge, inner_rows, cut]
            slot += wide


def beside_y(row_first, grid_rows, south_ref, north_ref, acc_ref, lhs_ref, rhs_ref):
    for parcels_ref, shift_y, window in (
        (south_ref, -CY, LEAD - REACH),
        (north_ref, CY, LEAD + CY - 3),
    ):
        for part, (shift_z, planes, plane_first) in enumerate(((0, 14, 2), (-CZ, 8, 0), (CZ, 8, 10))):
            deposit(
                parcels_ref, LIST * part, row_first, grid_rows, shift_z, shift_y, planes, plane_first,
                window, LEAD, 0, acc_ref, lhs_ref, rhs_ref,
            )


MID = slice(8, 80)
LOW = slice(7, 79)
HIGH = slice(9, 81)
OWN = slice(LEAD, LEAD + CY)


def x_pair(left, right):
    lane = lax.broadcasted_iota(jnp.int32, left.shape, 1)
    start, stop = lane == 0, lane == HALF - 1
    left_west, right_west = pltpu.roll(left, 1, 1), pltpu.roll(right, 1, 1)
    left_east, right_east = pltpu.roll(left, HALF - 1, 1), pltpu.roll(right, HALF - 1, 1)
    return (
        jnp.where(start, 0.0, left_west) + jnp.where(stop, right_east, left_east),
        jnp.where(start, left_west, right_west) + jnp.where(stop, 0.0, right_east),
    )


def x_slope(left, right):
    lane = lax.broadcasted_iota(jnp.int32, left.shape, 1)
    start, stop = lane == 0, lane == HALF - 1
    left_west, right_west = pltpu.roll(left, 1, 1), pltpu.roll(right, 1, 1)
    left_east, right_east = pltpu.roll(left, HALF - 1, 1), pltpu.roll(right, HALF - 1, 1)
    return (
        jnp.where(stop, right_east, left_east) - jnp.where(start, 0.0, left_west),
        jnp.where(stop, 0.0, right_east) - jnp.where(start, left_west, right_west),
    )


def beside_of(ref, plane):
    centre = [ref[plane, half, MID, :] for half in range(2)]
    pairs = x_pair(*centre)
    sums = [
        (ref[plane - 1, half, MID, :] + ref[plane + 1, half, MID, :])
        + (ref[plane, half, LOW, :] + ref[plane, half, HIGH, :])
        + pairs[half]
        for half in range(2)
    ]
    return centre, sums


def field_kernel(
    grid_rows,
    row_ref,
    below_ref,
    above_ref,
    south_ref,
    north_ref,
    acc_own_ref,
    acc_z_ref,
    density_own_ref,
    guess_own_ref,
    diverge_own_ref,
    fraction_ref,
    momentum_ref,
    residual_ref,
    direction_ref,
    mapped_ref,
    scaled_own_ref,
    twice_ref,
    high_ref,
    low_ref,
    north_edge_ref,
    south_edge_ref,
    high_face_ref,
    low_face_ref,
    north_face_ref,
    south_face_ref,
    dots_ref,
    scaled_ref,
    mobility_ref,
    diagonal_ref,
    first_ref,
    second_ref,
    mob_ref,
    guess_ref,
    wide_ref,
    density_ref,
    diverge_ref,
    rate_ref,
    lhs_ref,
    rhs_ref,
    load_sems,
):
    row_first = row_ref[0].astype(jnp.float32)
    loads = [
        pltpu.make_async_copy(acc_z_ref.at[:, 0:CZ], first_ref.at[:, 0:CZ, :, MID, :], load_sems.at[0]),
        pltpu.make_async_copy(
            acc_z_ref.at[:, CZ : 2 * CZ], first_ref.at[:, CZ + 2 : ZE, :, MID, :], load_sems.at[1]
        ),
        pltpu.make_async_copy(acc_own_ref, second_ref.at[:, 2:16, :, MID, :], load_sems.at[2]),
    ]
    for load in loads:
        load.start()
    for field in range(4):
        edge = jnp.zeros((ZE, 2, 8, HALF), jnp.float32)
        first_ref[field, :, :, 0 : MID.start, :] = edge
        first_ref[field, :, :, MID.stop : YE, :] = edge
        first_ref[field, CZ : CZ + 2, :, MID, :] = jnp.zeros((2, 2, 72, HALF), jnp.float32)
    gather_fields(
        south_ref,
        north_ref,
        below_ref,
        above_ref,
        (guess_own_ref, density_own_ref, diverge_own_ref),
        (guess_ref, density_ref, diverge_ref),
    )
    loads[0].wait()
    loads[1].wait()
    beside_y(row_first, grid_rows, south_ref, north_ref, first_ref, lhs_ref, rhs_ref)
    loads[2].wait()

    def add_own(plane, carry):
        for field in range(4):
            for half in range(2):
                first_ref[field, plane, half, MID, :] += second_ref[field, plane, half, MID, :]
        return carry

    lax.fori_loop(2, 16, add_own, 0)

    row = lax.broadcasted_iota(jnp.int32, (YE, HALF), 0).astype(jnp.float32) + (row_first - LEAD)
    lane = lax.broadcasted_iota(jnp.int32, (YE, HALF), 1)
    within = (row >= 0.0) & (row < grid_rows)
    inside = within.astype(jnp.float32)
    count_y = (row >= 1.0).astype(jnp.float32) + (row < grid_rows - 1.0).astype(jnp.float32)
    for half in range(2):
        count_x = 2.0 - (lane == (0, HALF - 1)[half]).astype(jnp.float32)
        rate_ref[half] = inside * (1.0 - smooth_rate * (2.0 + count_y + count_x))
    rate_ref[2] = inside * smooth_rate
    for index, reach in enumerate((2.0, 1.0, 0.0)):
        near = within & (row >= row_first - reach) & (row < row_first + (CY + reach))
        rate_ref[3 + index] = near.astype(jnp.float32)

    for sweep, (source, target) in enumerate(
        ((first_ref, second_ref), (second_ref, first_ref), (first_ref, second_ref))
    ):

        def sweep_plane(plane, fields, source=source, target=target):
            for field in fields:
                centre, sums = beside_of(source.at[field], plane)
                for half in range(2):
                    target[field, plane, half, MID, :] = (
                        rate_ref[half, MID, :] * centre[half] + rate_ref[2, MID, :] * sums[half]
                    )

        def sweep_step(plane, carry, sweep_plane=sweep_plane):
            sweep_plane(plane, (0, 1, 2, 3))
            return carry

        sweep_plane(sweep + 1, (0, 1))
        lax.fori_loop(sweep + 2, ZE - 2 - sweep, sweep_step, 0)
        sweep_plane(ZE - 2 - sweep, (0, 1))

    filtered = second_ref

    def mobility_step(plane, carry):
        known = rate_ref[3] > 0.5
        for half in range(2):
            fraction = 1.0 / (1.0 + filtered[0, plane + 3, half])
            mobility = jnp.where(known, fraction / density_ref[plane, half], 0.0)
            mob_ref[plane, half] = mobility
            wide_ref[plane, half] = mobility * guess_ref[plane, half]
        return carry

    lax.fori_loop(0, CZ + 4, mobility_step, 0)

    def output_step(plane, carry):
        for half in range(2):
            cut = slice(half * HALF, (half + 1) * HALF)
            fraction_ref[plane, :, cut] = 1.0 / (1.0 + filtered[0, plane + REACH, half, OWN, :])
            for part in range(3):
                momentum_ref[plane, part, :, cut] = filtered[part + 1, plane + REACH, half, OWN, :]
        return carry

    lax.fori_loop(0, CZ, output_step, 0)

    direct_ref, product_ref, remain_ref = first_ref.at[0], first_ref.at[1], first_ref.at[2]

    def first_residual(plane, carry):
        at = plane + 1
        near = rate_ref[4, MID, :] > 0.5
        mobility, beside_mobility = beside_of(mob_ref, at)
        guess, beside_guess = beside_of(guess_ref, at)
        unused, beside_wide = beside_of(wide_ref, at)
        slope = x_slope(filtered[3, at + 3, 0, MID, :], filtered[3, at + 3, 1, MID, :])
        for half in range(2):
            diagonal = (3.0 + stiffness) * mobility[half] + 0.5 * beside_mobility[half]
            operated = diagonal * guess[half] - 0.5 * (
                mobility[half] * beside_guess[half] + beside_wide[half]
            )
            spread = 0.5 * (filtered[1, at + 4, half, MID, :] - filtered[1, at + 2, half, MID, :])
            spread = spread + 0.5 * (
                filtered[2, at + 3, half, HIGH, :] - filtered[2, at + 3, half, LOW, :]
            )
            spread = spread + 0.5 * slope[half]
            residual = jnp.where(near, diverge_ref[plane, half, MID, :] - spread - operated, 0.0)
            direction = jnp.where(near, residual / diagonal, 0.0)
            remain_ref[plane, half, MID, :] = residual
            direct_ref[plane, half, MID, :] = direction
            product_ref[plane, half, MID, :] = direction * mobility[half]
            diagonal_ref[plane, half, MID, :] = diagonal
            mobility_ref[plane, half, MID, :] = mobility[half]
        return carry

    lax.fori_loop(0, CZ + 2, first_residual, 0)

    scaled_ref[...] = jnp.zeros_like(scaled_ref)
    again_ref = first_ref.at[3]
    for plane in (0, CZ + 1):
        again_ref[plane] = jnp.zeros((2, YE, HALF), jnp.float32)

    def map_step(plane, sums):
        at = plane + 1
        own = rate_ref[5, MID, :] > 0.5
        directions, beside_direction = beside_of(direct_ref, at)
        unused, beside_product = beside_of(product_ref, at)
        sum_rz, sum_dw, sum_uw = sums
        for half in range(2):
            residual = jnp.where(own, remain_ref[at, half, MID, :], 0.0)
            diagonal = diagonal_ref[at, half, MID, :]
            mapped = diagonal * directions[half] - 0.5 * (
                mobility_ref[at, half, MID, :] * beside_direction[half] + beside_product[half]
            )
            mapped = jnp.where(own, mapped, 0.0)
            scaled = jnp.where(own, mapped / diagonal, 0.0)
            scaled_ref[at, half, MID, :] = scaled
            again_ref[at, half, MID, :] = scaled * mobility_ref[at, half, MID, :]
            scaled_own_ref[plane, half] = scaled[4:68]
            residual_ref[plane, half] = residual[4:68]
            direction_ref[plane, half] = directions[half][4:68]
            mapped_ref[plane, half] = mapped[4:68]
            sum_rz = sum_rz + residual * directions[half]
            sum_dw = sum_dw + directions[half] * mapped
            sum_uw = sum_uw + scaled * mapped
        return sum_rz, sum_dw, sum_uw

    zero = jnp.zeros((72, HALF), jnp.float32)
    sums = lax.fori_loop(0, CZ, map_step, (zero, zero, zero))
    for index in range(3):
        dots_ref[index] = jnp.sum(sums[index])
    def again_step(plane, total):
        at = plane + 1
        centre, beside = beside_of(scaled_ref, at)
        unused, beside_again = beside_of(again_ref, at)
        for half in range(2):
            twice = diagonal_ref[at, half, MID, :] * centre[half] - 0.5 * (
                mobility_ref[at, half, MID, :] * beside[half] + beside_again[half]
            )
            twice_ref[plane, half] = twice[4:68]
            total = total + (centre[half] * twice)[4:68]
        return total

    total = lax.fori_loop(0, CZ, again_step, jnp.zeros((CY, HALF), jnp.float32))
    dots_ref[3] = jnp.sum(total)
    high_face_ref[...] = 0.5 * (mobility_ref[CZ, :, OWN, :] + mobility_ref[CZ + 1, :, OWN, :])
    low_face_ref[...] = 0.5 * (mobility_ref[1, :, OWN, :] + mobility_ref[0, :, OWN, :])
    for face_ref, inner in ((north_face_ref, LEAD + CY - 1), (south_face_ref, LEAD - 1)):
        for plane in range(CZ):
            for half in range(2):
                face_ref[plane, half : half + 1] = 0.5 * (
                    mobility_ref[plane + 1, half, inner : inner + 1, :]
                    + mobility_ref[plane + 1, half, inner + 1 : inner + 2, :]
                )
    high_ref[...] = scaled_ref[CZ, :, OWN, :]
    low_ref[...] = scaled_ref[1, :, OWN, :]
    for plane in range(CZ):
        for half in range(2):
            north_edge_ref[plane, half : half + 1] = scaled_ref[plane + 1, half, LEAD + CY - 1 : LEAD + CY, :]
            south_edge_ref[plane, half : half + 1] = scaled_ref[plane + 1, half, LEAD : LEAD + 1, :]


def second_kernel(dots_ref, *refs):
    received, own_edges, faces, sent_ref = refs[0:4], refs[4:8], refs[8:12], refs[12]
    missing = jnp.float32(0.0)
    for got_ref, own_ref, face_ref in zip(received, own_edges, faces):
        missing = missing + jnp.sum(got_ref[...] * own_ref[...] * face_ref[...])
    values = (dots_ref[0], dots_ref[1], dots_ref[2], dots_ref[3] - missing)
    column = lax.broadcasted_iota(jnp.int32, sent_ref.shape, 1)
    sent = jnp.zeros(sent_ref.shape, jnp.float32)
    for index, value in enumerate(values):
        sent = jnp.where(column == index, value, sent)
    sent_ref[...] = sent


def final_kernel(got_ref, guess_ref, residual_ref, direction_ref, mapped_ref, scaled_ref, twice_ref, below_ref, above_ref, south_ref, north_ref, low_face_ref, high_face_ref, south_face_ref, north_face_ref, pressure_ref, final_ref):
    sums = jnp.sum(got_ref[...], axis=0, keepdims=True)
    sum_rz, sum_dw, sum_uw, sum_uv = (sums[:, index : index + 1] for index in range(4))
    step = sum_rz / sum_dw
    next_rz = sum_rz - 2.0 * step * sum_dw + step * step * sum_uw
    along = 1.0 + next_rz / sum_rz
    curvature = along * along * sum_dw - 2.0 * step * along * sum_uw + step * step * sum_uv
    next_step = next_rz / curvature
    first = step + next_step * along
    last = next_step * step

    row = lax.broadcasted_iota(jnp.int32, (CY, HALF), 0)
    for plane in range(CZ):
        for half in range(2):
            cut = slice(half * HALF, (half + 1) * HALF)
            south = south_ref[plane, half : half + 1] * south_face_ref[plane, half : half + 1]
            north = north_ref[plane, half : half + 1] * north_face_ref[plane, half : half + 1]
            past = jnp.where(row == 0, south, 0.0) + jnp.where(row == CY - 1, north, 0.0)
            if plane == 0:
                past = past + below_ref[half] * low_face_ref[half]
            if plane == CZ - 1:
                past = past + above_ref[half] * high_face_ref[half]
            twice = twice_ref[plane, half] - past
            pressure_ref[plane, :, cut] = (
                guess_ref[plane, :, cut]
                + first * direction_ref[plane, half]
                - last * scaled_ref[plane, half]
            )
            final_ref[plane, :, cut] = (
                residual_ref[plane, half] - first * mapped_ref[plane, half] + last * twice
            )


def vmem_spec():
    return pl.BlockSpec(memory_space=pltpu.VMEM)


def smem_spec():
    return pl.BlockSpec(memory_space=pltpu.SMEM)


def f32(*shape):
    return jax.ShapeDtypeStruct(shape, jnp.float32)


def params():
    return pltpu.CompilerParams(vmem_limit_bytes=VMEM_LIMIT)


def hbm_spec():
    return pl.BlockSpec(memory_space=pltpu.HBM)


def deposit_scratch():
    return [
        pltpu.VMEM((4 * 14 * TALL, CHUNK), jnp.bfloat16),
        pltpu.VMEM((CX, CHUNK), jnp.bfloat16),
    ]


def on_device(
    parcel_cell,
    parcel_offset,
    parcel_volume,
    parcel_force,
    brick_counts,
    divergence,
    pressure_prev,
    gas_density,
):
    size_z = lax.axis_size("gz")
    size_y = lax.axis_size("gy")
    grid_rows = float(size_y * CY)
    row_first = (lax.axis_index("gy") * CY).astype(jnp.int32)[None]
    up_z = [(i, (i + 1) % size_z) for i in range(size_z)]
    down_z = [((i + 1) % size_z, i) for i in range(size_z)]
    up_y = [(i, i + 1) for i in range(size_y - 1)]
    down_y = [(i + 1, i) for i in range(size_y - 1)]

    message = f32(LIST + 5 * TILES, 8, CX)
    tiled = [values.reshape(CZ, TILES, 8, CX) for values in (pressure_prev, gas_density, divergence)]
    to_up, to_down, brick_rows = pl.pallas_call(
        sort_kernel,
        out_shape=(message, message, f32(6, CZ, 8, CX)),
        in_specs=[smem_spec()] + [hbm_spec()] * 7,
        out_specs=(vmem_spec(), vmem_spec(), vmem_spec()),
        scratch_shapes=[
            pltpu.VMEM((1, PCAP), jnp.int32),
            pltpu.VMEM((8, PCAP), jnp.float32),
            pltpu.VMEM((PCAP // 256 * CY, 256), jnp.bfloat16),
            pltpu.VMEM((PCAP // 256 * CY, 256), jnp.float32),
            pltpu.VMEM((1, PCAP), jnp.int32),
            pltpu.VMEM((384, 512), jnp.bfloat16),
            pltpu.VMEM((384, 256), jnp.float32),
            pltpu.SemaphoreType.DMA((20,)),
        ],
        compiler_params=pltpu.CompilerParams(vmem_limit_bytes=60 * 1024 * 1024),
        name="order",
    )(brick_counts, parcel_cell[None], parcel_offset, parcel_volume[None], parcel_force, *tiled)
    acc_own = pl.pallas_call(
        functools.partial(own_kernel, grid_rows),
        out_shape=f32(4, 14, 2, MID.stop - MID.start, HALF),
        in_specs=[smem_spec(), vmem_spec()],
        out_specs=vmem_spec(),
        scratch_shapes=deposit_scratch(),
        compiler_params=params(),
        cost_estimate=pl.CostEstimate(flops=8_000_000_000, bytes_accessed=8_000_000, transcendentals=0),
        name="own",
    )(row_first, to_up)
    below = lax.ppermute(to_up, "gz", up_z)
    above = lax.ppermute(to_down, "gz", down_z)
    edge_rows = f32(3 * LIST + 8, 8, CX)
    to_north, to_south = pl.pallas_call(
        pack_kernel,
        out_shape=(edge_rows, edge_rows),
        in_specs=[vmem_spec()] * 4,
        out_specs=(vmem_spec(), vmem_spec()),
        compiler_params=params(),
        name="pack",
    )(to_up, below, above, brick_rows)
    south = lax.ppermute(to_north, "gy", up_y)
    north = lax.ppermute(to_south, "gy", down_y)
    acc_z = pl.pallas_call(
        functools.partial(z_kernel, grid_rows),
        out_shape=f32(4, 2 * CZ, 2, MID.stop - MID.start, HALF),
        in_specs=[smem_spec()] + [vmem_spec()] * 2,
        out_specs=vmem_spec(),
        scratch_shapes=deposit_scratch(),
        compiler_params=params(),
        cost_estimate=pl.CostEstimate(flops=8_000_000_000, bytes_accessed=8_000_000, transcendentals=0),
        name="beside_z",
    )(row_first, below, above)
    halves = f32(CZ, 2, CY, HALF)
    face_z, face_y = f32(2, CY, HALF), f32(CZ, 2, HALF)
    (
        fraction, momentum, residual, direction, mapped, scaled, twice,
        high, low, north_edge, south_edge, high_face, low_face, north_face, south_face, dots,
    ) = pl.pallas_call(
        functools.partial(field_kernel, grid_rows),
        out_shape=(f32(CZ, CY, CX), f32(CZ, 3, CY, CX))
        + (halves,) * 5
        + (face_z, face_z, face_y, face_y) * 2
        + (f32(4),),
        in_specs=[smem_spec()] + [vmem_spec()] * 4 + [pl.BlockSpec(memory_space=pl.ANY)] * 2 + [vmem_spec()] * 3,
        out_specs=tuple([vmem_spec()] * 15 + [smem_spec()]),
        scratch_shapes=[pltpu.VMEM((CZ + 2, 2, YE, HALF), jnp.float32)] * 3
        + [
            pltpu.VMEM((4, ZE, 2, YE, HALF), jnp.float32),
            pltpu.VMEM((4, ZE, 2, YE, HALF), jnp.float32),
            pltpu.VMEM((CZ + 4, 2, YE, HALF), jnp.float32),
            pltpu.VMEM((CZ + 4, 2, YE, HALF), jnp.float32),
            pltpu.VMEM((CZ + 4, 2, YE, HALF), jnp.float32),
            pltpu.VMEM((CZ + 4, 2, YE, HALF), jnp.float32),
            pltpu.VMEM((CZ + 2, 2, YE, HALF), jnp.float32),
            pltpu.VMEM((6, YE, HALF), jnp.float32),
        ]
        + deposit_scratch()
        + [pltpu.SemaphoreType.DMA((3,))],
        compiler_params=params(),
        name="fields",
    )(row_first, below, above, south, north, acc_own, acc_z, gas_density, pressure_prev, divergence)

    scaled_below = lax.ppermute(high, "gz", up_z)
    scaled_above = lax.ppermute(low, "gz", down_z)
    scaled_south = lax.ppermute(north_edge, "gy", up_y)
    scaled_north = lax.ppermute(south_edge, "gy", down_y)
    every = size_z * size_y
    received = (scaled_below, scaled_above, scaled_south, scaled_north)
    faces = (low_face, high_face, south_face, north_face)
    sent = pl.pallas_call(
        second_kernel,
        out_shape=f32(every, 128),
        in_specs=[smem_spec()] + [vmem_spec()] * 12,
        out_specs=vmem_spec(),
        compiler_params=params(),
        name="second",
    )(dots, *received, low, high, south_edge, north_edge, *faces)
    got = lax.all_to_all(sent, ("gz", "gy"), 0, 0, tiled=True)
    pressure, final = pl.pallas_call(
        final_kernel,
        out_shape=(f32(CZ, CY, CX), f32(CZ, CY, CX)),
        in_specs=[vmem_spec()] * 15,
        out_specs=(vmem_spec(), vmem_spec()),
        compiler_params=params(),
        name="final",
    )(got, pressure_prev, residual, direction, mapped, scaled, twice, *received, *faces)
    return (fraction, momentum, pressure, final)


def solution(mesh):
    return jax.shard_map(
        on_device,
        mesh=mesh,
        in_specs=(
            P(("gz", "gy")),
            P(None, ("gz", "gy")),
            P(("gz", "gy")),
            P(None, ("gz", "gy")),
            P("gz", "gy"),
            P("gz", "gy", None),
            P("gz", "gy", None),
            P("gz", "gy", None),
        ),
        out_specs=(
            P("gz", "gy", None),
            P("gz", None, "gy", None),
            P("gz", "gy", None),
            P("gz", "gy", None),
        ),
        check_vma=False,
    )
```

```python
import functools

import jax
import jax.numpy as jnp
from jax import lax
from jax.experimental import pallas as pl
from jax.experimental.pallas import tpu as pltpu
from jax.sharding import PartitionSpec as P

CZ = 8
CY = 64
CX = 256
PCAP = 4096
ITERS = 2
REACH = 5
ZE = CZ + 2 * REACH
YE = 88
LEAD = 12
LIST = PCAP // 256
TILES = CY // 8
HALF = 128
CHUNK = 256
TALL = 16

smooth_rate = 0.15
stiffness = 0.002

VMEM_LIMIT = 36 * 1024 * 1024


def chunk_values(parcels, grid_rows, row_first, shift_y):
    cell = parcels[0:1].astype(jnp.int32)
    home_z = lax.shift_right_logical(cell, 14)
    home_y = lax.shift_right_logical(cell, 8) & 63
    home_x = cell & 255
    count = parcels.shape[1]
    taps = lax.broadcasted_iota(jnp.int32, (8, count), 0).astype(jnp.float32) - 3.0

    def tap_table(offset, inside):
        distance = taps + 0.5 - offset
        weight = jnp.where(inside, jnp.exp(-0.5 * distance * distance), 0.0)
        return weight * (1.0 / jnp.sum(weight, axis=0, keepdims=True))

    seven = taps < 3.5
    place_y = taps + (home_y.astype(jnp.float32) + (row_first + shift_y))
    place_x = taps + home_x.astype(jnp.float32)
    table_z = tap_table(parcels[1:2], seven)
    table_y = tap_table(parcels[2:3], seven & (place_y >= 0.0) & (place_y < grid_rows))
    table_x = tap_table(parcels[3:4], seven & (place_x >= 0.0) & (place_x < float(CX)))
    return home_z, home_y, home_x, table_z, table_y, table_x


def axis_rows(rows, first, home, table, least=None):
    count = home.shape[1]
    lane_row = lax.broadcasted_iota(jnp.int32, (8, count), 0)
    tap_base = lane_row - (home - 3)
    tiles = []
    for tile in range(rows // 8):
        at = first + 8 * tile
        tap = tap_base + at
        fits = (tap & -8) == 0
        if least is not None:
            fits = fits & (lane_row >= least - at)
        tiles.append(jnp.take_along_axis(table, jnp.where(fits, tap, 7), axis=0))
    return tiles[0] if len(tiles) == 1 else jnp.concatenate(tiles, axis=0)


def row_of(cell):
    return lax.shift_right_logical(cell.astype(jnp.int32), 8) & 63


def count_where(condition):
    return jnp.sum(condition.astype(jnp.float32)).astype(jnp.int32)


def deposit(parcels_ref, base, row_first, grid_rows, shift_z, shift_y, planes, plane_first, window, lead, acc_first, acc_ref, lhs_ref, rhs_ref):
    rows = TALL if window is None else 8
    volume = parcels_ref[base : base + LIST, 4, :]
    begin = 0
    if shift_y == 0:
        total = count_where(volume != 0.0)
    else:
        home_row = row_of(parcels_ref[base : base + LIST, 0, :])
        if shift_y < 0:
            total = count_where(volume != 0.0)
            begin = lax.shift_right_logical(
                count_where((volume != 0.0) & (home_row < CY - 3 - REACH)), CHUNK.bit_length() - 1
            )
        else:
            total = count_where((volume != 0.0) & (home_row < 3 + REACH))

    def chunk_step(index, carry):
        start = index * CHUNK
        parcels = parcels_ref[base + index]
        home_z, home_y, home_x, table_z, table_y, table_x = chunk_values(
            parcels, grid_rows, row_first, float(shift_y)
        )
        block = 64
        for part in range(CX // block):
            weight_x = axis_rows(block, part * block, home_x, table_x)
            rhs_ref[part * block : (part + 1) * block, :] = weight_x.astype(jnp.bfloat16)
        rows_z = -(-planes // 8) * 8
        weight_z = axis_rows(rows_z, plane_first - REACH - shift_z, home_z, table_z)
        loaded = [
            weight_z * (parcels[4:5] if field == 0 else parcels[4:5] * parcels[4 + field : 5 + field])
            for field in range(4)
        ]

        def spread_window(first, least):
            weight_y = axis_rows(
                rows, first - (lead + shift_y), home_y, table_y,
                None if least is None else least - lead,
            )
            for field in range(4):
                for pair in range(planes // 2):
                    both = jnp.concatenate(
                        [
                            loaded[field][2 * pair : 2 * pair + 1] * weight_y,
                            loaded[field][2 * pair + 1 : 2 * pair + 2] * weight_y,
                        ],
                        axis=0,
                    )
                    at = (field * planes + 2 * pair) * rows
                    lhs_ref[at : at + 2 * rows, :] = both.astype(jnp.bfloat16)

        def add_window(first):
            for field in range(4):
                product = lax.dot_general(
                    lhs_ref[field * planes * rows : (field + 1) * planes * rows, :],
                    rhs_ref[...],
                    (((1,), (1,)), ((), ())),
                    preferred_element_type=jnp.float32,
                )
                for plane in range(planes):
                    for half in range(2):
                        acc_ref[field, plane_first - acc_first + plane, half, pl.ds(first, rows), :] += product[
                            plane * rows : (plane + 1) * rows, half * HALF : (half + 1) * HALF
                        ]

        if window is not None:
            spread_window(window, None)
            add_window(window)
            return carry

        slot = lax.broadcasted_iota(jnp.int32, (1, CHUNK), 1) + start
        row_home = home_y.astype(jnp.float32)
        lowest = jnp.min(jnp.where(slot < total, row_home, float(CY))).astype(jnp.int32)
        highest = jnp.max(jnp.where(slot < total, row_home, 0.0)).astype(jnp.int32)
        row_low = lowest + (lead - 3)
        row_high = highest + (lead + 4)

        def window_step(carried):
            logical = carried
            first = jnp.minimum(logical, acc_ref.shape[3] - TALL)
            spread_window(first, logical)
            add_window(first)
            return logical + TALL

        lax.while_loop(lambda carried: carried < row_high, window_step, row_low)
        return carry

    end = lax.shift_right_logical(total + (CHUNK - 1), CHUNK.bit_length() - 1)
    lax.fori_loop(begin, end, chunk_step, 0)


def sort_kernel(count_ref, cell_ref, offset_ref, volume_ref, force_ref, guess_ref, density_ref, diverge_ref, up_ref, down_ref, rows_ref, cell_held_ref, data_ref, hot_ref, prefix_ref, dest_ref, lhs_ref, total_ref, sems):
    lists = [
        pltpu.make_async_copy(cell_ref, cell_held_ref, sems.at[0]),
        pltpu.make_async_copy(offset_ref, data_ref.at[1:4], sems.at[1]),
        pltpu.make_async_copy(volume_ref, data_ref.at[4:5], sems.at[2]),
        pltpu.make_async_copy(force_ref, data_ref.at[5:8], sems.at[3]),
    ]
    edges = []
    for out_ref, upper in ((up_ref, True), (down_ref, False)):
        at = LIST
        for source, depth in ((guess_ref, 2), (density_ref, 2), (diverge_ref, 1)):
            for plane in range(depth):
                edges.append(
                    pltpu.make_async_copy(
                        source.at[CZ - depth + plane if upper else plane],
                        out_ref.at[at : at + TILES],
                        sems.at[4 + len(edges)],
                    )
                )
                at += TILES
    for part, source in enumerate((guess_ref, density_ref, diverge_ref)):
        for side in range(2):
            edges.append(
                pltpu.make_async_copy(
                    source.at[:, side * (TILES - 1)], rows_ref.at[2 * part + side], sems.at[4 + len(edges)]
                )
            )
    for copy in lists + edges:
        copy.start()
    for copy in lists:
        copy.wait()
    data_ref[0:1, :] = cell_held_ref[...].astype(jnp.float32)
    live_count = count_ref[0, 0]
    block = 256
    blocks = PCAP // block
    bins = lax.broadcasted_iota(jnp.int32, (CY, block), 0)
    slots = lax.broadcasted_iota(jnp.int32, (1, block), 1)

    def hot_of(index):
        cut = slice(index * block, (index + 1) * block)
        home_row = lax.shift_right_logical(cell_held_ref[:, cut], 8) & 63
        return (bins == home_row) & (slots + index * block < live_count)

    for index in range(blocks):
        hot_ref[index * CY : (index + 1) * CY, :] = hot_of(index).astype(jnp.float32).astype(jnp.bfloat16)
    before = lax.broadcasted_iota(jnp.int32, (block, block), 0)
    after = lax.broadcasted_iota(jnp.int32, (block, block), 1)
    upto = (before <= after).astype(jnp.float32).astype(jnp.bfloat16)
    prefix_ref[...] = jnp.dot(hot_ref[...], upto, preferred_element_type=jnp.float32)
    carry = jnp.zeros((CY, 1), jnp.float32)
    carries = []
    for index in range(blocks):
        carries.append(carry)
        carry = carry + prefix_ref[index * CY : (index + 1) * CY, block - 1 : block]
    total = jnp.broadcast_to(carry, (CY, 128))
    row = lax.broadcasted_iota(jnp.int32, (CY, 128), 0)
    summed = total
    for shift in (1, 2, 4, 8, 16, 32):
        summed = summed + jnp.where(row >= shift, pltpu.roll(summed, shift, 0), 0.0)
    first = (summed - total)[:, 0:1]
    for index in range(blocks):
        cut = slice(index * block, (index + 1) * block)
        place = prefix_ref[index * CY : (index + 1) * CY, :] + (first + carries[index])
        hot = hot_of(index)
        dest = jnp.sum(jnp.where(hot, place, 0.0), axis=0, keepdims=True) - 1.0
        dest_ref[:, cut] = dest.astype(jnp.int32)

    total_ref[...] = jnp.zeros_like(total_ref)
    width = 512

    def route(index, unused):
        start = pl.multiple_of(index * width, width)
        dest = dest_ref[:, pl.ds(start, width)]
        high = lax.shift_right_arithmetic(dest, 8)
        low = dest & 255
        data = data_ref[:, pl.ds(start, width)]
        top = data.astype(jnp.bfloat16).astype(jnp.float32)
        rest = data - top
        middle = rest.astype(jnp.bfloat16).astype(jnp.float32)
        lanes = lax.broadcasted_iota(jnp.int32, (256, width), 0)
        rhs = (lanes == low).astype(jnp.float32).astype(jnp.bfloat16)
        wide = jnp.broadcast_to(high, (8, width))
        for split, values in enumerate((top, middle, rest - middle)):
            for pair in range(8):
                both = jnp.concatenate(
                    [
                        jnp.where(wide == 2 * pair, values, 0.0),
                        jnp.where(wide == 2 * pair + 1, values, 0.0),
                    ],
                    axis=0,
                )
                at = split * 128 + pair * 16
                lhs_ref[at : at + 16, :] = both.astype(jnp.bfloat16)
        total_ref[...] += lax.dot_general(
            lhs_ref[...], rhs, (((1,), (1,)), ((), ())), preferred_element_type=jnp.float32
        )
        return unused

    steps = lax.shift_right_logical(live_count + (width - 1), 9)
    lax.fori_loop(0, steps, route, 0)
    for part in range(LIST):
        at = part * 8
        sorted_part = (
            total_ref[at : at + 8, :] + total_ref[128 + at : 136 + at, :]
        ) + total_ref[256 + at : 264 + at, :]
        up_ref[part] = sorted_part
        down_ref[part] = sorted_part
    for copy in edges:
        copy.wait()


FIELDS = ((2, 2), (2, 2), (1, 1))


def pack_kernel(sorted_ref, below_ref, above_ref, edge_ref, north_ref, south_ref):
    for out_ref in (north_ref, south_ref):
        for index, source in enumerate((sorted_ref, below_ref, above_ref)):
            out_ref[index * LIST : (index + 1) * LIST] = source[0:LIST]
        out_ref[3 * LIST + 7, 2:8, :] = jnp.zeros((6, CX), jnp.float32)
    for side, out_ref in ((1, north_ref), (0, south_ref)):
        slot = 0
        for part, (depth, wide) in enumerate(FIELDS):
            first = (0, 2, 4)[part]
            rows = slice(8 - wide, 8) if side else slice(0, wide)
            for plane in range(CZ + 2 * depth):
                if depth <= plane < CZ + depth:
                    values = edge_ref[2 * part + side, plane - depth, rows, :]
                else:
                    ref, inner = (below_ref, plane) if plane < depth else (above_ref, plane - CZ - depth)
                    values = ref[LIST + (first + inner) * TILES + side * (TILES - 1), rows, :]
                out_ref[3 * LIST + slot // 8, slot % 8 : slot % 8 + wide, :] = values
                slot += wide


def middle_deposit(list_ref, row_first, grid_rows, shift_z, planes, plane_first, acc_first, acc_ref, lhs_ref, rhs_ref):
    deposit(
        list_ref, 0, row_first, grid_rows, shift_z, 0, planes, plane_first, None, LEAD - MID.start,
        acc_first, acc_ref, lhs_ref, rhs_ref,
    )


def own_kernel(grid_rows, row_ref, parcels_ref, acc_ref, lhs_ref, rhs_ref):
    row_first = row_ref[0].astype(jnp.float32)
    acc_ref[...] = jnp.zeros_like(acc_ref)
    middle_deposit(parcels_ref, row_first, grid_rows, 0, 14, 2, 2, acc_ref, lhs_ref, rhs_ref)


def z_kernel(grid_rows, row_ref, below_ref, above_ref, acc_ref, lhs_ref, rhs_ref):
    row_first = row_ref[0].astype(jnp.float32)
    acc_ref[...] = jnp.zeros_like(acc_ref)
    middle_deposit(below_ref, row_first, grid_rows, -CZ, 8, 0, 0, acc_ref, lhs_ref, rhs_ref)
    middle_deposit(above_ref, row_first, grid_rows, CZ, 8, 10, 2, acc_ref, lhs_ref, rhs_ref)


def gather_fields(south_ref, north_ref, below_ref, above_ref, sources, targets):
    slot = 0
    for part, (own_ref, out_ref, (depth, wide)) in enumerate(zip(sources, targets, FIELDS)):
        first = (0, 2, 4)[part]
        for plane in range(CZ + 2 * depth):
            for half in range(2):
                cut = slice(half * HALF, (half + 1) * HALF)
                if depth <= plane < CZ + depth:
                    out_ref[plane, half, OWN, :] = own_ref[plane - depth, :, cut]
                else:
                    ref, inner = (below_ref, plane) if plane < depth else (above_ref, plane - CZ - depth)
                    at = LIST + (first + inner) * TILES
                    for tile in range(TILES):
                        out_ref[plane, half, LEAD + 8 * tile : LEAD + 8 * tile + 8, :] = ref[at + tile, :, cut]
                edge = 3 * LIST + slot // 8
                inner_rows = slice(slot % 8, slot % 8 + wide)
                out_ref[plane, half, LEAD - wide : LEAD, :] = south_ref[edge, inner_rows, cut]
                out_ref[plane, half, LEAD + CY : LEAD + CY + wide, :] = north_ref[edge, inner_rows, cut]
            slot += wide


def beside_y(row_first, grid_rows, south_ref, north_ref, acc_ref, lhs_ref, rhs_ref):
    for parcels_ref, shift_y, window in (
        (south_ref, -CY, LEAD - REACH),
        (north_ref, CY, LEAD + CY - 3),
    ):
        for part, (shift_z, planes, plane_first) in enumerate(((0, 14, 2), (-CZ, 8, 0), (CZ, 8, 10))):
            deposit(
                parcels_ref, LIST * part, row_first, grid_rows, shift_z, shift_y, planes, plane_first,
                window, LEAD, 0, acc_ref, lhs_ref, rhs_ref,
            )


MID = slice(8, 80)
LOW = slice(7, 79)
HIGH = slice(9, 81)
OWN = slice(LEAD, LEAD + CY)


def x_pair(left, right):
    lane = lax.broadcasted_iota(jnp.int32, left.shape, 1)
    start, stop = lane == 0, lane == HALF - 1
    left_west, right_west = pltpu.roll(left, 1, 1), pltpu.roll(right, 1, 1)
    left_east, right_east = pltpu.roll(left, HALF - 1, 1), pltpu.roll(right, HALF - 1, 1)
    return (
        jnp.where(start, 0.0, left_west) + jnp.where(stop, right_east, left_east),
        jnp.where(start, left_west, right_west) + jnp.where(stop, 0.0, right_east),
    )


def x_slope(left, right):
    lane = lax.broadcasted_iota(jnp.int32, left.shape, 1)
    start, stop = lane == 0, lane == HALF - 1
    left_west, right_west = pltpu.roll(left, 1, 1), pltpu.roll(right, 1, 1)
    left_east, right_east = pltpu.roll(left, HALF - 1, 1), pltpu.roll(right, HALF - 1, 1)
    return (
        jnp.where(stop, right_east, left_east) - jnp.where(start, 0.0, left_west),
        jnp.where(stop, 0.0, right_east) - jnp.where(start, left_west, right_west),
    )


def beside_of(ref, plane):
    centre = [ref[plane, half, MID, :] for half in range(2)]
    pairs = x_pair(*centre)
    sums = [
        (ref[plane - 1, half, MID, :] + ref[plane + 1, half, MID, :])
        + (ref[plane, half, LOW, :] + ref[plane, half, HIGH, :])
        + pairs[half]
        for half in range(2)
    ]
    return centre, sums


def field_kernel(
    grid_rows,
    row_ref,
    below_ref,
    above_ref,
    south_ref,
    north_ref,
    acc_own_ref,
    acc_z_ref,
    density_own_ref,
    guess_own_ref,
    diverge_own_ref,
    fraction_ref,
    momentum_ref,
    residual_ref,
    direction_ref,
    mapped_ref,
    scaled_own_ref,
    twice_ref,
    high_ref,
    low_ref,
    north_edge_ref,
    south_edge_ref,
    high_face_ref,
    low_face_ref,
    north_face_ref,
    south_face_ref,
    dots_ref,
    scaled_ref,
    mobility_ref,
    diagonal_ref,
    first_ref,
    second_ref,
    mob_ref,
    guess_ref,
    wide_ref,
    density_ref,
    diverge_ref,
    rate_ref,
    lhs_ref,
    rhs_ref,
    load_sems,
):
    row_first = row_ref[0].astype(jnp.float32)
    loads = [
        pltpu.make_async_copy(acc_z_ref.at[:, 0:CZ], first_ref.at[:, 0:CZ, :, MID, :], load_sems.at[0]),
        pltpu.make_async_copy(
            acc_z_ref.at[:, CZ : 2 * CZ], first_ref.at[:, CZ + 2 : ZE, :, MID, :], load_sems.at[1]
        ),
        pltpu.make_async_copy(acc_own_ref, second_ref.at[:, 2:16, :, MID, :], load_sems.at[2]),
    ]
    for load in loads:
        load.start()
    for field in range(4):
        edge = jnp.zeros((ZE, 2, 8, HALF), jnp.float32)
        first_ref[field, :, :, 0 : MID.start, :] = edge
        first_ref[field, :, :, MID.stop : YE, :] = edge
        first_ref[field, CZ : CZ + 2, :, MID, :] = jnp.zeros((2, 2, 72, HALF), jnp.float32)
    gather_fields(
        south_ref,
        north_ref,
        below_ref,
        above_ref,
        (guess_own_ref, density_own_ref, diverge_own_ref),
        (guess_ref, density_ref, diverge_ref),
    )
    loads[0].wait()
    loads[1].wait()
    beside_y(row_first, grid_rows, south_ref, north_ref, first_ref, lhs_ref, rhs_ref)
    loads[2].wait()

    def add_own(plane, carry):
        for field in range(4):
            for half in range(2):
                first_ref[field, plane, half, MID, :] += second_ref[field, plane, half, MID, :]
        return carry

    lax.fori_loop(2, 16, add_own, 0)

    row = lax.broadcasted_iota(jnp.int32, (YE, HALF), 0).astype(jnp.float32) + (row_first - LEAD)
    lane = lax.broadcasted_iota(jnp.int32, (YE, HALF), 1)
    within = (row >= 0.0) & (row < grid_rows)
    inside = within.astype(jnp.float32)
    count_y = (row >= 1.0).astype(jnp.float32) + (row < grid_rows - 1.0).astype(jnp.float32)
    for half in range(2):
        count_x = 2.0 - (lane == (0, HALF - 1)[half]).astype(jnp.float32)
        rate_ref[half] = inside * (1.0 - smooth_rate * (2.0 + count_y + count_x))
    rate_ref[2] = inside * smooth_rate
    for index, reach in enumerate((2.0, 1.0, 0.0)):
        near = within & (row >= row_first - reach) & (row < row_first + (CY + reach))
        rate_ref[3 + index] = near.astype(jnp.float32)

    for sweep, (source, target) in enumerate(
        ((first_ref, second_ref), (second_ref, first_ref), (first_ref, second_ref))
    ):

        def sweep_plane(plane, fields, source=source, target=target):
            for field in fields:
                centre, sums = beside_of(source.at[field], plane)
                for half in range(2):
                    target[field, plane, half, MID, :] = (
                        rate_ref[half, MID, :] * centre[half] + rate_ref[2, MID, :] * sums[half]
                    )

        def sweep_step(plane, carry, sweep_plane=sweep_plane):
            sweep_plane(plane, (0, 1, 2, 3))
            return carry

        sweep_plane(sweep + 1, (0, 1))
        lax.fori_loop(sweep + 2, ZE - 2 - sweep, sweep_step, 0)
        sweep_plane(ZE - 2 - sweep, (0, 1))

    filtered = second_ref

    def mobility_step(plane, carry):
        known = rate_ref[3] > 0.5
        for half in range(2):
            fraction = 1.0 / (1.0 + filtered[0, plane + 3, half])
            mobility = jnp.where(known, fraction / density_ref[plane, half], 0.0)
            mob_ref[plane, half] = mobility
            wide_ref[plane, half] = mobility * guess_ref[plane, half]
        return carry

    lax.fori_loop(0, CZ + 4, mobility_step, 0)

    def output_step(plane, carry):
        for half in range(2):
            cut = slice(half * HALF, (half + 1) * HALF)
            fraction_ref[plane, :, cut] = 1.0 / (1.0 + filtered[0, plane + REACH, half, OWN, :])
            for part in range(3):
                momentum_ref[plane, part, :, cut] = filtered[part + 1, plane + REACH, half, OWN, :]
        return carry

    lax.fori_loop(0, CZ, output_step, 0)

    direct_ref, product_ref, remain_ref = first_ref.at[0], first_ref.at[1], first_ref.at[2]

    def first_residual(plane, carry):
        at = plane + 1
        near = rate_ref[4, MID, :] > 0.5
        mobility, beside_mobility = beside_of(mob_ref, at)
        guess, beside_guess = beside_of(guess_ref, at)
        unused, beside_wide = beside_of(wide_ref, at)
        slope = x_slope(filtered[3, at + 3, 0, MID, :], filtered[3, at + 3, 1, MID, :])
        for half in range(2):
            diagonal = (3.0 + stiffness) * mobility[half] + 0.5 * beside_mobility[half]
            operated = diagonal * guess[half] - 0.5 * (
                mobility[half] * beside_guess[half] + beside_wide[half]
            )
            spread = 0.5 * (filtered[1, at + 4, half, MID, :] - filtered[1, at + 2, half, MID, :])
            spread = spread + 0.5 * (
                filtered[2, at + 3, half, HIGH, :] - filtered[2, at + 3, half, LOW, :]
            )
            spread = spread + 0.5 * slope[half]
            residual = jnp.where(near, diverge_ref[plane, half, MID, :] - spread - operated, 0.0)
            direction = jnp.where(near, residual / diagonal, 0.0)
            remain_ref[plane, half, MID, :] = residual
            direct_ref[plane, half, MID, :] = direction
            product_ref[plane, half, MID, :] = direction * mobility[half]
            diagonal_ref[plane, half, MID, :] = diagonal
            mobility_ref[plane, half, MID, :] = mobility[half]
        return carry

    lax.fori_loop(0, CZ + 2, first_residual, 0)

    scaled_ref[...] = jnp.zeros_like(scaled_ref)
    again_ref = first_ref.at[3]
    for plane in (0, CZ + 1):
        again_ref[plane] = jnp.zeros((2, YE, HALF), jnp.float32)

    def map_step(plane, sums):
        at = plane + 1
        own = rate_ref[5, MID, :] > 0.5
        directions, beside_direction = beside_of(direct_ref, at)
        unused, beside_product = beside_of(product_ref, at)
        sum_rz, sum_dw, sum_uw = sums
        for half in range(2):
            residual = jnp.where(own, remain_ref[at, half, MID, :], 0.0)
            diagonal = diagonal_ref[at, half, MID, :]
            mapped = diagonal * directions[half] - 0.5 * (
                mobility_ref[at, half, MID, :] * beside_direction[half] + beside_product[half]
            )
            mapped = jnp.where(own, mapped, 0.0)
            scaled = jnp.where(own, mapped / diagonal, 0.0)
            scaled_ref[at, half, MID, :] = scaled
            again_ref[at, half, MID, :] = scaled * mobility_ref[at, half, MID, :]
            scaled_own_ref[plane, half] = scaled[4:68]
            residual_ref[plane, half] = residual[4:68]
            direction_ref[plane, half] = directions[half][4:68]
            mapped_ref[plane, half] = mapped[4:68]
            sum_rz = sum_rz + residual * directions[half]
            sum_dw = sum_dw + directions[half] * mapped
            sum_uw = sum_uw + scaled * mapped
        return sum_rz, sum_dw, sum_uw

    zero = jnp.zeros((72, HALF), jnp.float32)
    sums = lax.fori_loop(0, CZ, map_step, (zero, zero, zero))
    for index in range(3):
        dots_ref[index] = jnp.sum(sums[index])
    def again_step(plane, total):
        at = plane + 1
        centre, beside = beside_of(scaled_ref, at)
        unused, beside_again = beside_of(again_ref, at)
        for half in range(2):
            twice = diagonal_ref[at, half, MID, :] * centre[half] - 0.5 * (
                mobility_ref[at, half, MID, :] * beside[half] + beside_again[half]
            )
            twice_ref[plane, half] = twice[4:68]
            total = total + (centre[half] * twice)[4:68]
        return total

    total = lax.fori_loop(0, CZ, again_step, jnp.zeros((CY, HALF), jnp.float32))
    dots_ref[3] = jnp.sum(total)
    high_face_ref[...] = 0.5 * (mobility_ref[CZ, :, OWN, :] + mobility_ref[CZ + 1, :, OWN, :])
    low_face_ref[...] = 0.5 * (mobility_ref[1, :, OWN, :] + mobility_ref[0, :, OWN, :])
    for face_ref, inner in ((north_face_ref, LEAD + CY - 1), (south_face_ref, LEAD - 1)):
        for plane in range(CZ):
            for half in range(2):
                face_ref[plane, half : half + 1] = 0.5 * (
                    mobility_ref[plane + 1, half, inner : inner + 1, :]
                    + mobility_ref[plane + 1, half, inner + 1 : inner + 2, :]
                )
    high_ref[...] = scaled_ref[CZ, :, OWN, :]
    low_ref[...] = scaled_ref[1, :, OWN, :]
    for plane in range(CZ):
        for half in range(2):
            north_edge_ref[plane, half : half + 1] = scaled_ref[plane + 1, half, LEAD + CY - 1 : LEAD + CY, :]
            south_edge_ref[plane, half : half + 1] = scaled_ref[plane + 1, half, LEAD : LEAD + 1, :]


def second_kernel(dots_ref, *refs):
    received, own_edges, faces, sent_ref = refs[0:4], refs[4:8], refs[8:12], refs[12]
    missing = jnp.float32(0.0)
    for got_ref, own_ref, face_ref in zip(received, own_edges, faces):
        missing = missing + jnp.sum(got_ref[...] * own_ref[...] * face_ref[...])
    values = (dots_ref[0], dots_ref[1], dots_ref[2], dots_ref[3] - missing)
    column = lax.broadcasted_iota(jnp.int32, sent_ref.shape, 1)
    sent = jnp.zeros(sent_ref.shape, jnp.float32)
    for index, value in enumerate(values):
        sent = jnp.where(column == index, value, sent)
    sent_ref[...] = sent


def final_kernel(got_ref, guess_ref, residual_ref, direction_ref, mapped_ref, scaled_ref, twice_ref, below_ref, above_ref, south_ref, north_ref, low_face_ref, high_face_ref, south_face_ref, north_face_ref, pressure_ref, final_ref):
    sums = jnp.sum(got_ref[...], axis=0, keepdims=True)
    sum_rz, sum_dw, sum_uw, sum_uv = (sums[:, index : index + 1] for index in range(4))
    step = sum_rz / sum_dw
    next_rz = sum_rz - 2.0 * step * sum_dw + step * step * sum_uw
    along = 1.0 + next_rz / sum_rz
    curvature = along * along * sum_dw - 2.0 * step * along * sum_uw + step * step * sum_uv
    next_step = next_rz / curvature
    first = step + next_step * along
    last = next_step * step

    row = lax.broadcasted_iota(jnp.int32, (CY, HALF), 0)
    for plane in range(CZ):
        for half in range(2):
            cut = slice(half * HALF, (half + 1) * HALF)
            south = south_ref[plane, half : half + 1] * south_face_ref[plane, half : half + 1]
            north = north_ref[plane, half : half + 1] * north_face_ref[plane, half : half + 1]
            past = jnp.where(row == 0, south, 0.0) + jnp.where(row == CY - 1, north, 0.0)
            if plane == 0:
                past = past + below_ref[half] * low_face_ref[half]
            if plane == CZ - 1:
                past = past + above_ref[half] * high_face_ref[half]
            twice = twice_ref[plane, half] - past
            pressure_ref[plane, :, cut] = (
                guess_ref[plane, :, cut]
                + first * direction_ref[plane, half]
                - last * scaled_ref[plane, half]
            )
            final_ref[plane, :, cut] = (
                residual_ref[plane, half] - first * mapped_ref[plane, half] + last * twice
            )


def vmem_spec():
    return pl.BlockSpec(memory_space=pltpu.VMEM)


def smem_spec():
    return pl.BlockSpec(memory_space=pltpu.SMEM)


def f32(*shape):
    return jax.ShapeDtypeStruct(shape, jnp.float32)


def params():
    return pltpu.CompilerParams(vmem_limit_bytes=VMEM_LIMIT)


def hbm_spec():
    return pl.BlockSpec(memory_space=pltpu.HBM)


def deposit_scratch():
    return [
        pltpu.VMEM((4 * 14 * TALL, CHUNK), jnp.bfloat16),
        pltpu.VMEM((CX, CHUNK), jnp.bfloat16),
    ]


def on_device(
    parcel_cell,
    parcel_offset,
    parcel_volume,
    parcel_force,
    brick_counts,
    divergence,
    pressure_prev,
    gas_density,
):
    size_z = lax.axis_size("gz")
    size_y = lax.axis_size("gy")
    grid_rows = float(size_y * CY)
    row_first = (lax.axis_index("gy") * CY).astype(jnp.int32)[None]
    up_z = [(i, (i + 1) % size_z) for i in range(size_z)]
    down_z = [((i + 1) % size_z, i) for i in range(size_z)]
    up_y = [(i, i + 1) for i in range(size_y - 1)]
    down_y = [(i + 1, i) for i in range(size_y - 1)]

    message = f32(LIST + 5 * TILES, 8, CX)
    tiled = [values.reshape(CZ, TILES, 8, CX) for values in (pressure_prev, gas_density, divergence)]
    to_up, to_down, brick_rows = pl.pallas_call(
        sort_kernel,
        out_shape=(message, message, f32(6, CZ, 8, CX)),
        in_specs=[smem_spec()] + [hbm_spec()] * 7,
        out_specs=(vmem_spec(), vmem_spec(), vmem_spec()),
        scratch_shapes=[
            pltpu.VMEM((1, PCAP), jnp.int32),
            pltpu.VMEM((8, PCAP), jnp.float32),
            pltpu.VMEM((PCAP // 256 * CY, 256), jnp.bfloat16),
            pltpu.VMEM((PCAP // 256 * CY, 256), jnp.float32),
            pltpu.VMEM((1, PCAP), jnp.int32),
            pltpu.VMEM((384, 512), jnp.bfloat16),
            pltpu.VMEM((384, 256), jnp.float32),
            pltpu.SemaphoreType.DMA((20,)),
        ],
        compiler_params=pltpu.CompilerParams(vmem_limit_bytes=60 * 1024 * 1024),
        name="order",
    )(brick_counts, parcel_cell[None], parcel_offset, parcel_volume[None], parcel_force, *tiled)
    acc_own = pl.pallas_call(
        functools.partial(own_kernel, grid_rows),
        out_shape=f32(4, 14, 2, MID.stop - MID.start, HALF),
        in_specs=[smem_spec(), vmem_spec()],
        out_specs=vmem_spec(),
        scratch_shapes=deposit_scratch(),
        compiler_params=params(),
        cost_estimate=pl.CostEstimate(flops=8_000_000_000, bytes_accessed=8_000_000, transcendentals=0),
        name="own",
    )(row_first, to_up)
    below = lax.ppermute(to_up, "gz", up_z)
    above = lax.ppermute(to_down, "gz", down_z)
    edge_rows = f32(3 * LIST + 8, 8, CX)
    to_north, to_south = pl.pallas_call(
        pack_kernel,
        out_shape=(edge_rows, edge_rows),
        in_specs=[vmem_spec()] * 4,
        out_specs=(vmem_spec(), vmem_spec()),
        compiler_params=params(),
        name="pack",
    )(to_up, below, above, brick_rows)
    south = lax.ppermute(to_north, "gy", up_y)
    north = lax.ppermute(to_south, "gy", down_y)
    acc_z = pl.pallas_call(
        functools.partial(z_kernel, grid_rows),
        out_shape=f32(4, 2 * CZ, 2, MID.stop - MID.start, HALF),
        in_specs=[smem_spec()] + [vmem_spec()] * 2,
        out_specs=vmem_spec(),
        scratch_shapes=deposit_scratch(),
        compiler_params=params(),
        cost_estimate=pl.CostEstimate(flops=8_000_000_000, bytes_accessed=8_000_000, transcendentals=0),
        name="beside_z",
    )(row_first, below, above)
    halves = f32(CZ, 2, CY, HALF)
    face_z, face_y = f32(2, CY, HALF), f32(CZ, 2, HALF)
    (
        fraction, momentum, residual, direction, mapped, scaled, twice,
        high, low, north_edge, south_edge, high_face, low_face, north_face, south_face, dots,
    ) = pl.pallas_call(
        functools.partial(field_kernel, grid_rows),
        out_shape=(f32(CZ, CY, CX), f32(CZ, 3, CY, CX))
        + (halves,) * 5
        + (face_z, face_z, face_y, face_y) * 2
        + (f32(4),),
        in_specs=[smem_spec()] + [vmem_spec()] * 4 + [pl.BlockSpec(memory_space=pl.ANY)] * 2 + [vmem_spec()] * 3,
        out_specs=tuple([vmem_spec()] * 15 + [smem_spec()]),
        scratch_shapes=[pltpu.VMEM((CZ + 2, 2, YE, HALF), jnp.float32)] * 3
        + [
            pltpu.VMEM((4, ZE, 2, YE, HALF), jnp.float32),
            pltpu.VMEM((4, ZE, 2, YE, HALF), jnp.float32),
            pltpu.VMEM((CZ + 4, 2, YE, HALF), jnp.float32),
            pltpu.VMEM((CZ + 4, 2, YE, HALF), jnp.float32),
            pltpu.VMEM((CZ + 4, 2, YE, HALF), jnp.float32),
            pltpu.VMEM((CZ + 4, 2, YE, HALF), jnp.float32),
            pltpu.VMEM((CZ + 2, 2, YE, HALF), jnp.float32),
            pltpu.VMEM((6, YE, HALF), jnp.float32),
        ]
        + deposit_scratch()
        + [pltpu.SemaphoreType.DMA((3,))],
        compiler_params=params(),
        name="fields",
    )(row_first, below, above, south, north, acc_own, acc_z, gas_density, pressure_prev, divergence)

    scaled_below = lax.ppermute(high, "gz", up_z)
    scaled_above = lax.ppermute(low, "gz", down_z)
    scaled_south = lax.ppermute(north_edge, "gy", up_y)
    scaled_north = lax.ppermute(south_edge, "gy", down_y)
    every = size_z * size_y
    received = (scaled_below, scaled_above, scaled_south, scaled_north)
    faces = (low_face, high_face, south_face, north_face)
    sent = pl.pallas_call(
        second_kernel,
        out_shape=f32(every, 128),
        in_specs=[smem_spec()] + [vmem_spec()] * 12,
        out_specs=vmem_spec(),
        compiler_params=params(),
        name="second",
    )(dots, *received, low, high, south_edge, north_edge, *faces)
    got = lax.all_to_all(sent, ("gz", "gy"), 0, 0, tiled=True)
    pressure, final = pl.pallas_call(
        final_kernel,
        out_shape=(f32(CZ, CY, CX), f32(CZ, CY, CX)),
        in_specs=[vmem_spec()] * 15,
        out_specs=(vmem_spec(), vmem_spec()),
        compiler_params=params(),
        name="final",
    )(got, pressure_prev, residual, direction, mapped, scaled, twice, *received, *faces)
    return (fraction, momentum, pressure, final)


def solution(mesh):
    return jax.shard_map(
        on_device,
        mesh=mesh,
        in_specs=(
            P(("gz", "gy")),
            P(None, ("gz", "gy")),
            P(("gz", "gy")),
            P(None, ("gz", "gy")),
            P("gz", "gy"),
            P("gz", "gy", None),
            P("gz", "gy", None),
            P("gz", "gy", None),
        ),
        out_specs=(
            P("gz", "gy", None),
            P("gz", None, "gy", None),
            P("gz", "gy", None),
            P("gz", "gy", None),
        ),
        check_vma=False,
    )
```

```python
import functools

import jax
import jax.numpy as jnp
from jax import lax
from jax.experimental import pallas as pl
from jax.experimental.pallas import tpu as pltpu
from jax.sharding import PartitionSpec as P

CZ = 8
CY = 64
CX = 256
PCAP = 4096
ITERS = 2
REACH = 5
ZE = CZ + 2 * REACH
YE = 88
LEAD = 12
LIST = PCAP // 256
TILES = CY // 8
HALF = 128
CHUNK = 256
TALL = 16

smooth_rate = 0.15
stiffness = 0.002

VMEM_LIMIT = 36 * 1024 * 1024


def chunk_values(parcels, grid_rows, row_first, shift_y):
    cell = parcels[0:1].astype(jnp.int32)
    home_z = lax.shift_right_logical(cell, 14)
    home_y = lax.shift_right_logical(cell, 8) & 63
    home_x = cell & 255
    count = parcels.shape[1]
    taps = lax.broadcasted_iota(jnp.int32, (8, count), 0).astype(jnp.float32) - 3.0

    def tap_table(offset, inside):
        distance = taps + 0.5 - offset
        weight = jnp.where(inside, jnp.exp(-0.5 * distance * distance), 0.0)
        return weight * (1.0 / jnp.sum(weight, axis=0, keepdims=True))

    seven = taps < 3.5
    place_y = taps + (home_y.astype(jnp.float32) + (row_first + shift_y))
    place_x = taps + home_x.astype(jnp.float32)
    table_z = tap_table(parcels[1:2], seven)
    table_y = tap_table(parcels[2:3], seven & (place_y >= 0.0) & (place_y < grid_rows))
    table_x = tap_table(parcels[3:4], seven & (place_x >= 0.0) & (place_x < float(CX)))
    return home_z, home_y, home_x, table_z, table_y, table_x


def axis_rows(rows, first, home, table, least=None):
    count = home.shape[1]
    lane_row = lax.broadcasted_iota(jnp.int32, (8, count), 0)
    tap_base = lane_row - (home - 3)
    tiles = []
    for tile in range(rows // 8):
        at = first + 8 * tile
        tap = tap_base + at
        fits = (tap & -8) == 0
        if least is not None:
            fits = fits & (lane_row >= least - at)
        tiles.append(jnp.take_along_axis(table, jnp.where(fits, tap, 7), axis=0))
    return tiles[0] if len(tiles) == 1 else jnp.concatenate(tiles, axis=0)


def row_of(cell):
    return lax.shift_right_logical(cell.astype(jnp.int32), 8) & 63


def count_where(condition):
    return jnp.sum(condition.astype(jnp.float32)).astype(jnp.int32)


def deposit(parcels_ref, base, row_first, grid_rows, shift_z, shift_y, planes, plane_first, window, lead, acc_first, acc_ref, lhs_ref, rhs_ref):
    rows = TALL if window is None else 8
    volume = parcels_ref[base : base + LIST, 4, :]
    begin = 0
    if shift_y == 0:
        total = count_where(volume != 0.0)
    else:
        home_row = row_of(parcels_ref[base : base + LIST, 0, :])
        if shift_y < 0:
            total = count_where(volume != 0.0)
            begin = lax.shift_right_logical(
                count_where((volume != 0.0) & (home_row < CY - 3 - REACH)), CHUNK.bit_length() - 1
            )
        else:
            total = count_where((volume != 0.0) & (home_row < 3 + REACH))

    def chunk_step(index, carry):
        start = index * CHUNK
        parcels = parcels_ref[base + index]
        home_z, home_y, home_x, table_z, table_y, table_x = chunk_values(
            parcels, grid_rows, row_first, float(shift_y)
        )
        block = 64
        for part in range(CX // block):
            weight_x = axis_rows(block, part * block, home_x, table_x)
            rhs_ref[part * block : (part + 1) * block, :] = weight_x.astype(jnp.bfloat16)
        rows_z = -(-planes // 8) * 8
        weight_z = axis_rows(rows_z, plane_first - REACH - shift_z, home_z, table_z)
        loaded = [
            weight_z * (parcels[4:5] if field == 0 else parcels[4:5] * parcels[4 + field : 5 + field])
            for field in range(4)
        ]

        def spread_window(first, least):
            weight_y = axis_rows(
                rows, first - (lead + shift_y), home_y, table_y,
                None if least is None else least - lead,
            )
            for field in range(4):
                for pair in range(planes // 2):
                    both = jnp.concatenate(
                        [
                            loaded[field][2 * pair : 2 * pair + 1] * weight_y,
                            loaded[field][2 * pair + 1 : 2 * pair + 2] * weight_y,
                        ],
                        axis=0,
                    )
                    at = (field * planes + 2 * pair) * rows
                    lhs_ref[at : at + 2 * rows, :] = both.astype(jnp.bfloat16)

        def add_window(first):
            for field in range(4):
                product = lax.dot_general(
                    lhs_ref[field * planes * rows : (field + 1) * planes * rows, :],
                    rhs_ref[...],
                    (((1,), (1,)), ((), ())),
                    preferred_element_type=jnp.float32,
                )
                for plane in range(planes):
                    for half in range(2):
                        acc_ref[field, plane_first - acc_first + plane, half, pl.ds(first, rows), :] += product[
                            plane * rows : (plane + 1) * rows, half * HALF : (half + 1) * HALF
                        ]

        if window is not None:
            spread_window(window, None)
            add_window(window)
            return carry

        slot = lax.broadcasted_iota(jnp.int32, (1, CHUNK), 1) + start
        row_home = home_y.astype(jnp.float32)
        lowest = jnp.min(jnp.where(slot < total, row_home, float(CY))).astype(jnp.int32)
        highest = jnp.max(jnp.where(slot < total, row_home, 0.0)).astype(jnp.int32)
        row_low = lowest + (lead - 3)
        row_high = highest + (lead + 4)

        def window_step(carried):
            logical = carried
            first = jnp.minimum(logical, acc_ref.shape[3] - TALL)
            spread_window(first, logical)
            add_window(first)
            return logical + TALL

        lax.while_loop(lambda carried: carried < row_high, window_step, row_low)
        return carry

    end = lax.shift_right_logical(total + (CHUNK - 1), CHUNK.bit_length() - 1)
    lax.fori_loop(begin, end, chunk_step, 0)


def sort_kernel(count_ref, cell_ref, offset_ref, volume_ref, force_ref, guess_ref, density_ref, diverge_ref, up_ref, down_ref, rows_ref, cell_held_ref, data_ref, hot_ref, prefix_ref, dest_ref, lhs_ref, total_ref, sems):
    lists = [
        pltpu.make_async_copy(cell_ref, cell_held_ref, sems.at[0]),
        pltpu.make_async_copy(offset_ref, data_ref.at[1:4], sems.at[1]),
        pltpu.make_async_copy(volume_ref, data_ref.at[4:5], sems.at[2]),
        pltpu.make_async_copy(force_ref, data_ref.at[5:8], sems.at[3]),
    ]
    edges = []
    for out_ref, upper in ((up_ref, True), (down_ref, False)):
        at = LIST
        for source, depth in ((guess_ref, 2), (density_ref, 2), (diverge_ref, 1)):
            for plane in range(depth):
                edges.append(
                    pltpu.make_async_copy(
                        source.at[CZ - depth + plane if upper else plane],
                        out_ref.at[at : at + TILES],
                        sems.at[4 + len(edges)],
                    )
                )
                at += TILES
    for part, source in enumerate((guess_ref, density_ref, diverge_ref)):
        for side in range(2):
            edges.append(
                pltpu.make_async_copy(
                    source.at[:, side * (TILES - 1)], rows_ref.at[2 * part + side], sems.at[4 + len(edges)]
                )
            )
    for copy in lists + edges:
        copy.start()
    for copy in lists:
        copy.wait()
    data_ref[0:1, :] = cell_held_ref[...].astype(jnp.float32)
    live_count = count_ref[0, 0]
    block = 256
    blocks = PCAP // block
    bins = lax.broadcasted_iota(jnp.int32, (CY, block), 0)
    slots = lax.broadcasted_iota(jnp.int32, (1, block), 1)

    def hot_of(index):
        cut = slice(index * block, (index + 1) * block)
        home_row = lax.shift_right_logical(cell_held_ref[:, cut], 8) & 63
        return (bins == home_row) & (slots + index * block < live_count)

    for index in range(blocks):
        hot_ref[index * CY : (index + 1) * CY, :] = hot_of(index).astype(jnp.float32).astype(jnp.bfloat16)
    before = lax.broadcasted_iota(jnp.int32, (block, block), 0)
    after = lax.broadcasted_iota(jnp.int32, (block, block), 1)
    upto = (before <= after).astype(jnp.float32).astype(jnp.bfloat16)
    prefix_ref[...] = jnp.dot(hot_ref[...], upto, preferred_element_type=jnp.float32)
    carry = jnp.zeros((CY, 1), jnp.float32)
    carries = []
    for index in range(blocks):
        carries.append(carry)
        carry = carry + prefix_ref[index * CY : (index + 1) * CY, block - 1 : block]
    total = jnp.broadcast_to(carry, (CY, 128))
    row = lax.broadcasted_iota(jnp.int32, (CY, 128), 0)
    summed = total
    for shift in (1, 2, 4, 8, 16, 32):
        summed = summed + jnp.where(row >= shift, pltpu.roll(summed, shift, 0), 0.0)
    first = (summed - total)[:, 0:1]
    for index in range(blocks):
        cut = slice(index * block, (index + 1) * block)
        place = prefix_ref[index * CY : (index + 1) * CY, :] + (first + carries[index])
        hot = hot_of(index)
        dest = jnp.sum(jnp.where(hot, place, 0.0), axis=0, keepdims=True) - 1.0
        dest_ref[:, cut] = dest.astype(jnp.int32)

    total_ref[...] = jnp.zeros_like(total_ref)
    width = 512

    def route(index, unused):
        start = pl.multiple_of(index * width, width)
        dest = dest_ref[:, pl.ds(start, width)]
        high = lax.shift_right_arithmetic(dest, 8)
        low = dest & 255
        data = data_ref[:, pl.ds(start, width)]
        top = data.astype(jnp.bfloat16).astype(jnp.float32)
        rest = data - top
        middle = rest.astype(jnp.bfloat16).astype(jnp.float32)
        lanes = lax.broadcasted_iota(jnp.int32, (256, width), 0)
        rhs = (lanes == low).astype(jnp.float32).astype(jnp.bfloat16)
        wide = jnp.broadcast_to(high, (8, width))
        for split, values in enumerate((top, middle, rest - middle)):
            for pair in range(8):
                both = jnp.concatenate(
                    [
                        jnp.where(wide == 2 * pair, values, 0.0),
                        jnp.where(wide == 2 * pair + 1, values, 0.0),
                    ],
                    axis=0,
                )
                at = split * 128 + pair * 16
                lhs_ref[at : at + 16, :] = both.astype(jnp.bfloat16)
        total_ref[...] += lax.dot_general(
            lhs_ref[...], rhs, (((1,), (1,)), ((), ())), preferred_element_type=jnp.float32
        )
        return unused

    steps = lax.shift_right_logical(live_count + (width - 1), 9)
    lax.fori_loop(0, steps, route, 0)
    for part in range(LIST):
        at = part * 8
        sorted_part = (
            total_ref[at : at + 8, :] + total_ref[128 + at : 136 + at, :]
        ) + total_ref[256 + at : 264 + at, :]
        up_ref[part] = sorted_part
        down_ref[part] = sorted_part
    for copy in edges:
        copy.wait()


FIELDS = ((2, 2), (2, 2), (1, 1))


def pack_kernel(sorted_ref, below_ref, above_ref, edge_ref, north_ref, south_ref):
    for out_ref in (north_ref, south_ref):
        for index, source in enumerate((sorted_ref, below_ref, above_ref)):
            out_ref[index * LIST : (index + 1) * LIST] = source[0:LIST]
        out_ref[3 * LIST + 7, 2:8, :] = jnp.zeros((6, CX), jnp.float32)
    for side, out_ref in ((1, north_ref), (0, south_ref)):
        slot = 0
        for part, (depth, wide) in enumerate(FIELDS):
            first = (0, 2, 4)[part]
            rows = slice(8 - wide, 8) if side else slice(0, wide)
            for plane in range(CZ + 2 * depth):
                if depth <= plane < CZ + depth:
                    values = edge_ref[2 * part + side, plane - depth, rows, :]
                else:
                    ref, inner = (below_ref, plane) if plane < depth else (above_ref, plane - CZ - depth)
                    values = ref[LIST + (first + inner) * TILES + side * (TILES - 1), rows, :]
                out_ref[3 * LIST + slot // 8, slot % 8 : slot % 8 + wide, :] = values
                slot += wide


def middle_deposit(list_ref, row_first, grid_rows, shift_z, planes, plane_first, acc_first, acc_ref, lhs_ref, rhs_ref):
    deposit(
        list_ref, 0, row_first, grid_rows, shift_z, 0, planes, plane_first, None, LEAD - MID.start,
        acc_first, acc_ref, lhs_ref, rhs_ref,
    )


def own_kernel(grid_rows, row_ref, parcels_ref, acc_ref, lhs_ref, rhs_ref):
    row_first = row_ref[0].astype(jnp.float32)
    acc_ref[...] = jnp.zeros_like(acc_ref)
    middle_deposit(parcels_ref, row_first, grid_rows, 0, 14, 2, 2, acc_ref, lhs_ref, rhs_ref)


def z_kernel(grid_rows, row_ref, below_ref, above_ref, acc_ref, lhs_ref, rhs_ref):
    row_first = row_ref[0].astype(jnp.float32)
    acc_ref[...] = jnp.zeros_like(acc_ref)
    middle_deposit(below_ref, row_first, grid_rows, -CZ, 8, 0, 0, acc_ref, lhs_ref, rhs_ref)
    middle_deposit(above_ref, row_first, grid_rows, CZ, 8, 10, 2, acc_ref, lhs_ref, rhs_ref)


def gather_fields(south_ref, north_ref, below_ref, above_ref, sources, targets):
    slot = 0
    for part, (own_ref, out_ref, (depth, wide)) in enumerate(zip(sources, targets, FIELDS)):
        first = (0, 2, 4)[part]
        for plane in range(CZ + 2 * depth):
            for half in range(2):
                cut = slice(half * HALF, (half + 1) * HALF)
                if depth <= plane < CZ + depth:
                    out_ref[plane, half, OWN, :] = own_ref[plane - depth, :, cut]
                else:
                    ref, inner = (below_ref, plane) if plane < depth else (above_ref, plane - CZ - depth)
                    at = LIST + (first + inner) * TILES
                    for tile in range(TILES):
                        out_ref[plane, half, LEAD + 8 * tile : LEAD + 8 * tile + 8, :] = ref[at + tile, :, cut]
                edge = 3 * LIST + slot // 8
                inner_rows = slice(slot % 8, slot % 8 + wide)
                out_ref[plane, half, LEAD - wide : LEAD, :] = south_ref[edge, inner_rows, cut]
                out_ref[plane, half, LEAD + CY : LEAD + CY + wide, :] = north_ref[edge, inner_rows, cut]
            slot += wide


def beside_y(row_first, grid_rows, south_ref, north_ref, acc_ref, lhs_ref, rhs_ref):
    for parcels_ref, shift_y, window in (
        (south_ref, -CY, LEAD - REACH),
        (north_ref, CY, LEAD + CY - 3),
    ):
        for part, (shift_z, planes, plane_first) in enumerate(((0, 14, 2), (-CZ, 8, 0), (CZ, 8, 10))):
            deposit(
                parcels_ref, LIST * part, row_first, grid_rows, shift_z, shift_y, planes, plane_first,
                window, LEAD, 0, acc_ref, lhs_ref, rhs_ref,
            )


MID = slice(8, 80)
LOW = slice(7, 79)
HIGH = slice(9, 81)
OWN = slice(LEAD, LEAD + CY)


def x_pair(left, right):
    lane = lax.broadcasted_iota(jnp.int32, left.shape, 1)
    start, stop = lane == 0, lane == HALF - 1
    left_west, right_west = pltpu.roll(left, 1, 1), pltpu.roll(right, 1, 1)
    left_east, right_east = pltpu.roll(left, HALF - 1, 1), pltpu.roll(right, HALF - 1, 1)
    return (
        jnp.where(start, 0.0, left_west) + jnp.where(stop, right_east, left_east),
        jnp.where(start, left_west, right_west) + jnp.where(stop, 0.0, right_east),
    )


def x_slope(left, right):
    lane = lax.broadcasted_iota(jnp.int32, left.shape, 1)
    start, stop = lane == 0, lane == HALF - 1
    left_west, right_west = pltpu.roll(left, 1, 1), pltpu.roll(right, 1, 1)
    left_east, right_east = pltpu.roll(left, HALF - 1, 1), pltpu.roll(right, HALF - 1, 1)
    return (
        jnp.where(stop, right_east, left_east) - jnp.where(start, 0.0, left_west),
        jnp.where(stop, 0.0, right_east) - jnp.where(start, left_west, right_west),
    )


def beside_of(ref, plane):
    centre = [ref[plane, half, MID, :] for half in range(2)]
    pairs = x_pair(*centre)
    sums = [
        (ref[plane - 1, half, MID, :] + ref[plane + 1, half, MID, :])
        + (ref[plane, half, LOW, :] + ref[plane, half, HIGH, :])
        + pairs[half]
        for half in range(2)
    ]
    return centre, sums


def field_kernel(
    grid_rows,
    row_ref,
    below_ref,
    above_ref,
    south_ref,
    north_ref,
    acc_own_ref,
    acc_z_ref,
    density_own_ref,
    guess_own_ref,
    diverge_own_ref,
    fraction_ref,
    momentum_ref,
    residual_ref,
    direction_ref,
    mapped_ref,
    scaled_own_ref,
    twice_ref,
    high_ref,
    low_ref,
    north_edge_ref,
    south_edge_ref,
    high_face_ref,
    low_face_ref,
    north_face_ref,
    south_face_ref,
    dots_ref,
    scaled_ref,
    mobility_ref,
    diagonal_ref,
    first_ref,
    second_ref,
    mob_ref,
    guess_ref,
    wide_ref,
    density_ref,
    diverge_ref,
    rate_ref,
    lhs_ref,
    rhs_ref,
    load_sems,
):
    row_first = row_ref[0].astype(jnp.float32)
    loads = [
        pltpu.make_async_copy(acc_z_ref.at[:, 0:CZ], first_ref.at[:, 0:CZ, :, MID, :], load_sems.at[0]),
        pltpu.make_async_copy(
            acc_z_ref.at[:, CZ : 2 * CZ], first_ref.at[:, CZ + 2 : ZE, :, MID, :], load_sems.at[1]
        ),
        pltpu.make_async_copy(acc_own_ref, second_ref.at[:, 2:16, :, MID, :], load_sems.at[2]),
    ]
    for load in loads:
        load.start()
    for field in range(4):
        edge = jnp.zeros((ZE, 2, 8, HALF), jnp.float32)
        first_ref[field, :, :, 0 : MID.start, :] = edge
        first_ref[field, :, :, MID.stop : YE, :] = edge
        first_ref[field, CZ : CZ + 2, :, MID, :] = jnp.zeros((2, 2, 72, HALF), jnp.float32)
    gather_fields(
        south_ref,
        north_ref,
        below_ref,
        above_ref,
        (guess_own_ref, density_own_ref, diverge_own_ref),
        (guess_ref, density_ref, diverge_ref),
    )
    loads[0].wait()
    loads[1].wait()
    beside_y(row_first, grid_rows, south_ref, north_ref, first_ref, lhs_ref, rhs_ref)
    loads[2].wait()

    def add_own(plane, carry):
        for field in range(4):
            for half in range(2):
                first_ref[field, plane, half, MID, :] += second_ref[field, plane, half, MID, :]
        return carry

    lax.fori_loop(2, 16, add_own, 0)

    row = lax.broadcasted_iota(jnp.int32, (YE, HALF), 0).astype(jnp.float32) + (row_first - LEAD)
    lane = lax.broadcasted_iota(jnp.int32, (YE, HALF), 1)
    within = (row >= 0.0) & (row < grid_rows)
    inside = within.astype(jnp.float32)
    count_y = (row >= 1.0).astype(jnp.float32) + (row < grid_rows - 1.0).astype(jnp.float32)
    for half in range(2):
        count_x = 2.0 - (lane == (0, HALF - 1)[half]).astype(jnp.float32)
        rate_ref[half] = inside * (1.0 - smooth_rate * (2.0 + count_y + count_x))
    rate_ref[2] = inside * smooth_rate
    for index, reach in enumerate((2.0, 1.0, 0.0)):
        near = within & (row >= row_first - reach) & (row < row_first + (CY + reach))
        rate_ref[3 + index] = near.astype(jnp.float32)

    for sweep, (source, target) in enumerate(
        ((first_ref, second_ref), (second_ref, first_ref), (first_ref, second_ref))
    ):

        def sweep_plane(plane, fields, source=source, target=target):
            for field in fields:
                centre, sums = beside_of(source.at[field], plane)
                for half in range(2):
                    target[field, plane, half, MID, :] = (
                        rate_ref[half, MID, :] * centre[half] + rate_ref[2, MID, :] * sums[half]
                    )

        def sweep_step(plane, carry, sweep_plane=sweep_plane):
            sweep_plane(plane, (0, 1, 2, 3))
            return carry

        sweep_plane(sweep + 1, (0, 1))
        lax.fori_loop(sweep + 2, ZE - 2 - sweep, sweep_step, 0, unroll=2)
        sweep_plane(ZE - 2 - sweep, (0, 1))

    filtered = second_ref

    def mobility_step(plane, carry):
        known = rate_ref[3] > 0.5
        for half in range(2):
            fraction = 1.0 / (1.0 + filtered[0, plane + 3, half])
            mobility = jnp.where(known, fraction / density_ref[plane, half], 0.0)
            mob_ref[plane, half] = mobility
            wide_ref[plane, half] = mobility * guess_ref[plane, half]
        return carry

    lax.fori_loop(0, CZ + 4, mobility_step, 0)

    def output_step(plane, carry):
        for half in range(2):
            cut = slice(half * HALF, (half + 1) * HALF)
            fraction_ref[plane, :, cut] = 1.0 / (1.0 + filtered[0, plane + REACH, half, OWN, :])
            for part in range(3):
                momentum_ref[plane, part, :, cut] = filtered[part + 1, plane + REACH, half, OWN, :]
        return carry

    lax.fori_loop(0, CZ, output_step, 0)

    direct_ref, product_ref, remain_ref = first_ref.at[0], first_ref.at[1], first_ref.at[2]

    def first_residual(plane, carry):
        at = plane + 1
        near = rate_ref[4, MID, :] > 0.5
        mobility, beside_mobility = beside_of(mob_ref, at)
        guess, beside_guess = beside_of(guess_ref, at)
        unused, beside_wide = beside_of(wide_ref, at)
        slope = x_slope(filtered[3, at + 3, 0, MID, :], filtered[3, at + 3, 1, MID, :])
        for half in range(2):
            diagonal = (3.0 + stiffness) * mobility[half] + 0.5 * beside_mobility[half]
            operated = diagonal * guess[half] - 0.5 * (
                mobility[half] * beside_guess[half] + beside_wide[half]
            )
            spread = 0.5 * (filtered[1, at + 4, half, MID, :] - filtered[1, at + 2, half, MID, :])
            spread = spread + 0.5 * (
                filtered[2, at + 3, half, HIGH, :] - filtered[2, at + 3, half, LOW, :]
            )
            spread = spread + 0.5 * slope[half]
            residual = jnp.where(near, diverge_ref[plane, half, MID, :] - spread - operated, 0.0)
            direction = jnp.where(near, residual / diagonal, 0.0)
            remain_ref[plane, half, MID, :] = residual
            direct_ref[plane, half, MID, :] = direction
            product_ref[plane, half, MID, :] = direction * mobility[half]
            diagonal_ref[plane, half, MID, :] = diagonal
            mobility_ref[plane, half, MID, :] = mobility[half]
        return carry

    lax.fori_loop(0, CZ + 2, first_residual, 0)

    scaled_ref[...] = jnp.zeros_like(scaled_ref)
    again_ref = first_ref.at[3]
    for plane in (0, CZ + 1):
        again_ref[plane] = jnp.zeros((2, YE, HALF), jnp.float32)

    def map_step(plane, sums):
        at = plane + 1
        own = rate_ref[5, MID, :] > 0.5
        directions, beside_direction = beside_of(direct_ref, at)
        unused, beside_product = beside_of(product_ref, at)
        sum_rz, sum_dw, sum_uw = sums
        for half in range(2):
            residual = jnp.where(own, remain_ref[at, half, MID, :], 0.0)
            diagonal = diagonal_ref[at, half, MID, :]
            mapped = diagonal * directions[half] - 0.5 * (
                mobility_ref[at, half, MID, :] * beside_direction[half] + beside_product[half]
            )
            mapped = jnp.where(own, mapped, 0.0)
            scaled = jnp.where(own, mapped / diagonal, 0.0)
            scaled_ref[at, half, MID, :] = scaled
            again_ref[at, half, MID, :] = scaled * mobility_ref[at, half, MID, :]
            scaled_own_ref[plane, half] = scaled[4:68]
            residual_ref[plane, half] = residual[4:68]
            direction_ref[plane, half] = directions[half][4:68]
            mapped_ref[plane, half] = mapped[4:68]
            sum_rz = sum_rz + residual * directions[half]
            sum_dw = sum_dw + directions[half] * mapped
            sum_uw = sum_uw + scaled * mapped
        return sum_rz, sum_dw, sum_uw

    zero = jnp.zeros((72, HALF), jnp.float32)
    sums = lax.fori_loop(0, CZ, map_step, (zero, zero, zero))
    for index in range(3):
        dots_ref[index] = jnp.sum(sums[index])
    def again_step(plane, total):
        at = plane + 1
        centre, beside = beside_of(scaled_ref, at)
        unused, beside_again = beside_of(again_ref, at)
        for half in range(2):
            twice = diagonal_ref[at, half, MID, :] * centre[half] - 0.5 * (
                mobility_ref[at, half, MID, :] * beside[half] + beside_again[half]
            )
            twice_ref[plane, half] = twice[4:68]
            total = total + (centre[half] * twice)[4:68]
        return total

    total = lax.fori_loop(0, CZ, again_step, jnp.zeros((CY, HALF), jnp.float32))
    dots_ref[3] = jnp.sum(total)
    high_face_ref[...] = 0.5 * (mobility_ref[CZ, :, OWN, :] + mobility_ref[CZ + 1, :, OWN, :])
    low_face_ref[...] = 0.5 * (mobility_ref[1, :, OWN, :] + mobility_ref[0, :, OWN, :])
    for face_ref, inner in ((north_face_ref, LEAD + CY - 1), (south_face_ref, LEAD - 1)):
        for plane in range(CZ):
            for half in range(2):
                face_ref[plane, half : half + 1] = 0.5 * (
                    mobility_ref[plane + 1, half, inner : inner + 1, :]
                    + mobility_ref[plane + 1, half, inner + 1 : inner + 2, :]
                )
    high_ref[...] = scaled_ref[CZ, :, OWN, :]
    low_ref[...] = scaled_ref[1, :, OWN, :]
    for plane in range(CZ):
        for half in range(2):
            north_edge_ref[plane, half : half + 1] = scaled_ref[plane + 1, half, LEAD + CY - 1 : LEAD + CY, :]
            south_edge_ref[plane, half : half + 1] = scaled_ref[plane + 1, half, LEAD : LEAD + 1, :]


def second_kernel(dots_ref, *refs):
    received, own_edges, faces, sent_ref = refs[0:4], refs[4:8], refs[8:12], refs[12]
    missing = jnp.float32(0.0)
    for got_ref, own_ref, face_ref in zip(received, own_edges, faces):
        missing = missing + jnp.sum(got_ref[...] * own_ref[...] * face_ref[...])
    values = (dots_ref[0], dots_ref[1], dots_ref[2], dots_ref[3] - missing)
    column = lax.broadcasted_iota(jnp.int32, sent_ref.shape, 1)
    sent = jnp.zeros(sent_ref.shape, jnp.float32)
    for index, value in enumerate(values):
        sent = jnp.where(column == index, value, sent)
    sent_ref[...] = sent


def final_kernel(got_ref, guess_ref, residual_ref, direction_ref, mapped_ref, scaled_ref, twice_ref, below_ref, above_ref, south_ref, north_ref, low_face_ref, high_face_ref, south_face_ref, north_face_ref, pressure_ref, final_ref):
    sums = jnp.sum(got_ref[...], axis=0, keepdims=True)
    sum_rz, sum_dw, sum_uw, sum_uv = (sums[:, index : index + 1] for index in range(4))
    step = sum_rz / sum_dw
    next_rz = sum_rz - 2.0 * step * sum_dw + step * step * sum_uw
    along = 1.0 + next_rz / sum_rz
    curvature = along * along * sum_dw - 2.0 * step * along * sum_uw + step * step * sum_uv
    next_step = next_rz / curvature
    first = step + next_step * along
    last = next_step * step

    row = lax.broadcasted_iota(jnp.int32, (CY, HALF), 0)
    for plane in range(CZ):
        for half in range(2):
            cut = slice(half * HALF, (half + 1) * HALF)
            south = south_ref[plane, half : half + 1] * south_face_ref[plane, half : half + 1]
            north = north_ref[plane, half : half + 1] * north_face_ref[plane, half : half + 1]
            past = jnp.where(row == 0, south, 0.0) + jnp.where(row == CY - 1, north, 0.0)
            if plane == 0:
                past = past + below_ref[half] * low_face_ref[half]
            if plane == CZ - 1:
                past = past + above_ref[half] * high_face_ref[half]
            twice = twice_ref[plane, half] - past
            pressure_ref[plane, :, cut] = (
                guess_ref[plane, :, cut]
                + first * direction_ref[plane, half]
                - last * scaled_ref[plane, half]
            )
            final_ref[plane, :, cut] = (
                residual_ref[plane, half] - first * mapped_ref[plane, half] + last * twice
            )


def vmem_spec():
    return pl.BlockSpec(memory_space=pltpu.VMEM)


def smem_spec():
    return pl.BlockSpec(memory_space=pltpu.SMEM)


def f32(*shape):
    return jax.ShapeDtypeStruct(shape, jnp.float32)


def params():
    return pltpu.CompilerParams(vmem_limit_bytes=VMEM_LIMIT)


def hbm_spec():
    return pl.BlockSpec(memory_space=pltpu.HBM)


def deposit_scratch():
    return [
        pltpu.VMEM((4 * 14 * TALL, CHUNK), jnp.bfloat16),
        pltpu.VMEM((CX, CHUNK), jnp.bfloat16),
    ]


def on_device(
    parcel_cell,
    parcel_offset,
    parcel_volume,
    parcel_force,
    brick_counts,
    divergence,
    pressure_prev,
    gas_density,
):
    size_z = lax.axis_size("gz")
    size_y = lax.axis_size("gy")
    grid_rows = float(size_y * CY)
    row_first = (lax.axis_index("gy") * CY).astype(jnp.int32)[None]
    up_z = [(i, (i + 1) % size_z) for i in range(size_z)]
    down_z = [((i + 1) % size_z, i) for i in range(size_z)]
    up_y = [(i, i + 1) for i in range(size_y - 1)]
    down_y = [(i + 1, i) for i in range(size_y - 1)]

    message = f32(LIST + 5 * TILES, 8, CX)
    tiled = [values.reshape(CZ, TILES, 8, CX) for values in (pressure_prev, gas_density, divergence)]
    to_up, to_down, brick_rows = pl.pallas_call(
        sort_kernel,
        out_shape=(message, message, f32(6, CZ, 8, CX)),
        in_specs=[smem_spec()] + [hbm_spec()] * 7,
        out_specs=(vmem_spec(), vmem_spec(), vmem_spec()),
        scratch_shapes=[
            pltpu.VMEM((1, PCAP), jnp.int32),
            pltpu.VMEM((8, PCAP), jnp.float32),
            pltpu.VMEM((PCAP // 256 * CY, 256), jnp.bfloat16),
            pltpu.VMEM((PCAP // 256 * CY, 256), jnp.float32),
            pltpu.VMEM((1, PCAP), jnp.int32),
            pltpu.VMEM((384, 512), jnp.bfloat16),
            pltpu.VMEM((384, 256), jnp.float32),
            pltpu.SemaphoreType.DMA((20,)),
        ],
        compiler_params=pltpu.CompilerParams(vmem_limit_bytes=60 * 1024 * 1024),
        name="order",
    )(brick_counts, parcel_cell[None], parcel_offset, parcel_volume[None], parcel_force, *tiled)
    acc_own = pl.pallas_call(
        functools.partial(own_kernel, grid_rows),
        out_shape=f32(4, 14, 2, MID.stop - MID.start, HALF),
        in_specs=[smem_spec(), vmem_spec()],
        out_specs=vmem_spec(),
        scratch_shapes=deposit_scratch(),
        compiler_params=params(),
        cost_estimate=pl.CostEstimate(flops=8_000_000_000, bytes_accessed=8_000_000, transcendentals=0),
        name="own",
    )(row_first, to_up)
    below = lax.ppermute(to_up, "gz", up_z)
    above = lax.ppermute(to_down, "gz", down_z)
    edge_rows = f32(3 * LIST + 8, 8, CX)
    to_north, to_south = pl.pallas_call(
        pack_kernel,
        out_shape=(edge_rows, edge_rows),
        in_specs=[vmem_spec()] * 4,
        out_specs=(vmem_spec(), vmem_spec()),
        compiler_params=params(),
        name="pack",
    )(to_up, below, above, brick_rows)
    south = lax.ppermute(to_north, "gy", up_y)
    north = lax.ppermute(to_south, "gy", down_y)
    acc_z = pl.pallas_call(
        functools.partial(z_kernel, grid_rows),
        out_shape=f32(4, 2 * CZ, 2, MID.stop - MID.start, HALF),
        in_specs=[smem_spec()] + [vmem_spec()] * 2,
        out_specs=vmem_spec(),
        scratch_shapes=deposit_scratch(),
        compiler_params=params(),
        cost_estimate=pl.CostEstimate(flops=8_000_000_000, bytes_accessed=8_000_000, transcendentals=0),
        name="beside_z",
    )(row_first, below, above)
    halves = f32(CZ, 2, CY, HALF)
    face_z, face_y = f32(2, CY, HALF), f32(CZ, 2, HALF)
    (
        fraction, momentum, residual, direction, mapped, scaled, twice,
        high, low, north_edge, south_edge, high_face, low_face, north_face, south_face, dots,
    ) = pl.pallas_call(
        functools.partial(field_kernel, grid_rows),
        out_shape=(f32(CZ, CY, CX), f32(CZ, 3, CY, CX))
        + (halves,) * 5
        + (face_z, face_z, face_y, face_y) * 2
        + (f32(4),),
        in_specs=[smem_spec()] + [vmem_spec()] * 4 + [pl.BlockSpec(memory_space=pl.ANY)] * 2 + [vmem_spec()] * 3,
        out_specs=tuple([vmem_spec()] * 15 + [smem_spec()]),
        scratch_shapes=[pltpu.VMEM((CZ + 2, 2, YE, HALF), jnp.float32)] * 3
        + [
            pltpu.VMEM((4, ZE, 2, YE, HALF), jnp.float32),
            pltpu.VMEM((4, ZE, 2, YE, HALF), jnp.float32),
            pltpu.VMEM((CZ + 4, 2, YE, HALF), jnp.float32),
            pltpu.VMEM((CZ + 4, 2, YE, HALF), jnp.float32),
            pltpu.VMEM((CZ + 4, 2, YE, HALF), jnp.float32),
            pltpu.VMEM((CZ + 4, 2, YE, HALF), jnp.float32),
            pltpu.VMEM((CZ + 2, 2, YE, HALF), jnp.float32),
            pltpu.VMEM((6, YE, HALF), jnp.float32),
        ]
        + deposit_scratch()
        + [pltpu.SemaphoreType.DMA((3,))],
        compiler_params=params(),
        name="fields",
    )(row_first, below, above, south, north, acc_own, acc_z, gas_density, pressure_prev, divergence)

    scaled_below = lax.ppermute(high, "gz", up_z)
    scaled_above = lax.ppermute(low, "gz", down_z)
    scaled_south = lax.ppermute(north_edge, "gy", up_y)
    scaled_north = lax.ppermute(south_edge, "gy", down_y)
    every = size_z * size_y
    received = (scaled_below, scaled_above, scaled_south, scaled_north)
    faces = (low_face, high_face, south_face, north_face)
    sent = pl.pallas_call(
        second_kernel,
        out_shape=f32(every, 128),
        in_specs=[smem_spec()] + [vmem_spec()] * 12,
        out_specs=vmem_spec(),
        compiler_params=params(),
        name="second",
    )(dots, *received, low, high, south_edge, north_edge, *faces)
    got = lax.all_to_all(sent, ("gz", "gy"), 0, 0, tiled=True)
    pressure, final = pl.pallas_call(
        final_kernel,
        out_shape=(f32(CZ, CY, CX), f32(CZ, CY, CX)),
        in_specs=[vmem_spec()] * 15,
        out_specs=(vmem_spec(), vmem_spec()),
        compiler_params=params(),
        name="final",
    )(got, pressure_prev, residual, direction, mapped, scaled, twice, *received, *faces)
    return (fraction, momentum, pressure, final)


def solution(mesh):
    return jax.shard_map(
        on_device,
        mesh=mesh,
        in_specs=(
            P(("gz", "gy")),
            P(None, ("gz", "gy")),
            P(("gz", "gy")),
            P(None, ("gz", "gy")),
            P("gz", "gy"),
            P("gz", "gy", None),
            P("gz", "gy", None),
            P("gz", "gy", None),
        ),
        out_specs=(
            P("gz", "gy", None),
            P("gz", None, "gy", None),
            P("gz", "gy", None),
            P("gz", "gy", None),
        ),
        check_vma=False,
    )
```

```python
import functools

import jax
import jax.numpy as jnp
from jax import lax
from jax.experimental import pallas as pl
from jax.experimental.pallas import tpu as pltpu
from jax.sharding import PartitionSpec as P

CZ = 8
CY = 64
CX = 256
PCAP = 4096
ITERS = 2
REACH = 5
ZE = CZ + 2 * REACH
YE = 88
LEAD = 12
LIST = PCAP // 256
TILES = CY // 8
HALF = 128
CHUNK = 256
TALL = 16

smooth_rate = 0.15
stiffness = 0.002

VMEM_LIMIT = 36 * 1024 * 1024


def chunk_values(parcels, grid_rows, row_first, shift_y):
    cell = parcels[0:1].astype(jnp.int32)
    home_z = lax.shift_right_logical(cell, 14)
    home_y = lax.shift_right_logical(cell, 8) & 63
    home_x = cell & 255
    count = parcels.shape[1]
    taps = lax.broadcasted_iota(jnp.int32, (8, count), 0).astype(jnp.float32) - 3.0

    def tap_table(offset, inside):
        distance = taps + 0.5 - offset
        weight = jnp.where(inside, jnp.exp(-0.5 * distance * distance), 0.0)
        return weight * (1.0 / jnp.sum(weight, axis=0, keepdims=True))

    seven = taps < 3.5
    place_y = taps + (home_y.astype(jnp.float32) + (row_first + shift_y))
    place_x = taps + home_x.astype(jnp.float32)
    table_z = tap_table(parcels[1:2], seven)
    table_y = tap_table(parcels[2:3], seven & (place_y >= 0.0) & (place_y < grid_rows))
    table_x = tap_table(parcels[3:4], seven & (place_x >= 0.0) & (place_x < float(CX)))
    return home_z, home_y, home_x, table_z, table_y, table_x


def axis_rows(rows, first, home, table, least=None):
    count = home.shape[1]
    lane_row = lax.broadcasted_iota(jnp.int32, (8, count), 0)
    tap_base = lane_row - (home - 3)
    tiles = []
    for tile in range(rows // 8):
        at = first + 8 * tile
        tap = tap_base + at
        fits = (tap & -8) == 0
        if least is not None:
            fits = fits & (lane_row >= least - at)
        tiles.append(jnp.take_along_axis(table, jnp.where(fits, tap, 7), axis=0))
    return tiles[0] if len(tiles) == 1 else jnp.concatenate(tiles, axis=0)


def row_of(cell):
    return lax.shift_right_logical(cell.astype(jnp.int32), 8) & 63


def count_where(condition):
    return jnp.sum(condition.astype(jnp.float32)).astype(jnp.int32)


def deposit(parcels_ref, base, row_first, grid_rows, shift_z, shift_y, planes, plane_first, window, lead, acc_first, acc_ref, lhs_ref, rhs_ref):
    rows = TALL if window is None else 8
    volume = parcels_ref[base : base + LIST, 4, :]
    begin = 0
    if shift_y == 0:
        total = count_where(volume != 0.0)
    else:
        home_row = row_of(parcels_ref[base : base + LIST, 0, :])
        if shift_y < 0:
            total = count_where(volume != 0.0)
            begin = lax.shift_right_logical(
                count_where((volume != 0.0) & (home_row < CY - 3 - REACH)), CHUNK.bit_length() - 1
            )
        else:
            total = count_where((volume != 0.0) & (home_row < 3 + REACH))

    def chunk_step(index, carry):
        start = index * CHUNK
        parcels = parcels_ref[base + index]
        home_z, home_y, home_x, table_z, table_y, table_x = chunk_values(
            parcels, grid_rows, row_first, float(shift_y)
        )
        block = 64
        for part in range(CX // block):
            weight_x = axis_rows(block, part * block, home_x, table_x)
            rhs_ref[part * block : (part + 1) * block, :] = weight_x.astype(jnp.bfloat16)
        rows_z = -(-planes // 8) * 8
        weight_z = axis_rows(rows_z, plane_first - REACH - shift_z, home_z, table_z)
        loaded = [
            weight_z * (parcels[4:5] if field == 0 else parcels[4:5] * parcels[4 + field : 5 + field])
            for field in range(4)
        ]

        def spread_window(first, least):
            weight_y = axis_rows(
                rows, first - (lead + shift_y), home_y, table_y,
                None if least is None else least - lead,
            )
            for field in range(4):
                for pair in range(planes // 2):
                    both = jnp.concatenate(
                        [
                            loaded[field][2 * pair : 2 * pair + 1] * weight_y,
                            loaded[field][2 * pair + 1 : 2 * pair + 2] * weight_y,
                        ],
                        axis=0,
                    )
                    at = (field * planes + 2 * pair) * rows
                    lhs_ref[at : at + 2 * rows, :] = both.astype(jnp.bfloat16)

        def add_window(first):
            for field in range(4):
                product = lax.dot_general(
                    lhs_ref[field * planes * rows : (field + 1) * planes * rows, :],
                    rhs_ref[...],
                    (((1,), (1,)), ((), ())),
                    preferred_element_type=jnp.float32,
                )
                for plane in range(planes):
                    for half in range(2):
                        acc_ref[field, plane_first - acc_first + plane, half, pl.ds(first, rows), :] += product[
                            plane * rows : (plane + 1) * rows, half * HALF : (half + 1) * HALF
                        ]

        if window is not None:
            spread_window(window, None)
            add_window(window)
            return carry

        slot = lax.broadcasted_iota(jnp.int32, (1, CHUNK), 1) + start
        row_home = home_y.astype(jnp.float32)
        lowest = jnp.min(jnp.where(slot < total, row_home, float(CY))).astype(jnp.int32)
        highest = jnp.max(jnp.where(slot < total, row_home, 0.0)).astype(jnp.int32)
        row_low = lowest + (lead - 3)
        row_high = highest + (lead + 4)

        def window_step(carried):
            logical = carried
            first = jnp.minimum(logical, acc_ref.shape[3] - TALL)
            spread_window(first, logical)
            add_window(first)
            return logical + TALL

        lax.while_loop(lambda carried: carried < row_high, window_step, row_low)
        return carry

    end = lax.shift_right_logical(total + (CHUNK - 1), CHUNK.bit_length() - 1)
    lax.fori_loop(begin, end, chunk_step, 0)


def sort_kernel(count_ref, cell_ref, offset_ref, volume_ref, force_ref, guess_ref, density_ref, diverge_ref, up_ref, down_ref, rows_ref, cell_held_ref, data_ref, hot_ref, prefix_ref, dest_ref, lhs_ref, total_ref, sems):
    lists = [
        pltpu.make_async_copy(cell_ref, cell_held_ref, sems.at[0]),
        pltpu.make_async_copy(offset_ref, data_ref.at[1:4], sems.at[1]),
        pltpu.make_async_copy(volume_ref, data_ref.at[4:5], sems.at[2]),
        pltpu.make_async_copy(force_ref, data_ref.at[5:8], sems.at[3]),
    ]
    edges = []
    for out_ref, upper in ((up_ref, True), (down_ref, False)):
        at = LIST
        for source, depth in ((guess_ref, 2), (density_ref, 2), (diverge_ref, 1)):
            for plane in range(depth):
                edges.append(
                    pltpu.make_async_copy(
                        source.at[CZ - depth + plane if upper else plane],
                        out_ref.at[at : at + TILES],
                        sems.at[4 + len(edges)],
                    )
                )
                at += TILES
    for part, source in enumerate((guess_ref, density_ref, diverge_ref)):
        for side in range(2):
            edges.append(
                pltpu.make_async_copy(
                    source.at[:, side * (TILES - 1)], rows_ref.at[2 * part + side], sems.at[4 + len(edges)]
                )
            )
    for copy in lists + edges:
        copy.start()
    for copy in lists:
        copy.wait()
    data_ref[0:1, :] = cell_held_ref[...].astype(jnp.float32)
    live_count = count_ref[0, 0]
    block = 256
    blocks = PCAP // block
    bins = lax.broadcasted_iota(jnp.int32, (CY, block), 0)
    slots = lax.broadcasted_iota(jnp.int32, (1, block), 1)

    def hot_of(index):
        cut = slice(index * block, (index + 1) * block)
        home_row = lax.shift_right_logical(cell_held_ref[:, cut], 8) & 63
        return (bins == home_row) & (slots + index * block < live_count)

    for index in range(blocks):
        hot_ref[index * CY : (index + 1) * CY, :] = hot_of(index).astype(jnp.float32).astype(jnp.bfloat16)
    before = lax.broadcasted_iota(jnp.int32, (block, block), 0)
    after = lax.broadcasted_iota(jnp.int32, (block, block), 1)
    upto = (before <= after).astype(jnp.float32).astype(jnp.bfloat16)
    prefix_ref[...] = jnp.dot(hot_ref[...], upto, preferred_element_type=jnp.float32)
    carry = jnp.zeros((CY, 1), jnp.float32)
    carries = []
    for index in range(blocks):
        carries.append(carry)
        carry = carry + prefix_ref[index * CY : (index + 1) * CY, block - 1 : block]
    total = jnp.broadcast_to(carry, (CY, 128))
    row = lax.broadcasted_iota(jnp.int32, (CY, 128), 0)
    summed = total
    for shift in (1, 2, 4, 8, 16, 32):
        summed = summed + jnp.where(row >= shift, pltpu.roll(summed, shift, 0), 0.0)
    first = (summed - total)[:, 0:1]
    for index in range(blocks):
        cut = slice(index * block, (index + 1) * block)
        place = prefix_ref[index * CY : (index + 1) * CY, :] + (first + carries[index])
        hot = hot_of(index)
        dest = jnp.sum(jnp.where(hot, place, 0.0), axis=0, keepdims=True) - 1.0
        dest_ref[:, cut] = dest.astype(jnp.int32)

    total_ref[...] = jnp.zeros_like(total_ref)
    width = 512

    def route(index, unused):
        start = pl.multiple_of(index * width, width)
        dest = dest_ref[:, pl.ds(start, width)]
        high = lax.shift_right_arithmetic(dest, 8)
        low = dest & 255
        data = data_ref[:, pl.ds(start, width)]
        top = data.astype(jnp.bfloat16).astype(jnp.float32)
        rest = data - top
        middle = rest.astype(jnp.bfloat16).astype(jnp.float32)
        lanes = lax.broadcasted_iota(jnp.int32, (256, width), 0)
        rhs = (lanes == low).astype(jnp.float32).astype(jnp.bfloat16)
        wide = jnp.broadcast_to(high, (8, width))
        for split, values in enumerate((top, middle, rest - middle)):
            for pair in range(8):
                both = jnp.concatenate(
                    [
                        jnp.where(wide == 2 * pair, values, 0.0),
                        jnp.where(wide == 2 * pair + 1, values, 0.0),
                    ],
                    axis=0,
                )
                at = split * 128 + pair * 16
                lhs_ref[at : at + 16, :] = both.astype(jnp.bfloat16)
        total_ref[...] += lax.dot_general(
            lhs_ref[...], rhs, (((1,), (1,)), ((), ())), preferred_element_type=jnp.float32
        )
        return unused

    steps = lax.shift_right_logical(live_count + (width - 1), 9)
    lax.fori_loop(0, steps, route, 0)
    for part in range(LIST):
        at = part * 8
        sorted_part = (
            total_ref[at : at + 8, :] + total_ref[128 + at : 136 + at, :]
        ) + total_ref[256 + at : 264 + at, :]
        up_ref[part] = sorted_part
        down_ref[part] = sorted_part
    for copy in edges:
        copy.wait()


FIELDS = ((2, 2), (2, 2), (1, 1))


def pack_kernel(sorted_ref, below_ref, above_ref, edge_ref, north_ref, south_ref):
    for out_ref in (north_ref, south_ref):
        for index, source in enumerate((sorted_ref, below_ref, above_ref)):
            out_ref[index * LIST : (index + 1) * LIST] = source[0:LIST]
        out_ref[3 * LIST + 7, 2:8, :] = jnp.zeros((6, CX), jnp.float32)
    for side, out_ref in ((1, north_ref), (0, south_ref)):
        slot = 0
        for part, (depth, wide) in enumerate(FIELDS):
            first = (0, 2, 4)[part]
            rows = slice(8 - wide, 8) if side else slice(0, wide)
            for plane in range(CZ + 2 * depth):
                if depth <= plane < CZ + depth:
                    values = edge_ref[2 * part + side, plane - depth, rows, :]
                else:
                    ref, inner = (below_ref, plane) if plane < depth else (above_ref, plane - CZ - depth)
                    values = ref[LIST + (first + inner) * TILES + side * (TILES - 1), rows, :]
                out_ref[3 * LIST + slot // 8, slot % 8 : slot % 8 + wide, :] = values
                slot += wide


def middle_deposit(list_ref, row_first, grid_rows, shift_z, planes, plane_first, acc_first, acc_ref, lhs_ref, rhs_ref):
    deposit(
        list_ref, 0, row_first, grid_rows, shift_z, 0, planes, plane_first, None, LEAD - MID.start,
        acc_first, acc_ref, lhs_ref, rhs_ref,
    )


def own_kernel(grid_rows, row_ref, parcels_ref, acc_ref, lhs_ref, rhs_ref):
    row_first = row_ref[0].astype(jnp.float32)
    acc_ref[...] = jnp.zeros_like(acc_ref)
    middle_deposit(parcels_ref, row_first, grid_rows, 0, 14, 2, 2, acc_ref, lhs_ref, rhs_ref)


def z_kernel(grid_rows, row_ref, below_ref, above_ref, acc_ref, lhs_ref, rhs_ref):
    row_first = row_ref[0].astype(jnp.float32)
    acc_ref[...] = jnp.zeros_like(acc_ref)
    middle_deposit(below_ref, row_first, grid_rows, -CZ, 8, 0, 0, acc_ref, lhs_ref, rhs_ref)
    middle_deposit(above_ref, row_first, grid_rows, CZ, 8, 10, 2, acc_ref, lhs_ref, rhs_ref)


def gather_fields(south_ref, north_ref, below_ref, above_ref, sources, targets):
    slot = 0
    for part, (own_ref, out_ref, (depth, wide)) in enumerate(zip(sources, targets, FIELDS)):
        first = (0, 2, 4)[part]
        for plane in range(CZ + 2 * depth):
            for half in range(2):
                cut = slice(half * HALF, (half + 1) * HALF)
                if depth <= plane < CZ + depth:
                    out_ref[plane, half, OWN, :] = own_ref[plane - depth, :, cut]
                else:
                    ref, inner = (below_ref, plane) if plane < depth else (above_ref, plane - CZ - depth)
                    at = LIST + (first + inner) * TILES
                    for tile in range(TILES):
                        out_ref[plane, half, LEAD + 8 * tile : LEAD + 8 * tile + 8, :] = ref[at + tile, :, cut]
                edge = 3 * LIST + slot // 8
                inner_rows = slice(slot % 8, slot % 8 + wide)
                out_ref[plane, half, LEAD - wide : LEAD, :] = south_ref[edge, inner_rows, cut]
                out_ref[plane, half, LEAD + CY : LEAD + CY + wide, :] = north_ref[edge, inner_rows, cut]
            slot += wide


def beside_y(row_first, grid_rows, south_ref, north_ref, acc_ref, lhs_ref, rhs_ref):
    for parcels_ref, shift_y, window in (
        (south_ref, -CY, LEAD - REACH),
        (north_ref, CY, LEAD + CY - 3),
    ):
        for part, (shift_z, planes, plane_first) in enumerate(((0, 14, 2), (-CZ, 8, 0), (CZ, 8, 10))):
            deposit(
                parcels_ref, LIST * part, row_first, grid_rows, shift_z, shift_y, planes, plane_first,
                window, LEAD, 0, acc_ref, lhs_ref, rhs_ref,
            )


MID = slice(8, 80)
LOW = slice(7, 79)
HIGH = slice(9, 81)
OWN = slice(LEAD, LEAD + CY)


def x_pair(left, right):
    lane = lax.broadcasted_iota(jnp.int32, left.shape, 1)
    start, stop = lane == 0, lane == HALF - 1
    left_west, right_west = pltpu.roll(left, 1, 1), pltpu.roll(right, 1, 1)
    left_east, right_east = pltpu.roll(left, HALF - 1, 1), pltpu.roll(right, HALF - 1, 1)
    return (
        jnp.where(start, 0.0, left_west) + jnp.where(stop, right_east, left_east),
        jnp.where(start, left_west, right_west) + jnp.where(stop, 0.0, right_east),
    )


def x_slope(left, right):
    lane = lax.broadcasted_iota(jnp.int32, left.shape, 1)
    start, stop = lane == 0, lane == HALF - 1
    left_west, right_west = pltpu.roll(left, 1, 1), pltpu.roll(right, 1, 1)
    left_east, right_east = pltpu.roll(left, HALF - 1, 1), pltpu.roll(right, HALF - 1, 1)
    return (
        jnp.where(stop, right_east, left_east) - jnp.where(start, 0.0, left_west),
        jnp.where(stop, 0.0, right_east) - jnp.where(start, left_west, right_west),
    )


def beside_of(ref, plane):
    centre = [ref[plane, half, MID, :] for half in range(2)]
    pairs = x_pair(*centre)
    sums = [
        (ref[plane - 1, half, MID, :] + ref[plane + 1, half, MID, :])
        + (ref[plane, half, LOW, :] + ref[plane, half, HIGH, :])
        + pairs[half]
        for half in range(2)
    ]
    return centre, sums


def field_kernel(
    grid_rows,
    row_ref,
    below_ref,
    above_ref,
    south_ref,
    north_ref,
    acc_own_ref,
    acc_z_ref,
    density_own_ref,
    guess_own_ref,
    diverge_own_ref,
    fraction_ref,
    momentum_ref,
    residual_ref,
    direction_ref,
    mapped_ref,
    scaled_own_ref,
    twice_ref,
    high_ref,
    low_ref,
    north_edge_ref,
    south_edge_ref,
    high_face_ref,
    low_face_ref,
    north_face_ref,
    south_face_ref,
    dots_ref,
    scaled_ref,
    mobility_ref,
    diagonal_ref,
    first_ref,
    second_ref,
    mob_ref,
    guess_ref,
    wide_ref,
    density_ref,
    diverge_ref,
    rate_ref,
    lhs_ref,
    rhs_ref,
    load_sems,
):
    row_first = row_ref[0].astype(jnp.float32)
    loads = [
        pltpu.make_async_copy(acc_z_ref.at[:, 0:CZ], first_ref.at[:, 0:CZ, :, MID, :], load_sems.at[0]),
        pltpu.make_async_copy(
            acc_z_ref.at[:, CZ : 2 * CZ], first_ref.at[:, CZ + 2 : ZE, :, MID, :], load_sems.at[1]
        ),
        pltpu.make_async_copy(acc_own_ref, second_ref.at[:, 2:16, :, MID, :], load_sems.at[2]),
    ]
    for load in loads:
        load.start()
    for field in range(4):
        edge = jnp.zeros((ZE, 2, 8, HALF), jnp.float32)
        first_ref[field, :, :, 0 : MID.start, :] = edge
        first_ref[field, :, :, MID.stop : YE, :] = edge
        first_ref[field, CZ : CZ + 2, :, MID, :] = jnp.zeros((2, 2, 72, HALF), jnp.float32)
    gather_fields(
        south_ref,
        north_ref,
        below_ref,
        above_ref,
        (guess_own_ref, density_own_ref, diverge_own_ref),
        (guess_ref, density_ref, diverge_ref),
    )
    loads[0].wait()
    loads[1].wait()
    beside_y(row_first, grid_rows, south_ref, north_ref, first_ref, lhs_ref, rhs_ref)
    loads[2].wait()

    def add_own(plane, carry):
        for field in range(4):
            for half in range(2):
                first_ref[field, plane, half, MID, :] += second_ref[field, plane, half, MID, :]
        return carry

    lax.fori_loop(2, 16, add_own, 0, unroll=2)

    row = lax.broadcasted_iota(jnp.int32, (YE, HALF), 0).astype(jnp.float32) + (row_first - LEAD)
    lane = lax.broadcasted_iota(jnp.int32, (YE, HALF), 1)
    within = (row >= 0.0) & (row < grid_rows)
    inside = within.astype(jnp.float32)
    count_y = (row >= 1.0).astype(jnp.float32) + (row < grid_rows - 1.0).astype(jnp.float32)
    for half in range(2):
        count_x = 2.0 - (lane == (0, HALF - 1)[half]).astype(jnp.float32)
        rate_ref[half] = inside * (1.0 - smooth_rate * (2.0 + count_y + count_x))
    rate_ref[2] = inside * smooth_rate
    for index, reach in enumerate((2.0, 1.0, 0.0)):
        near = within & (row >= row_first - reach) & (row < row_first + (CY + reach))
        rate_ref[3 + index] = near.astype(jnp.float32)

    for sweep, (source, target) in enumerate(
        ((first_ref, second_ref), (second_ref, first_ref), (first_ref, second_ref))
    ):

        def sweep_plane(plane, fields, source=source, target=target):
            for field in fields:
                centre, sums = beside_of(source.at[field], plane)
                for half in range(2):
                    target[field, plane, half, MID, :] = (
                        rate_ref[half, MID, :] * centre[half] + rate_ref[2, MID, :] * sums[half]
                    )

        def sweep_step(plane, carry, sweep_plane=sweep_plane):
            sweep_plane(plane, (0, 1, 2, 3))
            return carry

        sweep_plane(sweep + 1, (0, 1))
        lax.fori_loop(sweep + 2, ZE - 2 - sweep, sweep_step, 0, unroll=2)
        sweep_plane(ZE - 2 - sweep, (0, 1))

    filtered = second_ref

    def mobility_step(plane, carry):
        known = rate_ref[3] > 0.5
        for half in range(2):
            fraction = 1.0 / (1.0 + filtered[0, plane + 3, half])
            mobility = jnp.where(known, fraction / density_ref[plane, half], 0.0)
            mob_ref[plane, half] = mobility
            wide_ref[plane, half] = mobility * guess_ref[plane, half]
        return carry

    lax.fori_loop(0, CZ + 4, mobility_step, 0, unroll=2)

    def output_step(plane, carry):
        for half in range(2):
            cut = slice(half * HALF, (half + 1) * HALF)
            fraction_ref[plane, :, cut] = 1.0 / (1.0 + filtered[0, plane + REACH, half, OWN, :])
            for part in range(3):
                momentum_ref[plane, part, :, cut] = filtered[part + 1, plane + REACH, half, OWN, :]
        return carry

    lax.fori_loop(0, CZ, output_step, 0)

    direct_ref, product_ref, remain_ref = first_ref.at[0], first_ref.at[1], first_ref.at[2]

    def first_residual(plane, carry):
        at = plane + 1
        near = rate_ref[4, MID, :] > 0.5
        mobility, beside_mobility = beside_of(mob_ref, at)
        guess, beside_guess = beside_of(guess_ref, at)
        unused, beside_wide = beside_of(wide_ref, at)
        slope = x_slope(filtered[3, at + 3, 0, MID, :], filtered[3, at + 3, 1, MID, :])
        for half in range(2):
            diagonal = (3.0 + stiffness) * mobility[half] + 0.5 * beside_mobility[half]
            operated = diagonal * guess[half] - 0.5 * (
                mobility[half] * beside_guess[half] + beside_wide[half]
            )
            spread = 0.5 * (filtered[1, at + 4, half, MID, :] - filtered[1, at + 2, half, MID, :])
            spread = spread + 0.5 * (
                filtered[2, at + 3, half, HIGH, :] - filtered[2, at + 3, half, LOW, :]
            )
            spread = spread + 0.5 * slope[half]
            residual = jnp.where(near, diverge_ref[plane, half, MID, :] - spread - operated, 0.0)
            direction = jnp.where(near, residual / diagonal, 0.0)
            remain_ref[plane, half, MID, :] = residual
            direct_ref[plane, half, MID, :] = direction
            product_ref[plane, half, MID, :] = direction * mobility[half]
            diagonal_ref[plane, half, MID, :] = diagonal
            mobility_ref[plane, half, MID, :] = mobility[half]
        return carry

    lax.fori_loop(0, CZ + 2, first_residual, 0, unroll=2)

    scaled_ref[...] = jnp.zeros_like(scaled_ref)
    again_ref = first_ref.at[3]
    for plane in (0, CZ + 1):
        again_ref[plane] = jnp.zeros((2, YE, HALF), jnp.float32)

    def map_step(plane, sums):
        at = plane + 1
        own = rate_ref[5, MID, :] > 0.5
        directions, beside_direction = beside_of(direct_ref, at)
        unused, beside_product = beside_of(product_ref, at)
        sum_rz, sum_dw, sum_uw = sums
        for half in range(2):
            residual = jnp.where(own, remain_ref[at, half, MID, :], 0.0)
            diagonal = diagonal_ref[at, half, MID, :]
            mapped = diagonal * directions[half] - 0.5 * (
                mobility_ref[at, half, MID, :] * beside_direction[half] + beside_product[half]
            )
            mapped = jnp.where(own, mapped, 0.0)
            scaled = jnp.where(own, mapped / diagonal, 0.0)
            scaled_ref[at, half, MID, :] = scaled
            again_ref[at, half, MID, :] = scaled * mobility_ref[at, half, MID, :]
            scaled_own_ref[plane, half] = scaled[4:68]
            residual_ref[plane, half] = residual[4:68]
            direction_ref[plane, half] = directions[half][4:68]
            mapped_ref[plane, half] = mapped[4:68]
            sum_rz = sum_rz + residual * directions[half]
            sum_dw = sum_dw + directions[half] * mapped
            sum_uw = sum_uw + scaled * mapped
        return sum_rz, sum_dw, sum_uw

    zero = jnp.zeros((72, HALF), jnp.float32)
    sums = lax.fori_loop(0, CZ, map_step, (zero, zero, zero), unroll=2)
    for index in range(3):
        dots_ref[index] = jnp.sum(sums[index])
    def again_step(plane, total):
        at = plane + 1
        centre, beside = beside_of(scaled_ref, at)
        unused, beside_again = beside_of(again_ref, at)
        for half in range(2):
            twice = diagonal_ref[at, half, MID, :] * centre[half] - 0.5 * (
                mobility_ref[at, half, MID, :] * beside[half] + beside_again[half]
            )
            twice_ref[plane, half] = twice[4:68]
            total = total + (centre[half] * twice)[4:68]
        return total

    total = lax.fori_loop(0, CZ, again_step, jnp.zeros((CY, HALF), jnp.float32), unroll=2)
    dots_ref[3] = jnp.sum(total)
    high_face_ref[...] = 0.5 * (mobility_ref[CZ, :, OWN, :] + mobility_ref[CZ + 1, :, OWN, :])
    low_face_ref[...] = 0.5 * (mobility_ref[1, :, OWN, :] + mobility_ref[0, :, OWN, :])
    for face_ref, inner in ((north_face_ref, LEAD + CY - 1), (south_face_ref, LEAD - 1)):
        for plane in range(CZ):
            for half in range(2):
                face_ref[plane, half : half + 1] = 0.5 * (
                    mobility_ref[plane + 1, half, inner : inner + 1, :]
                    + mobility_ref[plane + 1, half, inner + 1 : inner + 2, :]
                )
    high_ref[...] = scaled_ref[CZ, :, OWN, :]
    low_ref[...] = scaled_ref[1, :, OWN, :]
    for plane in range(CZ):
        for half in range(2):
            north_edge_ref[plane, half : half + 1] = scaled_ref[plane + 1, half, LEAD + CY - 1 : LEAD + CY, :]
            south_edge_ref[plane, half : half + 1] = scaled_ref[plane + 1, half, LEAD : LEAD + 1, :]


def second_kernel(dots_ref, *refs):
    received, own_edges, faces, sent_ref = refs[0:4], refs[4:8], refs[8:12], refs[12]
    missing = jnp.float32(0.0)
    for got_ref, own_ref, face_ref in zip(received, own_edges, faces):
        missing = missing + jnp.sum(got_ref[...] * own_ref[...] * face_ref[...])
    values = (dots_ref[0], dots_ref[1], dots_ref[2], dots_ref[3] - missing)
    column = lax.broadcasted_iota(jnp.int32, sent_ref.shape, 1)
    sent = jnp.zeros(sent_ref.shape, jnp.float32)
    for index, value in enumerate(values):
        sent = jnp.where(column == index, value, sent)
    sent_ref[...] = sent


def final_kernel(got_ref, guess_ref, residual_ref, direction_ref, mapped_ref, scaled_ref, twice_ref, below_ref, above_ref, south_ref, north_ref, low_face_ref, high_face_ref, south_face_ref, north_face_ref, pressure_ref, final_ref):
    sums = jnp.sum(got_ref[...], axis=0, keepdims=True)
    sum_rz, sum_dw, sum_uw, sum_uv = (sums[:, index : index + 1] for index in range(4))
    step = sum_rz / sum_dw
    next_rz = sum_rz - 2.0 * step * sum_dw + step * step * sum_uw
    along = 1.0 + next_rz / sum_rz
    curvature = along * along * sum_dw - 2.0 * step * along * sum_uw + step * step * sum_uv
    next_step = next_rz / curvature
    first = step + next_step * along
    last = next_step * step

    row = lax.broadcasted_iota(jnp.int32, (CY, HALF), 0)
    for plane in range(CZ):
        for half in range(2):
            cut = slice(half * HALF, (half + 1) * HALF)
            south = south_ref[plane, half : half + 1] * south_face_ref[plane, half : half + 1]
            north = north_ref[plane, half : half + 1] * north_face_ref[plane, half : half + 1]
            past = jnp.where(row == 0, south, 0.0) + jnp.where(row == CY - 1, north, 0.0)
            if plane == 0:
                past = past + below_ref[half] * low_face_ref[half]
            if plane == CZ - 1:
                past = past + above_ref[half] * high_face_ref[half]
            twice = twice_ref[plane, half] - past
            pressure_ref[plane, :, cut] = (
                guess_ref[plane, :, cut]
                + first * direction_ref[plane, half]
                - last * scaled_ref[plane, half]
            )
            final_ref[plane, :, cut] = (
                residual_ref[plane, half] - first * mapped_ref[plane, half] + last * twice
            )


def vmem_spec():
    return pl.BlockSpec(memory_space=pltpu.VMEM)


def smem_spec():
    return pl.BlockSpec(memory_space=pltpu.SMEM)


def f32(*shape):
    return jax.ShapeDtypeStruct(shape, jnp.float32)


def params():
    return pltpu.CompilerParams(vmem_limit_bytes=VMEM_LIMIT)


def hbm_spec():
    return pl.BlockSpec(memory_space=pltpu.HBM)


def deposit_scratch():
    return [
        pltpu.VMEM((4 * 14 * TALL, CHUNK), jnp.bfloat16),
        pltpu.VMEM((CX, CHUNK), jnp.bfloat16),
    ]


def on_device(
    parcel_cell,
    parcel_offset,
    parcel_volume,
    parcel_force,
    brick_counts,
    divergence,
    pressure_prev,
    gas_density,
):
    size_z = lax.axis_size("gz")
    size_y = lax.axis_size("gy")
    grid_rows = float(size_y * CY)
    row_first = (lax.axis_index("gy") * CY).astype(jnp.int32)[None]
    up_z = [(i, (i + 1) % size_z) for i in range(size_z)]
    down_z = [((i + 1) % size_z, i) for i in range(size_z)]
    up_y = [(i, i + 1) for i in range(size_y - 1)]
    down_y = [(i + 1, i) for i in range(size_y - 1)]

    message = f32(LIST + 5 * TILES, 8, CX)
    tiled = [values.reshape(CZ, TILES, 8, CX) for values in (pressure_prev, gas_density, divergence)]
    to_up, to_down, brick_rows = pl.pallas_call(
        sort_kernel,
        out_shape=(message, message, f32(6, CZ, 8, CX)),
        in_specs=[smem_spec()] + [hbm_spec()] * 7,
        out_specs=(vmem_spec(), vmem_spec(), vmem_spec()),
        scratch_shapes=[
            pltpu.VMEM((1, PCAP), jnp.int32),
            pltpu.VMEM((8, PCAP), jnp.float32),
            pltpu.VMEM((PCAP // 256 * CY, 256), jnp.bfloat16),
            pltpu.VMEM((PCAP // 256 * CY, 256), jnp.float32),
            pltpu.VMEM((1, PCAP), jnp.int32),
            pltpu.VMEM((384, 512), jnp.bfloat16),
            pltpu.VMEM((384, 256), jnp.float32),
            pltpu.SemaphoreType.DMA((20,)),
        ],
        compiler_params=pltpu.CompilerParams(vmem_limit_bytes=60 * 1024 * 1024),
        name="order",
    )(brick_counts, parcel_cell[None], parcel_offset, parcel_volume[None], parcel_force, *tiled)
    acc_own = pl.pallas_call(
        functools.partial(own_kernel, grid_rows),
        out_shape=f32(4, 14, 2, MID.stop - MID.start, HALF),
        in_specs=[smem_spec(), vmem_spec()],
        out_specs=vmem_spec(),
        scratch_shapes=deposit_scratch(),
        compiler_params=params(),
        cost_estimate=pl.CostEstimate(flops=8_000_000_000, bytes_accessed=8_000_000, transcendentals=0),
        name="own",
    )(row_first, to_up)
    below = lax.ppermute(to_up, "gz", up_z)
    above = lax.ppermute(to_down, "gz", down_z)
    edge_rows = f32(3 * LIST + 8, 8, CX)
    to_north, to_south = pl.pallas_call(
        pack_kernel,
        out_shape=(edge_rows, edge_rows),
        in_specs=[vmem_spec()] * 4,
        out_specs=(vmem_spec(), vmem_spec()),
        compiler_params=params(),
        name="pack",
    )(to_up, below, above, brick_rows)
    south = lax.ppermute(to_north, "gy", up_y)
    north = lax.ppermute(to_south, "gy", down_y)
    acc_z = pl.pallas_call(
        functools.partial(z_kernel, grid_rows),
        out_shape=f32(4, 2 * CZ, 2, MID.stop - MID.start, HALF),
        in_specs=[smem_spec()] + [vmem_spec()] * 2,
        out_specs=vmem_spec(),
        scratch_shapes=deposit_scratch(),
        compiler_params=params(),
        cost_estimate=pl.CostEstimate(flops=8_000_000_000, bytes_accessed=8_000_000, transcendentals=0),
        name="beside_z",
    )(row_first, below, above)
    halves = f32(CZ, 2, CY, HALF)
    face_z, face_y = f32(2, CY, HALF), f32(CZ, 2, HALF)
    (
        fraction, momentum, residual, direction, mapped, scaled, twice,
        high, low, north_edge, south_edge, high_face, low_face, north_face, south_face, dots,
    ) = pl.pallas_call(
        functools.partial(field_kernel, grid_rows),
        out_shape=(f32(CZ, CY, CX), f32(CZ, 3, CY, CX))
        + (halves,) * 5
        + (face_z, face_z, face_y, face_y) * 2
        + (f32(4),),
        in_specs=[smem_spec()] + [vmem_spec()] * 4 + [pl.BlockSpec(memory_space=pl.ANY)] * 2 + [vmem_spec()] * 3,
        out_specs=tuple([vmem_spec()] * 15 + [smem_spec()]),
        scratch_shapes=[pltpu.VMEM((CZ + 2, 2, YE, HALF), jnp.float32)] * 3
        + [
            pltpu.VMEM((4, ZE, 2, YE, HALF), jnp.float32),
            pltpu.VMEM((4, ZE, 2, YE, HALF), jnp.float32),
            pltpu.VMEM((CZ + 4, 2, YE, HALF), jnp.float32),
            pltpu.VMEM((CZ + 4, 2, YE, HALF), jnp.float32),
            pltpu.VMEM((CZ + 4, 2, YE, HALF), jnp.float32),
            pltpu.VMEM((CZ + 4, 2, YE, HALF), jnp.float32),
            pltpu.VMEM((CZ + 2, 2, YE, HALF), jnp.float32),
            pltpu.VMEM((6, YE, HALF), jnp.float32),
        ]
        + deposit_scratch()
        + [pltpu.SemaphoreType.DMA((3,))],
        compiler_params=params(),
        name="fields",
    )(row_first, below, above, south, north, acc_own, acc_z, gas_density, pressure_prev, divergence)

    scaled_below = lax.ppermute(high, "gz", up_z)
    scaled_above = lax.ppermute(low, "gz", down_z)
    scaled_south = lax.ppermute(north_edge, "gy", up_y)
    scaled_north = lax.ppermute(south_edge, "gy", down_y)
    every = size_z * size_y
    received = (scaled_below, scaled_above, scaled_south, scaled_north)
    faces = (low_face, high_face, south_face, north_face)
    sent = pl.pallas_call(
        second_kernel,
        out_shape=f32(every, 128),
        in_specs=[smem_spec()] + [vmem_spec()] * 12,
        out_specs=vmem_spec(),
        compiler_params=params(),
        name="second",
    )(dots, *received, low, high, south_edge, north_edge, *faces)
    got = lax.all_to_all(sent, ("gz", "gy"), 0, 0, tiled=True)
    pressure, final = pl.pallas_call(
        final_kernel,
        out_shape=(f32(CZ, CY, CX), f32(CZ, CY, CX)),
        in_specs=[vmem_spec()] * 15,
        out_specs=(vmem_spec(), vmem_spec()),
        compiler_params=params(),
        name="final",
    )(got, pressure_prev, residual, direction, mapped, scaled, twice, *received, *faces)
    return (fraction, momentum, pressure, final)


def solution(mesh):
    return jax.shard_map(
        on_device,
        mesh=mesh,
        in_specs=(
            P(("gz", "gy")),
            P(None, ("gz", "gy")),
            P(("gz", "gy")),
            P(None, ("gz", "gy")),
            P("gz", "gy"),
            P("gz", "gy", None),
            P("gz", "gy", None),
            P("gz", "gy", None),
        ),
        out_specs=(
            P("gz", "gy", None),
            P("gz", None, "gy", None),
            P("gz", "gy", None),
            P("gz", "gy", None),
        ),
        check_vma=False,
    )
```
